256 devices in a mesh: row: 32 (over z, x_hi, core), col: 8 (over x_lo, y).
Axes of the slice: x: 4 (x_hi: 2, x_lo: 2; x = x_hi * 2 + x_lo), y: 4, z: 8, core: 2. Of those that a mesh axis runs over, the one named last changes fastest.
Arguments:
- tokens: bfloat16 [512, 256, 512], P('row', 'col'), may hold values from -24 to 24, as said below
- die_mask: int32 [512, 256], P('row', 'col'), may hold values 0 or 1
- expert_ids: int32 [32, 8, 512, 2], P('row', 'col'), may hold values from 0 to 31, all different within a row; in each aligned block of 512 rows (0 to 511, 512 to 1023, ..., all dimensions but the last counted through in order) at most 96 rows name the same one
- gain_attn: float32 [512], replicated, may hold values from 0.25 to 1.75
- w_qkv: bfloat16 [512, 1536], replicated, may hold values from -1 to 1
- w_out: bfloat16 [512, 512], replicated, may hold values from -0.25 to 0.25
- gain_moe: float32 [512], replicated, may hold values from 0.25 to 1.75
- w_router: bfloat16 [512, 32], replicated, may hold values from -0.1875 to 0.1875
- w_in: bfloat16 [32, 512, 2048], P('row'), may hold values from -0.25 to 0.25
- w_down: bfloat16 [32, 2048, 512], P('row'), may hold values from -0.25 to 0.25
Outputs:
- layer_out: bfloat16 [512, 256, 512], P('row', 'col')
The draws below stay inside these ranges and needn't reach their ends.
Inputs may be any that keep to these rules, and one draw needn't show every extreme that they name: `tokens`: drawn features; at most 24 in magnitude. `expert_ids`: the two ids of a patch differ. Among the 512 patches of one device, no expert is named by more than 96 patches, a bound that some block reaches.
All inputs are finite; a program needn't handle non-finite values. No bound on the sum of `die_mask` on one device may be relied on, other than what follows from the above.
Results may differ from the reference program's by a relative error of at most 0.01.
Values may be sent and summed in bfloat16 or wider, within the bound.
No kernel may reach another device: no remote copies, remote signals or barrier semaphores. Data moves between devices by JAX's collectives and lax.ppermute only.
A program may use at most 128 MiB of HBM per device.

```python
import math
import jax
import jax.numpy as jnp
import numpy as np
from jax import lax

D = 512
HEADS = 16
HEAD_DIM = 32
FF = 2048
RADIUS = 6
TOK_DEV = 512
CAP = 96
EXPERTS = 32
NH = 512
NW = 256
N_ROW = 32
N_COL = 8


def shared_pattern(key):
    signs = (2 * jax.random.randint(jax.random.fold_in(key, 101), (D,), 0, 2) - 1).astype(jnp.float32)
    column = jnp.clip(jax.random.normal(jax.random.fold_in(key, 102), (D,), jnp.float32), -3.0, 3.0)
    return (signs, column)


def aligned_field(noise, signs, picks, strength):
    mixed = strength * signs + jnp.sqrt(1.0 - strength * strength) * noise
    return jnp.where(picks, mixed, noise)


def draw_tokens(key, part):
    signs, leftover = shared_pattern(key)
    key = jax.random.fold_in(key, 11)
    first = jax.random.fold_in(key, 0)
    fourth = jax.random.fold_in(key, 3)
    fifth = jax.random.fold_in(key, 4)
    picks = jax.random.randint(fourth, (NH, NW, 1), 0, 16) == 0
    strength = jax.random.uniform(fifth, (NH, NW, 1), jnp.float32, 0.55, 0.85)
    values = aligned_field(jax.random.normal(first, (NH, NW, D), jnp.float32), signs, picks, strength)
    return jnp.clip(values, -24.0, 24.0).astype(jnp.bfloat16)


def draw_w_qkv(key, part):
    signs, column = shared_pattern(key)
    key = jax.random.fold_in(key, 12)
    random_part = jnp.clip(jax.random.normal(key, (D, 3 * D), jnp.float32), -6.0, 6.0) / math.sqrt(D)
    strength = 30.0
    factor = math.sqrt(strength * math.sqrt(HEAD_DIM) / D) / math.sqrt(D * HEAD_DIM)
    outer = factor * signs[:, None] * column[None, :]
    planted = jnp.concatenate([outer, outer, jnp.zeros((D, D), jnp.float32)], axis=1)
    return jnp.clip(random_part + planted, -1.0, 1.0).astype(jnp.bfloat16)


def touch_ends(entries, stream_key, low, high):
    longest = entries.shape.index(max(entries.shape))
    spots = []
    for shift in (0, 1):
        where = [jax.random.randint(jax.random.fold_in(stream_key, axis), (), 0, length) for axis, length in enumerate(entries.shape)]
        where[longest] = (where[longest] + shift) % entries.shape[longest]
        spots.append(tuple(where))
    return entries.at[spots[0]].set(low).at[spots[1]].set(high)


def block_levels(rng, dims, shards, low, high):
    def one(axis_at, shards_of):
        steps = jax.random.uniform(jax.random.fold_in(jax.random.fold_in(rng, 6), axis_at), (shards_of,), jnp.float32, low / len(shards), high / len(shards))
        return jnp.repeat(jnp.exp(steps), dims[axis_at] // shards_of).reshape((-1,) + (1,) * (len(dims) - axis_at - 1))

    level = one(*shards[0])
    for cut in shards[1:]:
        level = level * one(*cut)
    return level


def deal_out(stream_key, own, number, rows, count, top, limit, slope):
    ranking = jax.random.permutation(stream_key, count)
    crowded, ordinary = shares(count, rows * top, limit, slope, True), shares(count, rows * top, limit, slope, False)
    places = jnp.arange(count)

    def named(tallies, rotation):
        used = int((tallies > 0).sum())
        fixed = max(1, used // 4)
        shifted = fixed + (places - fixed + rotation * (used - fixed)) % max(1, count - fixed)
        return jnp.zeros((count,), jnp.int32).at[ranking[jnp.where(places < fixed, places, shifted)]].set(jnp.asarray(tallies, jnp.int32))

    tallies = jnp.where(number % 4 == 0, named(crowded, number // 4), named(ordinary, number - number // 4 - 1))
    mixed = jax.random.permutation(jax.random.fold_in(own, 3), count)
    giver, receiver = mixed[0:count // 2 * 2:2], mixed[1:count // 2 * 2:2]
    margin = jnp.minimum(tallies[giver] - 1, limit - tallies[receiver]) // 2
    margin = jnp.where((giver == ranking[0]) | (receiver == ranking[0]) | (tallies[receiver] == 0), 0, jnp.maximum(margin, 0))
    shifted = jax.random.randint(jax.random.fold_in(own, 4), (count // 2,), 0, 1 << 20) % (margin + 1)
    tallies = tallies.at[giver].add(-shifted).at[receiver].add(shifted)
    members = jnp.searchsorted(jnp.cumsum(tallies), jnp.arange(rows * top), side="right").astype(jnp.int32)
    table = members.reshape(top, rows).T
    table = table[jax.random.permutation(jax.random.fold_in(own, 1), rows)]
    rotation = jax.random.randint(jax.random.fold_in(own, 2), (rows, 1), 0, top)
    return jnp.take_along_axis(table, (jnp.arange(top)[None, :] + rotation) % top, axis=1)


def shares(number_of, total, limit, lean, full):
    portions = [(1 << 20) // math.isqrt(rank ** lean) + 1 for rank in range(1, number_of + 1)]
    largest = limit if full else min(limit, max(-(-total // number_of), total * portions[0] // sum(portions)))
    least = 1 if total - largest >= number_of - 1 else 0
    holding, spare = [largest] + [least] * (number_of - 1), total - largest - least * (number_of - 1)
    while spare > 0:
        free = [i for i in range(1, number_of) if holding[i] < largest] or [i for i in range(1, number_of) if holding[i] < limit]
        pool, left = sum([portions[i] for i in free]), spare
        for i in free:
            more = min(limit - holding[i], max(1, left * portions[i] // pool), spare)
            holding[i] = holding[i] + more
            spare = spare - more
    return np.array(holding)


def scatter_about(rng, extent, spread, reach, pieces=(), kind=jnp.bfloat16):
    level = block_levels(rng, extent, pieces, -0.22, 0.18) if pieces else 1.0
    array = jax.random.normal(rng, extent, jnp.float32) * spread * level
    return jnp.minimum(jnp.maximum(array, -reach), reach).astype(kind)


def setup_inputs(seed: int = 0) -> dict:
    seeds = jax.random.split(jax.random.key(seed), 11)
    tokens = draw_tokens(jax.random.fold_in(seeds[10], 71), 0)
    die_mask = touch_ends((jax.random.randint(seeds[1], (NH, NW), 0, 8) < 7).astype(jnp.int32), jax.random.fold_in(seeds[1], 1), 0, 1)
    expert_ids_keys = jax.random.split(jax.random.fold_in(seeds[2], 1), N_ROW * N_COL * TOK_DEV // TOK_DEV)
    expert_ids_turns = jax.random.permutation(jax.random.fold_in(seeds[2], 3), N_ROW * N_COL * TOK_DEV // TOK_DEV)
    expert_ids = jax.vmap(lambda own, number: deal_out(jax.random.fold_in(seeds[2], 2), own, number, TOK_DEV, EXPERTS, 2, CAP, 2))(expert_ids_keys, expert_ids_turns).reshape((N_ROW, N_COL, TOK_DEV, 2))
    gain_attn = jnp.clip(1.0 + 0.15 * jax.random.normal(seeds[3], (D,), jnp.float32), 0.25, 1.75)
    w_qkv = draw_w_qkv(jax.random.fold_in(seeds[10], 71), 0)
    w_out = scatter_about(seeds[5], (D, D), D ** -0.5, 0.25)
    gain_moe = jnp.clip(1.0 + 0.15 * jax.random.normal(seeds[6], (D,), jnp.float32), 0.25, 1.75)
    w_router = scatter_about(seeds[7], (D, EXPERTS), (2 * D) ** -0.5, 0.1875)
    w_in = scatter_about(seeds[8], (EXPERTS, D, FF), D ** -0.5, 0.25, ((0, 32),))
    w_down = scatter_about(seeds[9], (EXPERTS, FF, D), (FF // 4) ** -0.5, 0.25, ((0, 32),))
    return {"tokens": tokens, "die_mask": die_mask, "expert_ids": expert_ids, "gain_attn": gain_attn, "w_qkv": w_qkv, "w_out": w_out, "gain_moe": gain_moe, "w_router": w_router, "w_in": w_in, "w_down": w_down}


block_rows = 512

def rms_norm(values, gain):
    wide = values.astype(jnp.float32)
    power = lax.optimization_barrier(jnp.mean(wide * wide, axis=-1, keepdims=True))
    return (wide * lax.rsqrt(power + 1e-06) * gain).astype(jnp.bfloat16)

def expert_ffn(rows, weight_in, weight_down):
    hidden = jax.nn.gelu(jnp.dot(rows, weight_in, preferred_element_type=jnp.float32), approximate=True).astype(jnp.bfloat16)
    return jnp.dot(hidden, weight_down, preferred_element_type=jnp.float32).astype(jnp.bfloat16)

def reference(tokens, die_mask, expert_ids, gain_attn, w_qkv, w_out, gain_moe, w_router, w_in, w_down):
    nh, nw, width = tokens.shape
    heads = HEADS
    hdim = width // heads
    radius = RADIUS
    side = 2 * radius + 1
    normed = rms_norm(tokens, gain_attn)
    proj = jnp.dot(normed.reshape(-1, width), w_qkv, preferred_element_type=jnp.float32)
    query_short = lax.optimization_barrier((proj[:, :width] * hdim ** (-0.5)).astype(jnp.bfloat16))
    query = query_short.astype(jnp.float32).reshape(nh, nw, heads, hdim)
    pair = proj[:, width:].astype(jnp.bfloat16).reshape(nh, nw, 2 * width)
    padded = jnp.pad(pair, ((radius, radius), (radius, radius), (0, 0)))
    mask_pad = jnp.pad(die_mask.astype(jnp.float32), ((radius, radius), (radius, radius)))
    zero = jnp.zeros((), jnp.int32)
    centre = radius * side + radius
    offsets_all = jnp.arange(side * side, dtype=jnp.int32)

    def score_at(index):
        shift_y = (index // side).astype(jnp.int32)
        shift_x = (index % side).astype(jnp.int32)
        window = lax.dynamic_slice(padded, (shift_y, shift_x, zero), (nh, nw, 2 * width))
        marks = lax.dynamic_slice(mask_pad, (shift_y, shift_x), (nh, nw))
        keys = window[..., :width].astype(jnp.float32).reshape(nh, nw, heads, hdim)
        scores = lax.optimization_barrier(jnp.sum(query * keys, axis=-1))
        valid = (marks > 0.5)[..., None] | (index == centre)
        return (jnp.where(valid, scores, -1e+30), window)

    def find_top(top, index):
        masked, unused = score_at(index)
        return (jnp.maximum(top, masked), None)
    top, unused = lax.scan(find_top, jnp.full((nh, nw, heads), -1e+30, jnp.float32), offsets_all)

    def add_values(carry, index):
        total, acc = carry
        masked, window = score_at(index)
        weights = jnp.exp(masked - top)
        rounded = lax.optimization_barrier(weights.astype(jnp.bfloat16)).astype(jnp.float32)
        vals = window[..., width:].astype(jnp.float32).reshape(nh, nw, heads, hdim)
        return ((total + weights, acc + rounded[..., None] * vals), None)
    start = (jnp.zeros((nh, nw, heads), jnp.float32), jnp.zeros((nh, nw, heads, hdim), jnp.float32))
    (total, acc), unused = lax.scan(add_values, start, offsets_all)
    attended = (acc / total[..., None]).reshape(-1, width).astype(jnp.bfloat16)
    mixed = jnp.dot(attended, w_out, preferred_element_type=jnp.float32)
    resid = (tokens.reshape(-1, width).astype(jnp.float32) + mixed).astype(jnp.bfloat16)
    ht = nh // N_ROW
    wt = nw // N_COL
    tiled = resid.reshape(N_ROW, ht, N_COL, wt, width).transpose(0, 2, 1, 3, 4).reshape(-1, width)
    normed_moe = rms_norm(tiled, gain_moe)
    patches = tiled.shape[0]
    experts = w_router.shape[1]
    logits = jnp.dot(normed_moe, w_router, preferred_element_type=jnp.float32)
    ids = expert_ids.reshape(patches, 2).astype(jnp.int32)
    chosen = jnp.take_along_axis(logits, ids, axis=1)
    gates = jnp.stack([jax.nn.sigmoid(chosen[:, 0] - chosen[:, 1]), jax.nn.sigmoid(chosen[:, 1] - chosen[:, 0])], axis=1)
    flat_ids = ids.reshape(-1)
    owners = (jnp.arange(2 * patches, dtype=jnp.int32) // 2).astype(jnp.int32)
    order = jnp.argsort(flat_ids, stable=True).astype(jnp.int32)
    counts = lax.optimization_barrier(jnp.sum((flat_ids[:, None] == jnp.arange(experts, dtype=jnp.int32)[None, :]).astype(jnp.int32), axis=0)).astype(jnp.int32)
    offsets = (jnp.cumsum(counts) - counts).astype(jnp.int32)
    sorted_rows = jnp.concatenate([normed_moe[owners[order]], jnp.zeros((block_rows, width), jnp.bfloat16)], axis=0)

    def per_expert(expert, buffer):
        begin = offsets[expert]
        amount = counts[expert]
        weight_in = lax.dynamic_index_in_dim(w_in, expert, 0, keepdims=False)
        weight_down = lax.dynamic_index_in_dim(w_down, expert, 0, keepdims=False)

        def keep_going(state):
            return state[0] * block_rows < amount

        def one_block(state):
            blocks, buf = state
            at = (begin + blocks * block_rows).astype(jnp.int32)
            rows = lax.dynamic_slice_in_dim(sorted_rows, at, block_rows, 0)
            buf = lax.dynamic_update_slice_in_dim(buf, expert_ffn(rows, weight_in, weight_down), at, 0)
            return (blocks + 1, buf)
        return lax.while_loop(keep_going, one_block, (jnp.zeros((), jnp.int32), buffer))[1]
    results = lax.fori_loop(0, experts, per_expert, jnp.zeros_like(sorted_rows))
    unsorted = jnp.zeros((2 * patches, width), jnp.bfloat16).at[order].set(results[:2 * patches])
    picked = unsorted.reshape(patches, 2, width).astype(jnp.float32)
    moe = lax.optimization_barrier(jnp.sum(picked * gates[..., None], axis=1))
    final = (tiled.astype(jnp.float32) + moe).astype(jnp.bfloat16)
    return final.reshape(N_ROW, N_COL, ht, wt, width).transpose(0, 2, 1, 3, 4).reshape(nh, nw, width)
```

```python
import functools

import jax
import jax.numpy as jnp
import numpy as np
from jax import lax
from jax.experimental import pallas as pl
from jax.experimental.pallas import tpu as pltpu
from jax.sharding import Mesh, PartitionSpec as P

HEADS = 16
RADIUS = 6
CAP = 96
SIDE = 8
QROWS = 4
LANES = 128
BIG = 1e30

ROW = ("z", "xh", "core")
COL = ("xl", "y")


def norm(wide, gain):
    power = jnp.mean(wide * wide, axis=-1, keepdims=True)
    return (wide * lax.rsqrt(power + 1e-06) * gain).astype(jnp.bfloat16)


def geometry(wt):
    keyw = wt + 2 * SIDE
    krows = QROWS + 2 * RADIUS
    k = np.arange(krows * keyw)
    q = np.arange(QROWS * wt)
    kr, kc = k // keyw, k % keyw
    kc = np.where(kc < wt + SIDE, kc, kc - keyw)
    rise = kr[:, None] - q[None, :] // wt - RADIUS
    reach = kc[:, None] - q[None, :] % wt
    inside = (np.abs(rise) <= RADIUS) & (np.abs(reach) <= RADIUS)
    centre = (rise == 0) & (reach == 0)
    return (
        np.where(inside, 0.0, -BIG).astype(np.float32),
        np.where(centre, 0.0, 1.0).astype(np.float32),
    )


def attention_kernel(
    tok_ref, mask_ref, top_ref, bot_ref, left_ref, right_ref, gain_ref, wqkv_ref, wout_ref,
    gain2_ref, geo_ref, off_ref, resid_ref, moe_ref, xn, marks, keys, vals, kaug, vaug, qaug,
):
    ht, wt, width = tok_ref.shape
    keyw = wt + 2 * SIDE
    krows = QROWS + 2 * RADIUS
    slab = krows * keyw
    nq = QROWS * wt
    gain = gain_ref[...]
    step = pl.program_id(0)

    @pl.when(step == 0)
    def _prepare():
        for r in range(ht + 2 * RADIUS):
            at = r * keyw
            if r < RADIUS:
                body, mark = top_ref[r, :, :width], top_ref[r, :, width:]
            elif r < ht + RADIUS:
                body, mark = tok_ref[r - RADIUS], mask_ref[r - RADIUS]
            else:
                body = bot_ref[r - ht - RADIUS, :, :width]
                mark = bot_ref[r - ht - RADIUS, :, width:]
            xn[at : at + wt, :] = norm(body.astype(jnp.float32), gain)
            marks[at : at + wt, :] = mark.astype(jnp.float32)
            edge = jnp.concatenate(
                [right_ref[r].astype(jnp.float32), left_ref[r].astype(jnp.float32)], axis=0
            )
            xn[at + wt : at + keyw, :] = norm(edge[:, :width], gain)
            marks[at + wt : at + keyw, :] = edge[:, width:]
        every = xn[...]
        keys[...] = jnp.dot(
            every, wqkv_ref[:, width : 2 * width], preferred_element_type=jnp.float32
        ).astype(jnp.bfloat16)
        vals[...] = jnp.dot(
            every, wqkv_ref[:, 2 * width :], preferred_element_type=jnp.float32
        ).astype(jnp.bfloat16)
        vaug[:, LANES:] = jnp.ones((slab, LANES), jnp.bfloat16)
        spot = lax.broadcasted_iota(jnp.int32, (nq, nq), 0)
        lane = lax.broadcasted_iota(jnp.int32, (nq, nq), 1)
        unit = (spot == lane).astype(jnp.bfloat16)
        for i in range(4):
            qaug[i * nq : (i + 1) * nq, LANES:] = unit

    base = pl.multiple_of(step * (QROWS * keyw), QROWS * keyw)
    own = [
        xn[pl.ds(pl.multiple_of(base + (RADIUS + i) * keyw, 16), wt), :] for i in range(QROWS)
    ]
    query = jnp.dot(
        jnp.concatenate(own, axis=0), wqkv_ref[:, :width], preferred_element_type=jnp.float32
    )
    hdim = width // HEADS
    query = (query * hdim ** (-0.5)).astype(jnp.bfloat16)
    bias = geo_ref[...] + (marks[pl.ds(base, slab), :] - 1.0) * BIG * off_ref[...]
    kaug[:, LANES:] = bias.astype(jnp.bfloat16)
    per = LANES // hdim
    head_of = lax.broadcasted_iota(jnp.int32, (nq, LANES), 1) // hdim
    pieces = []
    for g in range(width // LANES):
        cols = slice(g * LANES, (g + 1) * LANES)
        qg = query[:, cols]
        for i in range(per):
            qaug[i * nq : (i + 1) * nq, :LANES] = jnp.where(head_of == i, qg, 0).astype(
                jnp.bfloat16
            )
        kaug[:, :LANES] = keys[pl.ds(base, slab), cols]
        vaug[:, :LANES] = vals[pl.ds(base, slab), cols]
        scores = lax.dot_general(
            qaug[...], kaug[...], (((1,), (1,)), ((), ())), preferred_element_type=jnp.float32
        )
        highest = jnp.max(scores, axis=-1, keepdims=True)
        weights = jnp.exp(scores - highest).astype(jnp.bfloat16)
        mixed = jnp.dot(weights, vaug[...], preferred_element_type=jnp.float32)
        share = mixed[:, :LANES] / mixed[:, LANES:]
        both = share[:nq]
        for i in range(1, per):
            both = jnp.where(head_of == i, share[i * nq : (i + 1) * nq], both)
        pieces.append(both.astype(jnp.bfloat16))
    attended = jnp.concatenate(pieces, axis=1)
    mixed = jnp.dot(attended, wout_ref[...], preferred_element_type=jnp.float32)
    mine = tok_ref[pl.ds(step * QROWS, QROWS)].reshape(nq, width)
    resid = (mine.astype(jnp.float32) + mixed).astype(jnp.bfloat16)
    resid_ref[...] = resid
    moe_ref[...] = norm(resid.astype(jnp.float32), gain2_ref[...])


def attention(tokens, marks, top, bot, left, right, gain, wqkv, wout, gain2):
    ht, wt, width = tokens.shape
    geo, off = geometry(wt)
    slab, nq = geo.shape
    total = (ht + 2 * RADIUS) * (wt + 2 * SIDE)
    whole = lambda a: pl.BlockSpec(a.shape, functools.partial(lambda n, i: (0,) * n, a.ndim))
    args = (
        tokens, marks, top, bot, left, right, gain.reshape(1, width), wqkv, wout,
        gain2.reshape(1, width), jnp.asarray(geo), jnp.asarray(off),
    )
    out = jax.ShapeDtypeStruct((ht * wt, width), jnp.bfloat16)
    bf = jnp.bfloat16
    return pl.pallas_call(
        attention_kernel,
        grid=(ht // QROWS,),
        in_specs=[whole(a) for a in args],
        out_specs=[pl.BlockSpec((nq, width), lambda i: (i, 0))] * 2,
        out_shape=[out, out],
        scratch_shapes=[
            pltpu.VMEM((total, width), bf),
            pltpu.VMEM((total, LANES), jnp.float32),
            pltpu.VMEM((total, width), bf),
            pltpu.VMEM((total, width), bf),
            pltpu.VMEM((slab, 2 * LANES), bf),
            pltpu.VMEM((slab, 2 * LANES), bf),
            pltpu.VMEM((4 * nq, 2 * LANES), bf),
        ],
        compiler_params=pltpu.CompilerParams(vmem_limit_bytes=48 << 20),
        cost_estimate=pl.CostEstimate(
            flops=10_000_000_000, bytes_accessed=6_000_000, transcendentals=6_000_000
        ),
    )(*args)


def halo(tokens, mask):
    ht, wt, width = tokens.shape
    count = lax.axis_size(ROW)
    across = lax.axis_size(COL)
    ahead = lambda n: [(i, i + 1) for i in range(n - 1)]
    back = lambda n: [(i + 1, i) for i in range(n - 1)]
    marks = jnp.broadcast_to(mask.astype(jnp.bfloat16)[..., None], (ht, wt, LANES))
    both = lambda rows: jnp.concatenate([tokens[rows], marks[rows]], axis=-1)
    top = lax.ppermute(both(slice(ht - RADIUS, ht)), ROW, ahead(count))
    bot = lax.ppermute(both(slice(0, RADIUS)), ROW, back(count))

    def edge(cols):
        mine = jnp.concatenate([tokens[:, cols], marks[:, cols]], axis=-1)
        return jnp.concatenate([top[:, cols], mine, bot[:, cols]], axis=0)

    left = lax.ppermute(edge(slice(wt - SIDE, wt)), COL, ahead(across))
    right = lax.ppermute(edge(slice(0, SIDE)), COL, back(across))
    return marks, top, bot, left, right


def experts_kernel(
    who_ref, ids_ref, x0, f1, f2, f3, f4, b4, b3, b2, b1, wr_ref, *refs
):
    w_in, w_down = refs[0:4], refs[4:8]
    outs = refs[8:16]
    rows, share, done, acc, buf_in, buf_down, sem = refs[16:]
    half = f4.shape[0]
    patches, width = x0.shape
    ff = w_in[0].shape[-1]
    chunk = buf_in.shape[-1]
    chunks = ff // chunk
    steps = 4 * chunks
    me = who_ref[0]
    z = me // 4

    def copies(n):
        j, c = n // chunks, n % chunks
        slot = n % 2
        span = pl.ds(c * chunk, chunk)
        return (
            pltpu.make_async_copy(w_in[j].at[:, span], buf_in.at[slot], sem.at[slot, 0]),
            pltpu.make_async_copy(w_down[j].at[span, :], buf_down.at[slot], sem.at[slot, 1]),
        )

    for c in copies(0):
        c.start()
    before = lax.broadcasted_iota(jnp.int32, (patches, patches), 0)
    after = lax.broadcasted_iota(jnp.int32, (patches, patches), 1)
    upper = (before < after).astype(jnp.bfloat16)
    slot_of = lax.broadcasted_iota(jnp.int32, (CAP, patches), 0).astype(jnp.float32)
    held = [me ^ j for j in range(4)]
    lane_expert = lax.broadcasted_iota(jnp.int32, (wr_ref.shape[0], patches), 0)
    for d in range(8):
        ids = ids_ref[(z + 8 - d) % 8]
        e0, e1 = ids[0:1], ids[1:2]
        if d == 4:
            x = jnp.concatenate([f4[...], b4[...]], axis=0)
        else:
            x = (x0, f1, f2, f3, None, b3, b2, b1)[d][...]
        logits = lax.dot_general(
            wr_ref[...], x, (((1,), (1,)), ((), ())), preferred_element_type=jnp.float32
        )
        pick = lambda e: jnp.sum(jnp.where(lane_expert == e, logits, 0.0), axis=0, keepdims=True)
        gap = pick(e0) - pick(e1)
        g0, g1 = jax.nn.sigmoid(gap), jax.nn.sigmoid(-gap)
        named = [((e0 == h) | (e1 == h)).astype(jnp.float32) for h in held]
        hot = jnp.concatenate(named + named, axis=0)
        rank = jnp.dot(hot.astype(jnp.bfloat16), upper, preferred_element_type=jnp.float32)
        for j in range(4):
            place = jnp.where(named[j] > 0.5, rank[j : j + 1], -1.0)
            hit = slot_of == place
            gate = jnp.where(e0 == held[j], g0, g1)
            share[d, j * CAP : (j + 1) * CAP, :] = jnp.where(hit, gate, 0.0).astype(jnp.bfloat16)
            one = hit.astype(jnp.float32).astype(jnp.bfloat16)
            rows[j, d * CAP : (d + 1) * CAP, :] = jnp.dot(
                one, x, preferred_element_type=jnp.float32
            ).astype(jnp.bfloat16)
    for n in range(steps):
        j, c = n // chunks, n % chunks
        if n + 1 < steps:
            for cp in copies(n + 1):
                cp.start()
        for cp in copies(n):
            cp.wait()
        hidden = jnp.dot(rows[j], buf_in[n % 2], preferred_element_type=jnp.float32)
        hidden = jax.nn.gelu(hidden, approximate=True).astype(jnp.bfloat16)
        part = jnp.dot(hidden, buf_down[n % 2], preferred_element_type=jnp.float32)
        if c == 0:
            acc[...] = part
        elif c < chunks - 1:
            acc[...] += part
        else:
            whole = (acc[...] + part).astype(jnp.bfloat16)
            for d in range(8):
                done[d, j * CAP : (j + 1) * CAP, :] = whole[d * CAP : (d + 1) * CAP]
    for d in range(8):
        outs[d][...] = lax.dot_general(
            share[d], done[d], (((0,), (0,)), ((), ())), preferred_element_type=jnp.float32
        ).astype(jnp.bfloat16)


def experts(who, ids, blocks, router, w_in, w_down):
    patches, width = blocks[0].shape
    ff = w_in[0].shape[-1]
    chunk = 512
    vm = pl.BlockSpec(memory_space=pltpu.VMEM)
    hbm = pl.BlockSpec(memory_space=pl.ANY)
    bf = jnp.bfloat16
    return pl.pallas_call(
        experts_kernel,
        in_specs=[pl.BlockSpec(memory_space=pltpu.SMEM)] + [vm] * 11 + [hbm] * 8,
        out_specs=[vm] * 8,
        out_shape=[jax.ShapeDtypeStruct((patches, width), bf)] * 8,
        scratch_shapes=[
            pltpu.VMEM((4, 8 * CAP, width), bf),
            pltpu.VMEM((8, 4 * CAP, patches), bf),
            pltpu.VMEM((8, 4 * CAP, width), bf),
            pltpu.VMEM((8 * CAP, width), jnp.float32),
            pltpu.VMEM((2, width, chunk), bf),
            pltpu.VMEM((2, chunk, width), bf),
            pltpu.SemaphoreType.DMA((2, 2)),
        ],
        compiler_params=pltpu.CompilerParams(vmem_limit_bytes=56 << 20),
        cost_estimate=pl.CostEstimate(
            flops=16_000_000_000, bytes_accessed=26_000_000, transcendentals=6_000_000
        ),
    )(who, ids, *blocks, router, *w_in, *w_down)


def around(step):
    count = lax.axis_size("z")
    return [(i, (i + step) % count) for i in range(count)]


def spread(x):
    half = x.shape[0] // 2
    ahead, back = around(1), around(-1)
    f, b = [x], [x]
    for _ in range(3):
        f.append(lax.ppermute(f[-1], "z", ahead))
        b.append(lax.ppermute(b[-1], "z", back))
    f4 = lax.ppermute(f[-1][:half], "z", ahead)
    b4 = lax.ppermute(b[-1][half:], "z", back)
    return x, f[1], f[2], f[3], f4, b4, b[3], b[2], b[1]


def collect(parts):
    half = parts[0].shape[0] // 2
    lo, hi = slice(0, half), slice(half, 2 * half)
    ahead, back = around(1), around(-1)

    def add(a, b):
        return (a.astype(jnp.float32) + b.astype(jnp.float32)).astype(jnp.bfloat16)

    f0 = lax.ppermute(parts[4][lo], "z", back)
    b1 = lax.ppermute(parts[4][hi], "z", ahead)
    f1 = lax.ppermute(parts[3][hi], "z", back)
    b0 = lax.ppermute(parts[5][lo], "z", ahead)
    for i in (3, 2, 1):
        f0 = lax.ppermute(add(f0, parts[i][lo]), "z", back)
        b1 = lax.ppermute(add(b1, parts[8 - i][hi]), "z", ahead)
        if i > 1:
            f1 = lax.ppermute(add(f1, parts[i - 1][hi]), "z", back)
            b0 = lax.ppermute(add(b0, parts[9 - i][lo]), "z", ahead)
    return jnp.concatenate(
        [f0.astype(jnp.float32) + b0.astype(jnp.float32), f1.astype(jnp.float32) + b1.astype(jnp.float32)],
        axis=0,
    )


def plane_weights(w):
    rows = w.shape[0]
    across = lax.axis_size(COL)
    piece = rows // across
    col = lax.axis_index(COL)
    per = across // 2
    want = (col + per) % across
    part = lax.dynamic_slice_in_dim(w, want * piece, piece, 0)
    part = lax.ppermute(part, ("xh", "xl"), [(0, 3), (3, 0), (1, 2), (2, 1)])
    far = lax.all_gather(part, COL, axis=0, tiled=True)
    swap = [(0, 1), (1, 0)]
    return w, lax.ppermute(w, "core", swap), far, lax.ppermute(far, "core", swap)


def per_device(
    tokens, die_mask, expert_ids, gain_attn, w_qkv, w_out, gain_moe, w_router, w_in, w_down
):
    ht, wt, width = tokens.shape
    patches = ht * wt
    marks, top, bot, left, right = halo(tokens, die_mask)
    ids = lax.all_gather(expert_ids.reshape(patches, 2).T, "z", axis=0)
    w_ins = plane_weights(w_in.reshape(w_in.shape[1:]))
    w_downs = plane_weights(w_down.reshape(w_down.shape[1:]))
    resid, normed_moe = attention(
        tokens, marks, top, bot, left, right, gain_attn, w_qkv, w_out, gain_moe
    )
    blocks = spread(normed_moe)
    who = lax.axis_index(ROW).reshape(1).astype(jnp.int32)
    parts = experts(who, ids, blocks, w_router.T, w_ins, w_downs)
    moe = parts[0].astype(jnp.float32) + collect(parts)
    final = (resid.astype(jnp.float32) + moe).astype(jnp.bfloat16)
    return final.reshape(ht, wt, width)


def solution(mesh):
    fine = Mesh(mesh.devices.reshape(8, 2, 2, 2, 4), ROW + COL)
    return jax.shard_map(
        per_device,
        mesh=fine,
        in_specs=(
            P(ROW, COL, None),
            P(ROW, COL),
            P(ROW, COL, None, None),
            P(),
            P(),
            P(),
            P(),
            P(),
            P(ROW, None, None),
            P(ROW, None, None),
        ),
        out_specs=P(ROW, COL, None),
        check_vma=False,
    )
```

```python
import functools

import jax
import jax.numpy as jnp
import numpy as np
from jax import lax
from jax.experimental import pallas as pl
from jax.experimental.pallas import tpu as pltpu
from jax.sharding import Mesh, PartitionSpec as P

HEADS = 16
RADIUS = 6
CAP = 96
SIDE = 8
QROWS = 4
LANES = 128
BIG = 1e30

ROW = ("z", "xh", "core")
COL = ("xl", "y")


def norm(wide, gain):
    power = jnp.mean(wide * wide, axis=-1, keepdims=True)
    return (wide * lax.rsqrt(power + 1e-06) * gain).astype(jnp.bfloat16)


def geometry(wt):
    keyw = wt + 2 * SIDE
    krows = QROWS + 2 * RADIUS
    k = np.arange(krows * keyw)
    q = np.arange(QROWS * wt)
    kr, kc = k // keyw, k % keyw
    kc = np.where(kc < wt + SIDE, kc, kc - keyw)
    rise = kr[:, None] - q[None, :] // wt - RADIUS
    reach = kc[:, None] - q[None, :] % wt
    inside = (np.abs(rise) <= RADIUS) & (np.abs(reach) <= RADIUS)
    centre = (rise == 0) & (reach == 0)
    return (
        np.where(inside, 0.0, -BIG).astype(np.float32),
        np.where(centre, 0.0, 1.0).astype(np.float32),
    )


def attention_kernel(
    tok_ref, mask_ref, top_ref, bot_ref, left_ref, right_ref, gain_ref, wqkv_ref, wout_ref,
    gain2_ref, ids_ref, geo_ref, off_ref, resid_ref, moe_ref, xn, marks, keys, vals, kaug, vaug, qaug,
):
    ht, wt, width = tok_ref.shape
    keyw = wt + 2 * SIDE
    krows = QROWS + 2 * RADIUS
    slab = krows * keyw
    nq = QROWS * wt
    gain = gain_ref[...]
    step = pl.program_id(0)

    @pl.when(step == 0)
    def _prepare():
        for r in range(ht + 2 * RADIUS):
            at = r * keyw
            if r < RADIUS:
                body, mark = top_ref[r, :, :width], top_ref[r, :, width:]
            elif r < ht + RADIUS:
                body, mark = tok_ref[r - RADIUS], mask_ref[r - RADIUS]
            else:
                body = bot_ref[r - ht - RADIUS, :, :width]
                mark = bot_ref[r - ht - RADIUS, :, width:]
            xn[at : at + wt, :] = norm(body.astype(jnp.float32), gain)
            marks[at : at + wt, :] = mark.astype(jnp.float32)
            edge = jnp.concatenate(
                [right_ref[r].astype(jnp.float32), left_ref[r].astype(jnp.float32)], axis=0
            )
            xn[at + wt : at + keyw, :] = norm(edge[:, :width], gain)
            marks[at + wt : at + keyw, :] = edge[:, width:]
        every = xn[...]
        keys[...] = jnp.dot(
            every, wqkv_ref[:, width : 2 * width], preferred_element_type=jnp.float32
        ).astype(jnp.bfloat16)
        vals[...] = jnp.dot(
            every, wqkv_ref[:, 2 * width :], preferred_element_type=jnp.float32
        ).astype(jnp.bfloat16)
        vaug[:, LANES:] = jnp.ones((slab, LANES), jnp.bfloat16)
        spot = lax.broadcasted_iota(jnp.int32, (nq, nq), 0)
        lane = lax.broadcasted_iota(jnp.int32, (nq, nq), 1)
        unit = (spot == lane).astype(jnp.bfloat16)
        for i in range(4):
            qaug[i * nq : (i + 1) * nq, LANES:] = unit
        named = ids_ref[...].astype(jnp.float32)
        spare = jnp.zeros((16 - named.shape[0], named.shape[1]), jnp.float32)
        moe_ref[ht * wt :, :] = jnp.concatenate([named, spare], axis=0).astype(jnp.bfloat16)

    base = pl.multiple_of(step * (QROWS * keyw), QROWS * keyw)
    own = [
        xn[pl.ds(pl.multiple_of(base + (RADIUS + i) * keyw, 16), wt), :] for i in range(QROWS)
    ]
    query = jnp.dot(
        jnp.concatenate(own, axis=0), wqkv_ref[:, :width], preferred_element_type=jnp.float32
    )
    hdim = width // HEADS
    query = (query * hdim ** (-0.5)).astype(jnp.bfloat16)
    bias = geo_ref[...] + (marks[pl.ds(base, slab), :] - 1.0) * BIG * off_ref[...]
    kaug[:, LANES:] = bias.astype(jnp.bfloat16)
    per = LANES // hdim
    head_of = lax.broadcasted_iota(jnp.int32, (nq, LANES), 1) // hdim
    pieces = []
    for g in range(width // LANES):
        cols = slice(g * LANES, (g + 1) * LANES)
        qg = query[:, cols]
        for i in range(per):
            qaug[i * nq : (i + 1) * nq, :LANES] = jnp.where(head_of == i, qg, 0).astype(
                jnp.bfloat16
            )
        kaug[:, :LANES] = keys[pl.ds(base, slab), cols]
        vaug[:, :LANES] = vals[pl.ds(base, slab), cols]
        scores = lax.dot_general(
            qaug[...], kaug[...], (((1,), (1,)), ((), ())), preferred_element_type=jnp.float32
        )
        highest = jnp.max(scores, axis=-1, keepdims=True)
        weights = jnp.exp(scores - highest).astype(jnp.bfloat16)
        mixed = jnp.dot(weights, vaug[...], preferred_element_type=jnp.float32)
        share = mixed[:, :LANES] / mixed[:, LANES:]
        both = share[:nq]
        for i in range(1, per):
            both = jnp.where(head_of == i, share[i * nq : (i + 1) * nq], both)
        pieces.append(both.astype(jnp.bfloat16))
    attended = jnp.concatenate(pieces, axis=1)
    mixed = jnp.dot(attended, wout_ref[...], preferred_element_type=jnp.float32)
    mine = tok_ref[pl.ds(step * QROWS, QROWS)].reshape(nq, width)
    resid = (mine.astype(jnp.float32) + mixed).astype(jnp.bfloat16)
    resid_ref[...] = resid
    moe_ref[pl.ds(pl.multiple_of(step * nq, nq), nq), :] = norm(
        resid.astype(jnp.float32), gain2_ref[...]
    )


def attention(tokens, marks, top, bot, left, right, gain, wqkv, wout, gain2, ids):
    ht, wt, width = tokens.shape
    geo, off = geometry(wt)
    slab, nq = geo.shape
    total = (ht + 2 * RADIUS) * (wt + 2 * SIDE)
    whole = lambda a: pl.BlockSpec(a.shape, functools.partial(lambda n, i: (0,) * n, a.ndim))
    args = (
        tokens, marks, top, bot, left, right, gain.reshape(1, width), wqkv, wout,
        gain2.reshape(1, width), ids, jnp.asarray(geo), jnp.asarray(off),
    )
    bf = jnp.bfloat16
    return pl.pallas_call(
        attention_kernel,
        grid=(ht // QROWS,),
        in_specs=[whole(a) for a in args],
        out_specs=[
            pl.BlockSpec((nq, width), lambda i: (i, 0)),
            pl.BlockSpec((ht * wt + 16, width), lambda i: (0, 0)),
        ],
        out_shape=[
            jax.ShapeDtypeStruct((ht * wt, width), bf),
            jax.ShapeDtypeStruct((ht * wt + 16, width), bf),
        ],
        scratch_shapes=[
            pltpu.VMEM((total, width), bf),
            pltpu.VMEM((total, LANES), jnp.float32),
            pltpu.VMEM((total, width), bf),
            pltpu.VMEM((total, width), bf),
            pltpu.VMEM((slab, 2 * LANES), bf),
            pltpu.VMEM((slab, 2 * LANES), bf),
            pltpu.VMEM((4 * nq, 2 * LANES), bf),
        ],
        compiler_params=pltpu.CompilerParams(vmem_limit_bytes=48 << 20),
        cost_estimate=pl.CostEstimate(
            flops=10_000_000_000, bytes_accessed=6_000_000, transcendentals=6_000_000
        ),
    )(*args)


def halo(tokens, mask):
    ht, wt, width = tokens.shape
    count = lax.axis_size(ROW)
    across = lax.axis_size(COL)
    ahead = lambda n: [(i, i + 1) for i in range(n - 1)]
    back = lambda n: [(i + 1, i) for i in range(n - 1)]
    marks = jnp.broadcast_to(mask.astype(jnp.bfloat16)[..., None], (ht, wt, LANES))
    both = lambda rows: jnp.concatenate([tokens[rows], marks[rows]], axis=-1)
    top = lax.ppermute(both(slice(ht - RADIUS, ht)), ROW, ahead(count))
    bot = lax.ppermute(both(slice(0, RADIUS)), ROW, back(count))

    def edge(cols):
        mine = jnp.concatenate([tokens[:, cols], marks[:, cols]], axis=-1)
        return jnp.concatenate([top[:, cols], mine, bot[:, cols]], axis=0)

    left = lax.ppermute(edge(slice(wt - SIDE, wt)), COL, ahead(across))
    right = lax.ppermute(edge(slice(0, SIDE)), COL, back(across))
    return marks, top, bot, left, right


CHUNK = 512


def experts_kernel(plan, prior, who_ref, wr_ref, *refs):
    ds = list(plan)
    blocks, at = {}, 0
    for d in ds:
        blocks[d] = refs[at : at + (2 if d == 4 else 1)]
        at += len(blocks[d])
    so_far = dict(zip(prior, refs[at : at + len(prior)]))
    at += len(prior)
    users = {j: [d for d in ds if j in plan[d]] for j in range(4)}
    todo = [j for j in range(4) if users[j]]
    held_w = {}
    for j in todo:
        held_w[j] = refs[at : at + (2 if j < 2 else 1)]
        at += len(held_w[j])
    outs = dict(zip(ds, refs[at : at + len(ds)]))
    rows, share, done, acc, buf_in, buf_down, sem = refs[at + len(ds) :]
    width = rows.shape[-1]
    patches = share.shape[-1]
    first = held_w[todo[0]]
    ff = first[0].shape[-1] if todo[0] < 2 else first[0].shape[0] * first[0].shape[-1]
    chunks = ff // CHUNK
    order = [(j, c) for j in todo for c in range(chunks)]
    me = who_ref[0]

    def copies(n):
        j, c = order[n]
        slot = n % 2
        put = lambda src, dst, i: pltpu.make_async_copy(src, dst, sem.at[slot, i])
        if j < 2:
            span = pl.ds(c * CHUNK, CHUNK)
            return (
                put(held_w[j][0].at[:, span], buf_in.at[slot], 0),
                put(held_w[j][1].at[span, :], buf_down.at[slot], 1),
            )
        out, packed = [], held_w[j][0]
        piece = packed.shape[-1]
        for i in range(CHUNK // piece):
            src = packed.at[c * (CHUNK // piece) + i]
            span = pl.ds(i * piece, piece)
            out.append(put(src.at[pl.ds(0, width)], buf_in.at[slot, :, span], 3 * i))
            for k in range(width // piece):
                out.append(
                    put(
                        src.at[pl.ds(width + k * piece, piece)],
                        buf_down.at[slot, span, pl.ds(k * piece, piece)],
                        3 * i + 1 + k,
                    )
                )
        return out

    for c in copies(0):
        c.start()
    before = lax.broadcasted_iota(jnp.int32, (patches, patches), 0)
    after = lax.broadcasted_iota(jnp.int32, (patches, patches), 1)
    upper = (before < after).astype(jnp.bfloat16)
    slot_of = lax.broadcasted_iota(jnp.int32, (CAP, patches), 0).astype(jnp.float32)
    held = [me ^ j for j in range(4)]
    lane_expert = lax.broadcasted_iota(jnp.int32, (wr_ref.shape[0], patches), 0)
    for i, d in enumerate(ds):
        if d == 4:
            f4, b4 = blocks[d]
            half = f4.shape[0]
            x = jnp.concatenate([f4[...], b4[: patches - half]], axis=0)
            ids = b4[patches - half :]
        else:
            x, ids = blocks[d][0][:patches], blocks[d][0][patches:]
        ids = ids.astype(jnp.float32).astype(jnp.int32)
        e0, e1 = ids[0:1], ids[1:2]
        logits = lax.dot_general(
            wr_ref[...], x, (((1,), (1,)), ((), ())), preferred_element_type=jnp.float32
        )
        pick = lambda e: jnp.sum(jnp.where(lane_expert == e, logits, 0.0), axis=0, keepdims=True)
        gap = pick(e0) - pick(e1)
        g0, g1 = jax.nn.sigmoid(gap), jax.nn.sigmoid(-gap)
        named = [((e0 == h) | (e1 == h)).astype(jnp.float32) for h in held]
        hot = jnp.concatenate(named + named, axis=0)
        rank = jnp.dot(hot.astype(jnp.bfloat16), upper, preferred_element_type=jnp.float32)
        for k, j in enumerate(plan[d]):
            place = jnp.where(named[j] > 0.5, rank[j : j + 1], -1.0)
            hit = slot_of == place
            gate = jnp.where(e0 == held[j], g0, g1)
            share[i, k * CAP : (k + 1) * CAP, :] = jnp.where(hit, gate, 0.0).astype(jnp.bfloat16)
            one = hit.astype(jnp.float32).astype(jnp.bfloat16)
            u = users[j].index(d)
            rows[todo.index(j), u * CAP : (u + 1) * CAP, :] = jnp.dot(
                one, x, preferred_element_type=jnp.float32
            ).astype(jnp.bfloat16)
    for n, (j, c) in enumerate(order):
        if n + 1 < len(order):
            for cp in copies(n + 1):
                cp.start()
        for cp in copies(n):
            cp.wait()
        m = len(users[j]) * CAP
        hidden = jnp.dot(
            rows[todo.index(j), :m], buf_in[n % 2], preferred_element_type=jnp.float32
        )
        hidden = jax.nn.gelu(hidden, approximate=True).astype(jnp.bfloat16)
        part = jnp.dot(hidden, buf_down[n % 2], preferred_element_type=jnp.float32)
        if c == 0:
            acc[:m] = part
        elif c < chunks - 1:
            acc[:m] += part
        else:
            whole = (acc[:m] + part).astype(jnp.bfloat16)
            for u, d in enumerate(users[j]):
                k = plan[d].index(j)
                done[ds.index(d), k * CAP : (k + 1) * CAP, :] = whole[u * CAP : (u + 1) * CAP]
    for i, d in enumerate(ds):
        n = len(plan[d]) * CAP
        total = lax.dot_general(
            share[i, :n], done[i, :n], (((0,), (0,)), ((), ())), preferred_element_type=jnp.float32
        )
        if d in so_far:
            total = total + so_far[d][...]
        outs[d][...] = total.astype(outs[d].dtype)


def experts(plan, who, router, blocks, prior, weights, dtype):
    ds = list(plan)
    width, ff = weights[0][0].shape
    patches = sum(a.shape[0] for a in blocks[ds[0]]) - 16
    most = max(len(v) for v in plan.values())
    users = [sum(j in v for v in plan.values()) for j in range(4)]
    needed = [w for j in range(4) if users[j] for w in weights[j]]
    given = [a for d in ds for a in blocks[d]]
    kept = [d for d in ds if d in prior]
    vm = pl.BlockSpec(memory_space=pltpu.VMEM)
    hbm = pl.BlockSpec(memory_space=pl.ANY)
    bf = jnp.bfloat16
    work = sum(users) * CAP * width * ff * 4
    got = pl.pallas_call(
        functools.partial(experts_kernel, plan, kept),
        in_specs=[pl.BlockSpec(memory_space=pltpu.SMEM), vm]
        + [vm] * (len(given) + len(kept))
        + [hbm] * len(needed),
        out_specs=[vm] * len(ds),
        out_shape=[jax.ShapeDtypeStruct((patches, width), dtype)] * len(ds),
        scratch_shapes=[
            pltpu.VMEM((sum(u > 0 for u in users), max(users) * CAP, width), bf),
            pltpu.VMEM((len(ds), most * CAP, patches), bf),
            pltpu.VMEM((len(ds), most * CAP, width), bf),
            pltpu.VMEM((max(users) * CAP, width), jnp.float32),
            pltpu.VMEM((2, width, CHUNK), bf),
            pltpu.VMEM((2, CHUNK, width), bf),
            pltpu.SemaphoreType.DMA((2, 6)),
        ],
        compiler_params=pltpu.CompilerParams(vmem_limit_bytes=40 << 20),
        cost_estimate=pl.CostEstimate(
            flops=2 * work, bytes_accessed=12_000_000, transcendentals=sum(users) * CAP * ff
        ),
    )(who, router, *given, *[prior[d] for d in kept], *needed)
    return dict(zip(ds, got))


def around(step):
    count = lax.axis_size("z")
    return [(i, (i + step) % count) for i in range(count)]


def add(a, b):
    return (a.astype(jnp.float32) + b.astype(jnp.float32)).astype(jnp.bfloat16)


def after(x, *others):
    return lax.optimization_barrier((x, *others))[0]


def expert_layer(x, who, router, weights):
    half = (x.shape[0] - 16) // 2
    lo, hi = slice(0, half), slice(half, 2 * half)
    ahead, back = around(1), around(-1)
    send = lambda a, way: lax.ppermute(a, "z", way)
    near = (0, 1)
    blocks, so_far = {0: (x,)}, {}
    run = lambda plan, dtype, prior={}: experts(plan, who, router, blocks, prior, weights, dtype)
    f, b = x, x
    latest = {}
    for hop in (1, 2, 3):
        f, b = send(f, ahead), send(b, back)
        blocks[hop], blocks[8 - hop] = (f,), (b,)
        if latest:
            f, b, *held = lax.optimization_barrier((f, b, *latest.values()))
            so_far.update(zip(latest, held))
        ds = (hop, 8 - hop) + ((0,) if hop == 1 else ())
        latest = run({d: near for d in ds}, jnp.float32)
    f, b = send(f[:half], ahead), send(b[half:], back)
    f, b, *held = lax.optimization_barrier((f, b, *latest.values()))
    so_far.update(zip(latest, held))
    blocks[4] = (f, b)
    every = (0, 1, 2, 3)
    bf = jnp.bfloat16
    parts = run({4: every, 3: (2, 3), 5: (2, 3)}, bf, so_far)
    f0 = send(parts[4][lo], back)
    b1 = send(parts[4][hi], ahead)
    f1 = send(parts[3][hi], back)
    b0 = send(parts[5][lo], ahead)
    parts.update(run({d: (2, 3) for d in (2, 6, 1, 7, 0)}, bf, so_far))
    for i in (3, 2, 1):
        f0 = send(add(f0, parts[i][lo]), back)
        b1 = send(add(b1, parts[8 - i][hi]), ahead)
        if i > 1:
            f1 = send(add(f1, parts[i - 1][hi]), back)
            b0 = send(add(b0, parts[9 - i][lo]), ahead)
    wide = lambda a: a.astype(jnp.float32)
    return wide(parts[0]) + jnp.concatenate([wide(f0) + wide(b0), wide(f1) + wide(b1)], axis=0)


def far_piece(w_in, w_down):
    across = lax.axis_size(COL)
    width, ff = w_in.shape
    piece = ff // across
    want = (lax.axis_index(COL) + across // 2) % across
    up = lax.dynamic_slice_in_dim(w_in, want * piece, piece, 1)
    down = lax.dynamic_slice_in_dim(w_down, want * piece, piece, 0)
    packed = jnp.concatenate(
        [up] + [down[:, k : k + piece] for k in range(0, width, piece)], axis=0
    )
    return lax.ppermute(packed, ("xh", "xl"), [(0, 3), (3, 0), (1, 2), (2, 1)])


def per_device(
    tokens, die_mask, expert_ids, gain_attn, w_qkv, w_out, gain_moe, w_router, w_in, w_down
):
    ht, wt, width = tokens.shape
    patches = ht * wt
    marks, top, bot, left, right = halo(tokens, die_mask)
    w_in, w_down = after(w_in[0], top, bot), after(w_down[0], top, bot)
    part = far_piece(w_in, w_down)
    swap = lambda a: lax.ppermute(a, "core", [(0, 1), (1, 0)])
    far = lax.all_gather(part, COL, axis=0)
    ids = expert_ids.reshape(patches, 2).T
    resid, x = attention(
        tokens, marks, top, bot, left, after(right, part), gain_attn, w_qkv, w_out, gain_moe, ids
    )
    who = lax.axis_index(ROW).reshape(1).astype(jnp.int32)
    weights = ((w_in, w_down), (swap(w_in), swap(w_down)), (far,), (swap(far),))
    moe = expert_layer(x, who, w_router.T, weights)
    final = (resid.astype(jnp.float32) + moe).astype(jnp.bfloat16)
    return final.reshape(ht, wt, width)


def solution(mesh):
    fine = Mesh(mesh.devices.reshape(8, 2, 2, 2, 4), ROW + COL)
    return jax.shard_map(
        per_device,
        mesh=fine,
        in_specs=(
            P(ROW, COL, None),
            P(ROW, COL),
            P(ROW, COL, None, None),
            P(),
            P(),
            P(),
            P(),
            P(),
            P(ROW, None, None),
            P(ROW, None, None),
        ),
        out_specs=P(ROW, COL, None),
        check_vma=False,
    )
```

```python
import functools

import jax
import jax.numpy as jnp
import numpy as np
from jax import lax
from jax.experimental import pallas as pl
from jax.experimental.pallas import tpu as pltpu
from jax.sharding import Mesh, PartitionSpec as P

HEADS = 16
RADIUS = 6
CAP = 96
SIDE = 8
QROWS = 4
LANES = 128
BIG = 1e30

ROW = ("z", "xh", "core")
COL = ("xl", "y")


def norm(wide, gain):
    power = jnp.mean(wide * wide, axis=-1, keepdims=True)
    return (wide * lax.rsqrt(power + 1e-06) * gain).astype(jnp.bfloat16)


def geometry(wt):
    keyw = wt + 2 * SIDE
    krows = QROWS + 2 * RADIUS
    k = np.arange(krows * keyw)
    q = np.arange(QROWS * wt)
    kr, kc = k // keyw, k % keyw
    kc = np.where(kc < wt + SIDE, kc, kc - keyw)
    rise = kr[:, None] - q[None, :] // wt - RADIUS
    reach = kc[:, None] - q[None, :] % wt
    inside = (np.abs(rise) <= RADIUS) & (np.abs(reach) <= RADIUS)
    centre = (rise == 0) & (reach == 0)
    return (
        np.where(inside, 0.0, -BIG).astype(np.float32),
        np.where(centre, 0.0, 1.0).astype(np.float32),
    )


def attention_kernel(
    tok_ref, mask_ref, top_ref, bot_ref, left_ref, right_ref, gain_ref, wqkv_ref, wout_ref,
    gain2_ref, ids_ref, geo_ref, off_ref, resid_ref, moe_ref, xn, marks, keys, vals, kaug, vaug, qaug,
):
    ht, wt, width = tok_ref.shape
    keyw = wt + 2 * SIDE
    krows = QROWS + 2 * RADIUS
    slab = krows * keyw
    nq = QROWS * wt
    gain = gain_ref[...]
    step = pl.program_id(0)

    @pl.when(step == 0)
    def _prepare():
        for r in range(ht + 2 * RADIUS):
            at = r * keyw
            if r < RADIUS:
                body, mark = top_ref[r, :, :width], top_ref[r, :, width:]
            elif r < ht + RADIUS:
                body, mark = tok_ref[r - RADIUS], mask_ref[r - RADIUS]
            else:
                body = bot_ref[r - ht - RADIUS, :, :width]
                mark = bot_ref[r - ht - RADIUS, :, width:]
            xn[at : at + wt, :] = norm(body.astype(jnp.float32), gain)
            marks[at : at + wt, :] = mark.astype(jnp.float32)
            edge = jnp.concatenate(
                [right_ref[r].astype(jnp.float32), left_ref[r].astype(jnp.float32)], axis=0
            )
            xn[at + wt : at + keyw, :] = norm(edge[:, :width], gain)
            marks[at + wt : at + keyw, :] = edge[:, width:]
        every = xn[...]
        keys[...] = jnp.dot(
            every, wqkv_ref[:, width : 2 * width], preferred_element_type=jnp.float32
        ).astype(jnp.bfloat16)
        vals[...] = jnp.dot(
            every, wqkv_ref[:, 2 * width :], preferred_element_type=jnp.float32
        ).astype(jnp.bfloat16)
        vaug[:, LANES:] = jnp.ones((slab, LANES), jnp.bfloat16)
        spot = lax.broadcasted_iota(jnp.int32, (nq, nq), 0)
        lane = lax.broadcasted_iota(jnp.int32, (nq, nq), 1)
        unit = (spot == lane).astype(jnp.bfloat16)
        for i in range(4):
            qaug[i * nq : (i + 1) * nq, LANES:] = unit
        named = ids_ref[...].astype(jnp.float32)
        spare = jnp.zeros((16 - named.shape[0], named.shape[1]), jnp.float32)
        moe_ref[ht * wt :, :] = jnp.concatenate([named, spare], axis=0).astype(jnp.bfloat16)

    base = pl.multiple_of(step * (QROWS * keyw), QROWS * keyw)
    own = [
        xn[pl.ds(pl.multiple_of(base + (RADIUS + i) * keyw, 16), wt), :] for i in range(QROWS)
    ]
    query = jnp.dot(
        jnp.concatenate(own, axis=0), wqkv_ref[:, :width], preferred_element_type=jnp.float32
    )
    hdim = width // HEADS
    query = (query * hdim ** (-0.5)).astype(jnp.bfloat16)
    bias = geo_ref[...] + (marks[pl.ds(base, slab), :] - 1.0) * BIG * off_ref[...]
    kaug[:, LANES:] = bias.astype(jnp.bfloat16)
    per = LANES // hdim
    head_of = lax.broadcasted_iota(jnp.int32, (nq, LANES), 1) // hdim
    pieces = []
    for g in range(width // LANES):
        cols = slice(g * LANES, (g + 1) * LANES)
        qg = query[:, cols]
        for i in range(per):
            qaug[i * nq : (i + 1) * nq, :LANES] = jnp.where(head_of == i, qg, 0).astype(
                jnp.bfloat16
            )
        kaug[:, :LANES] = keys[pl.ds(base, slab), cols]
        vaug[:, :LANES] = vals[pl.ds(base, slab), cols]
        scores = lax.dot_general(
            qaug[...], kaug[...], (((1,), (1,)), ((), ())), preferred_element_type=jnp.float32
        )
        highest = jnp.max(scores, axis=-1, keepdims=True)
        weights = jnp.exp(scores - highest).astype(jnp.bfloat16)
        mixed = jnp.dot(weights, vaug[...], preferred_element_type=jnp.float32)
        share = mixed[:, :LANES] / mixed[:, LANES:]
        both = share[:nq]
        for i in range(1, per):
            both = jnp.where(head_of == i, share[i * nq : (i + 1) * nq], both)
        pieces.append(both.astype(jnp.bfloat16))
    attended = jnp.concatenate(pieces, axis=1)
    mixed = jnp.dot(attended, wout_ref[...], preferred_element_type=jnp.float32)
    mine = tok_ref[pl.ds(step * QROWS, QROWS)].reshape(nq, width)
    resid = (mine.astype(jnp.float32) + mixed).astype(jnp.bfloat16)
    resid_ref[...] = resid
    moe_ref[pl.ds(pl.multiple_of(step * nq, nq), nq), :] = norm(
        resid.astype(jnp.float32), gain2_ref[...]
    )


def attention(tokens, marks, top, bot, left, right, gain, wqkv, wout, gain2, ids):
    ht, wt, width = tokens.shape
    geo, off = geometry(wt)
    slab, nq = geo.shape
    total = (ht + 2 * RADIUS) * (wt + 2 * SIDE)
    whole = lambda a: pl.BlockSpec(a.shape, functools.partial(lambda n, i: (0,) * n, a.ndim))
    args = (
        tokens, marks, top, bot, left, right, gain.reshape(1, width), wqkv, wout,
        gain2.reshape(1, width), ids, jnp.asarray(geo), jnp.asarray(off),
    )
    bf = jnp.bfloat16
    return pl.pallas_call(
        attention_kernel,
        grid=(ht // QROWS,),
        in_specs=[whole(a) for a in args],
        out_specs=[
            pl.BlockSpec((nq, width), lambda i: (i, 0)),
            pl.BlockSpec((ht * wt + 16, width), lambda i: (0, 0)),
        ],
        out_shape=[
            jax.ShapeDtypeStruct((ht * wt, width), bf),
            jax.ShapeDtypeStruct((ht * wt + 16, width), bf),
        ],
        scratch_shapes=[
            pltpu.VMEM((total, width), bf),
            pltpu.VMEM((total, LANES), jnp.float32),
            pltpu.VMEM((total, width), bf),
            pltpu.VMEM((total, width), bf),
            pltpu.VMEM((slab, 2 * LANES), bf),
            pltpu.VMEM((slab, 2 * LANES), bf),
            pltpu.VMEM((4 * nq, 2 * LANES), bf),
        ],
        compiler_params=pltpu.CompilerParams(vmem_limit_bytes=48 << 20),
        cost_estimate=pl.CostEstimate(
            flops=10_000_000_000, bytes_accessed=6_000_000, transcendentals=6_000_000
        ),
    )(*args)


def with_marks(tokens, mask):
    marks = jnp.broadcast_to(mask.astype(jnp.bfloat16)[..., None], (*mask.shape, LANES))
    return jnp.concatenate([tokens, marks], axis=-1)


def ahead_of(axis):
    return [(i, i + 1) for i in range(lax.axis_size(axis) - 1)]


def behind(axis):
    return [(i + 1, i) for i in range(lax.axis_size(axis) - 1)]


def halo_rows(tokens, mask):
    ht = tokens.shape[0]
    low, high = slice(ht - RADIUS, ht), slice(0, RADIUS)
    top = lax.ppermute(with_marks(tokens[low], mask[low]), ROW, ahead_of(ROW))
    bot = lax.ppermute(with_marks(tokens[high], mask[high]), ROW, behind(ROW))
    return top, bot


def halo_edges(tokens, mask, top, bot):
    def edge(cols):
        mine = with_marks(tokens[:, cols], mask[:, cols])
        return jnp.concatenate([top[:, cols], mine, bot[:, cols]], axis=0)

    wt = tokens.shape[1]
    return edge(slice(wt - SIDE, wt)), edge(slice(0, SIDE))


CHUNK = 512


def experts_kernel(plan, prior, who_ref, wr_ref, *refs):
    ds = list(plan)
    blocks, at = {}, 0
    for d in ds:
        blocks[d] = refs[at : at + (2 if d == 4 else 1)]
        at += len(blocks[d])
    so_far = {d: refs[at + 2 * i : at + 2 * i + 2] for i, d in enumerate(prior)}
    at += 2 * len(prior)
    users = {j: [d for d in ds if j in plan[d]] for j in range(4)}
    todo = [j for j in range(4) if users[j]]
    held_w = {}
    for j in todo:
        held_w[j] = refs[at : at + (2 if j < 2 else 1)]
        at += len(held_w[j])
    outs = {d: refs[at + 2 * i : at + 2 * i + 2] for i, d in enumerate(ds)}
    rows, share, done, acc, buf_in, buf_down, sem = refs[at + 2 * len(ds) :]
    width = rows.shape[-1]
    patches = share.shape[-1]
    first = held_w[todo[0]]
    ff = first[0].shape[-1] if todo[0] < 2 else first[0].shape[0] * first[0].shape[-1]
    chunks = ff // CHUNK
    order = [(j, c) for j in todo for c in range(chunks)]
    me = who_ref[0]

    def copies(n):
        j, c = order[n]
        slot = n % 2
        put = lambda src, dst, i: pltpu.make_async_copy(src, dst, sem.at[slot, i])
        if j < 2:
            span = pl.ds(c * CHUNK, CHUNK)
            return (
                put(held_w[j][0].at[:, span], buf_in.at[slot], 0),
                put(held_w[j][1].at[span, :], buf_down.at[slot], 1),
            )
        out, packed = [], held_w[j][0]
        piece = packed.shape[-1]
        for i in range(CHUNK // piece):
            src = packed.at[c * (CHUNK // piece) + i]
            span = pl.ds(i * piece, piece)
            out.append(put(src.at[pl.ds(0, width)], buf_in.at[slot, :, span], 3 * i))
            for k in range(width // piece):
                out.append(
                    put(
                        src.at[pl.ds(width + k * piece, piece)],
                        buf_down.at[slot, span, pl.ds(k * piece, piece)],
                        3 * i + 1 + k,
                    )
                )
        return out

    for c in copies(0):
        c.start()
    before = lax.broadcasted_iota(jnp.int32, (patches, patches), 0)
    after = lax.broadcasted_iota(jnp.int32, (patches, patches), 1)
    upper = (before < after).astype(jnp.bfloat16)
    slot_of = lax.broadcasted_iota(jnp.int32, (CAP, patches), 0).astype(jnp.float32)
    held = [me ^ j for j in range(4)]
    lane_expert = lax.broadcasted_iota(jnp.int32, (wr_ref.shape[0], patches), 0)
    for i, d in enumerate(ds):
        whole = [ref[...] for ref in blocks[d]]
        whole = whole[0] if len(whole) == 1 else jnp.concatenate(whole, axis=0)
        x = whole[:patches]
        ids = whole[patches:].astype(jnp.float32).astype(jnp.int32)
        e0, e1 = ids[0:1], ids[1:2]
        logits = lax.dot_general(
            wr_ref[...], x, (((1,), (1,)), ((), ())), preferred_element_type=jnp.float32
        )
        pick = lambda e: jnp.sum(jnp.where(lane_expert == e, logits, 0.0), axis=0, keepdims=True)
        gap = pick(e0) - pick(e1)
        g0, g1 = jax.nn.sigmoid(gap), jax.nn.sigmoid(-gap)
        named = [((e0 == h) | (e1 == h)).astype(jnp.float32) for h in held]
        hot = jnp.concatenate(named + named, axis=0)
        rank = jnp.dot(hot.astype(jnp.bfloat16), upper, preferred_element_type=jnp.float32)
        for k, j in enumerate(plan[d]):
            place = jnp.where(named[j] > 0.5, rank[j : j + 1], -1.0)
            hit = slot_of == place
            gate = jnp.where(e0 == held[j], g0, g1)
            share[i, k * CAP : (k + 1) * CAP, :] = jnp.where(hit, gate, 0.0).astype(jnp.bfloat16)
            one = hit.astype(jnp.float32).astype(jnp.bfloat16)
            u = users[j].index(d)
            rows[todo.index(j), u * CAP : (u + 1) * CAP, :] = jnp.dot(
                one, x, preferred_element_type=jnp.float32
            ).astype(jnp.bfloat16)
    for n, (j, c) in enumerate(order):
        if n + 1 < len(order):
            for cp in copies(n + 1):
                cp.start()
        for cp in copies(n):
            cp.wait()
        m = len(users[j]) * CAP
        hidden = jnp.dot(
            rows[todo.index(j), :m], buf_in[n % 2], preferred_element_type=jnp.float32
        )
        hidden = jax.nn.gelu(hidden, approximate=True).astype(jnp.bfloat16)
        part = jnp.dot(hidden, buf_down[n % 2], preferred_element_type=jnp.float32)
        if c == 0:
            acc[:m] = part
        elif c < chunks - 1:
            acc[:m] += part
        else:
            whole = (acc[:m] + part).astype(jnp.bfloat16)
            for u, d in enumerate(users[j]):
                k = plan[d].index(j)
                done[ds.index(d), k * CAP : (k + 1) * CAP, :] = whole[u * CAP : (u + 1) * CAP]
    for i, d in enumerate(ds):
        n = len(plan[d]) * CAP
        total = lax.dot_general(
            share[i, :n], done[i, :n], (((0,), (0,)), ((), ())), preferred_element_type=jnp.float32
        )
        for h, out in enumerate(outs[d]):
            half = total[h * out.shape[0] : (h + 1) * out.shape[0]]
            if d in so_far:
                half = half + so_far[d][h][...]
            out[...] = half.astype(out.dtype)


def experts(plan, who, router, blocks, prior, weights, dtype):
    ds = list(plan)
    width, ff = weights[0][0].shape
    half = (sum(a.shape[0] for a in blocks[ds[0]]) - 16) // 2
    most = max(len(v) for v in plan.values())
    users = [sum(j in v for v in plan.values()) for j in range(4)]
    needed = [w for j in range(4) if users[j] for w in weights[j]]
    given = [a for d in ds for a in blocks[d]]
    kept = [d for d in ds if d in prior]
    vm = pl.BlockSpec(memory_space=pltpu.VMEM)
    hbm = pl.BlockSpec(memory_space=pl.ANY)
    bf = jnp.bfloat16
    work = sum(users) * CAP * width * ff * 4
    got = pl.pallas_call(
        functools.partial(experts_kernel, plan, kept),
        in_specs=[pl.BlockSpec(memory_space=pltpu.SMEM), vm]
        + [vm] * (len(given) + 2 * len(kept))
        + [hbm] * len(needed),
        out_specs=[vm] * (2 * len(ds)),
        out_shape=[jax.ShapeDtypeStruct((half, width), dtype)] * (2 * len(ds)),
        scratch_shapes=[
            pltpu.VMEM((sum(u > 0 for u in users), max(users) * CAP, width), bf),
            pltpu.VMEM((len(ds), most * CAP, 2 * half), bf),
            pltpu.VMEM((len(ds), most * CAP, width), bf),
            pltpu.VMEM((max(users) * CAP, width), jnp.float32),
            pltpu.VMEM((2, width, CHUNK), bf),
            pltpu.VMEM((2, CHUNK, width), bf),
            pltpu.SemaphoreType.DMA((2, 6)),
        ],
        compiler_params=pltpu.CompilerParams(vmem_limit_bytes=40 << 20),
        cost_estimate=pl.CostEstimate(
            flops=2 * work, bytes_accessed=12_000_000, transcendentals=sum(users) * CAP * ff
        ),
    )(who, router, *given, *[a for d in kept for a in prior[d]], *needed)
    return {d: tuple(got[2 * i : 2 * i + 2]) for i, d in enumerate(ds)}


def around(step):
    count = lax.axis_size("z")
    return [(i, (i + step) % count) for i in range(count)]


def add(a, b):
    return (a.astype(jnp.float32) + b.astype(jnp.float32)).astype(jnp.bfloat16)


def after(x, *others):
    return lax.optimization_barrier((x, *others))[0]


def expert_layer(x, who, router, weights_with):
    ahead, back = around(1), around(-1)
    send = lambda a, way: lax.ppermute(a, "z", way)
    near, far, every = (0, 1), (2, 3), (0, 1, 2, 3)
    wide, bf = jnp.float32, jnp.bfloat16
    half = (x.shape[0] - 16) // 2
    blocks, so_far = {0: (x,)}, {}
    weights = weights_with(x)
    run = lambda plan, dtype, prior={}: experts(plan, who, router, blocks, prior, weights, dtype)

    def keep(results, *arrays):
        flat = [a for d in results for a in results[d]]
        out = lax.optimization_barrier((*arrays, *flat))
        held = out[len(arrays) :]
        so_far.update({d: held[2 * i : 2 * i + 2] for i, d in enumerate(results)})
        return out[: len(arrays)]

    f, b = send(x, ahead), send(x, back)
    blocks[1], blocks[7] = (f,), (b,)
    f, b = send(f, ahead), send(b, back)
    blocks[2], blocks[6] = (f,), (b,)
    f, b = keep(run({1: near, 7: near}, wide), f, b)
    weights = weights_with(f)
    f, b = send(f, ahead), send(b, back)
    blocks[3], blocks[5] = (f,), (b,)
    f, b = keep(run({2: near, 6: near}, wide), f, b)
    f, b = send(f[:half], ahead), send(b[half:], back)
    parts = run({3: every, 5: every}, bf)
    blocks[4] = tuple(lax.optimization_barrier((f, b, *parts[3], *parts[5]))[:2])
    f1, b0 = send(parts[3][1], back), send(parts[5][0], ahead)
    parts.update(run({4: every}, bf))
    f0, b1 = send(parts[4][0], back), send(parts[4][1], ahead)
    parts.update(run({2: far, 6: far}, bf, so_far))
    f1, b0 = add(f1, parts[2][1]), add(b0, parts[6][0])
    f0, b1 = add(f0, parts[3][0]), add(b1, parts[5][1])
    blocks[0] = (after(x, f0, b1, f1, b0),)
    f1, b0 = send(f1, back), send(b0, ahead)
    f0, b1 = send(f0, back), send(b1, ahead)
    parts.update(run({1: far, 7: far, 0: every}, bf, so_far))
    f1, b0 = send(add(f1, parts[1][1]), back), send(add(b0, parts[7][0]), ahead)
    f0, b1 = send(add(f0, parts[2][0]), back), send(add(b1, parts[6][1]), ahead)
    f0, b1 = send(add(f0, parts[1][0]), back), send(add(b1, parts[7][1]), ahead)
    return [(parts[0][0], f0, b0), (parts[0][1], f1, b1)]


def far_piece(w_in, w_down):
    across = lax.axis_size(COL)
    width, ff = w_in.shape
    piece = ff // across
    want = (lax.axis_index(COL) + across // 2) % across
    up = lax.dynamic_slice_in_dim(w_in, want * piece, piece, 1)
    down = lax.dynamic_slice_in_dim(w_down, want * piece, piece, 0)
    packed = jnp.concatenate(
        [up] + [down[:, k : k + piece] for k in range(0, width, piece)], axis=0
    )
    return lax.ppermute(packed, ("xh", "xl"), [(0, 3), (3, 0), (1, 2), (2, 1)])


def per_device(
    tokens, die_mask, expert_ids, gain_attn, w_qkv, w_out, gain_moe, w_router, w_in, w_down
):
    ht, wt, width = tokens.shape
    patches = ht * wt
    w_in, w_down = w_in[0], w_down[0]
    top, bot = halo_rows(tokens, die_mask)
    part = far_piece(w_in, w_down)
    to_right, to_left = halo_edges(tokens, die_mask, top, bot)
    part, to_right, to_left = lax.optimization_barrier((part, to_right, to_left))
    left = lax.ppermute(to_right, COL, ahead_of(COL))
    right = lax.ppermute(to_left, COL, behind(COL))
    far = lax.all_gather(part, COL, axis=0)
    ids = expert_ids.reshape(patches, 2).T
    marks = jnp.broadcast_to(die_mask.astype(jnp.bfloat16)[..., None], (ht, wt, LANES))
    resid, x = attention(
        tokens, marks, top, bot, left, right, gain_attn, w_qkv, w_out, gain_moe, ids
    )
    who = lax.axis_index(ROW).reshape(1).astype(jnp.int32)
    swap = lambda a: lax.ppermute(a, "core", [(0, 1), (1, 0)])
    other = swap(after(w_in, top)), swap(after(w_down, top))

    def weights(late):
        across = after(far, late)
        return ((w_in, w_down), other, (across,), (swap(across),))

    wide = lambda a: a.astype(jnp.float32)
    moe = expert_layer(x, who, w_router.T, weights)
    moe = jnp.concatenate([wide(p) + (wide(f) + wide(b)) for p, f, b in moe], axis=0)
    final = (wide(resid) + moe).astype(jnp.bfloat16)
    return final.reshape(ht, wt, width)


def solution(mesh):
    fine = Mesh(mesh.devices.reshape(8, 2, 2, 2, 4), ROW + COL)
    return jax.shard_map(
        per_device,
        mesh=fine,
        in_specs=(
            P(ROW, COL, None),
            P(ROW, COL),
            P(ROW, COL, None, None),
            P(),
            P(),
            P(),
            P(),
            P(),
            P(ROW, None, None),
            P(ROW, None, None),
        ),
        out_specs=P(ROW, COL, None),
        check_vma=False,
    )
```

```python
import functools

import jax
import jax.numpy as jnp
import numpy as np
from jax import lax
from jax.experimental import pallas as pl
from jax.experimental.pallas import tpu as pltpu
from jax.sharding import Mesh, PartitionSpec as P

HEADS = 16
RADIUS = 6
CAP = 96
SIDE = 8
QROWS = 4
LANES = 128
BIG = 1e30

ROW = ("z", "xh", "core")
COL = ("xl", "y")


def norm(wide, gain):
    power = jnp.mean(wide * wide, axis=-1, keepdims=True)
    return (wide * lax.rsqrt(power + 1e-06) * gain).astype(jnp.bfloat16)


def geometry(wt):
    keyw = wt + 2 * SIDE
    krows = QROWS + 2 * RADIUS
    k = np.arange(krows * keyw)
    q = np.arange(QROWS * wt)
    kr, kc = k // keyw, k % keyw
    kc = np.where(kc < wt + SIDE, kc, kc - keyw)
    rise = kr[:, None] - q[None, :] // wt - RADIUS
    reach = kc[:, None] - q[None, :] % wt
    inside = (np.abs(rise) <= RADIUS) & (np.abs(reach) <= RADIUS)
    centre = (rise == 0) & (reach == 0)
    return (
        np.where(inside, 0.0, -BIG).astype(np.float32),
        np.where(centre, 0.0, 1.0).astype(np.float32),
    )


def attention_kernel(
    tok_ref, mask_ref, top_ref, bot_ref, left_ref, right_ref, gain_ref, wqkv_ref, wout_ref,
    gain2_ref, ids_ref, geo_ref, off_ref, resid_ref, moe_ref, xn, marks, keys, vals, kaug, vaug, qaug,
):
    ht, wt, width = tok_ref.shape
    keyw = wt + 2 * SIDE
    krows = QROWS + 2 * RADIUS
    slab = krows * keyw
    nq = QROWS * wt
    gain = gain_ref[...]
    step = pl.program_id(0)

    @pl.when(step == 0)
    def _prepare():
        def rows(first, count, body_of):
            @pl.loop(0, count)
            def _row(i):
                body, mark = body_of(i)
                at = pl.multiple_of((first + i) * keyw, 16)
                xn[pl.ds(at, wt), :] = norm(body.astype(jnp.float32), gain)
                marks[pl.ds(at, wt), :] = mark.astype(jnp.float32)
                edge = jnp.concatenate(
                    [
                        right_ref[first + i].astype(jnp.float32),
                        left_ref[first + i].astype(jnp.float32),
                    ],
                    axis=0,
                )
                beside = pl.ds(pl.multiple_of(at + wt, 16), 2 * SIDE)
                xn[beside, :] = norm(edge[:, :width], gain)
                marks[beside, :] = edge[:, width:]

        rows(0, RADIUS, lambda i: (top_ref[i, :, :width], top_ref[i, :, width:]))
        rows(RADIUS, ht, lambda i: (tok_ref[i], mask_ref[i]))
        rows(ht + RADIUS, RADIUS, lambda i: (bot_ref[i, :, :width], bot_ref[i, :, width:]))
        every = xn[...]
        keys[...] = jnp.dot(
            every, wqkv_ref[:, width : 2 * width], preferred_element_type=jnp.float32
        ).astype(jnp.bfloat16)
        vals[...] = jnp.dot(
            every, wqkv_ref[:, 2 * width :], preferred_element_type=jnp.float32
        ).astype(jnp.bfloat16)
        vaug[:, LANES:] = jnp.ones((slab, LANES), jnp.bfloat16)
        spot = lax.broadcasted_iota(jnp.int32, (nq, nq), 0)
        lane = lax.broadcasted_iota(jnp.int32, (nq, nq), 1)
        unit = (spot == lane).astype(jnp.bfloat16)
        for i in range(4):
            qaug[i * nq : (i + 1) * nq, LANES:] = unit
        named = ids_ref[...].astype(jnp.float32)
        spare = jnp.zeros((16 - named.shape[0], named.shape[1]), jnp.float32)
        moe_ref[ht * wt :, :] = jnp.concatenate([named, spare], axis=0).astype(jnp.bfloat16)

    base = pl.multiple_of(step * (QROWS * keyw), QROWS * keyw)
    own = [
        xn[pl.ds(pl.multiple_of(base + (RADIUS + i) * keyw, 16), wt), :] for i in range(QROWS)
    ]
    query = jnp.dot(
        jnp.concatenate(own, axis=0), wqkv_ref[:, :width], preferred_element_type=jnp.float32
    )
    hdim = width // HEADS
    query = (query * hdim ** (-0.5)).astype(jnp.bfloat16)
    bias = geo_ref[...] + (marks[pl.ds(base, slab), :] - 1.0) * BIG * off_ref[...]
    kaug[:, LANES:] = bias.astype(jnp.bfloat16)
    per = LANES // hdim
    head_of = lax.broadcasted_iota(jnp.int32, (nq, LANES), 1) // hdim
    pieces = []
    for g in range(width // LANES):
        cols = slice(g * LANES, (g + 1) * LANES)
        qg = query[:, cols]
        for i in range(per):
            qaug[i * nq : (i + 1) * nq, :LANES] = jnp.where(head_of == i, qg, 0).astype(
                jnp.bfloat16
            )
        kaug[:, :LANES] = keys[pl.ds(base, slab), cols]
        vaug[:, :LANES] = vals[pl.ds(base, slab), cols]
        scores = lax.dot_general(
            qaug[...], kaug[...], (((1,), (1,)), ((), ())), preferred_element_type=jnp.float32
        )
        highest = jnp.max(scores, axis=-1, keepdims=True)
        weights = jnp.exp(scores - highest).astype(jnp.bfloat16)
        mixed = jnp.dot(weights, vaug[...], preferred_element_type=jnp.float32)
        share = mixed[:, :LANES] / mixed[:, LANES:]
        both = share[:nq]
        for i in range(1, per):
            both = jnp.where(head_of == i, share[i * nq : (i + 1) * nq], both)
        pieces.append(both.astype(jnp.bfloat16))
    attended = jnp.concatenate(pieces, axis=1)
    mixed = jnp.dot(attended, wout_ref[...], preferred_element_type=jnp.float32)
    mine = tok_ref[pl.ds(step * QROWS, QROWS)].reshape(nq, width)
    resid = (mine.astype(jnp.float32) + mixed).astype(jnp.bfloat16)
    resid_ref[...] = resid
    moe_ref[pl.ds(pl.multiple_of(step * nq, nq), nq), :] = norm(
        resid.astype(jnp.float32), gain2_ref[...]
    )


def attention(tokens, marks, top, bot, left, right, gain, wqkv, wout, gain2, ids):
    ht, wt, width = tokens.shape
    geo, off = geometry(wt)
    slab, nq = geo.shape
    total = (ht + 2 * RADIUS) * (wt + 2 * SIDE)
    whole = lambda a: pl.BlockSpec(a.shape, functools.partial(lambda n, i: (0,) * n, a.ndim))
    args = (
        tokens, marks, top, bot, left, right, gain.reshape(1, width), wqkv, wout,
        gain2.reshape(1, width), ids, jnp.asarray(geo), jnp.asarray(off),
    )
    bf = jnp.bfloat16
    return pl.pallas_call(
        attention_kernel,
        grid=(ht // QROWS,),
        in_specs=[whole(a) for a in args],
        out_specs=[
            pl.BlockSpec((nq, width), lambda i: (i, 0)),
            pl.BlockSpec((ht * wt + 16, width), lambda i: (0, 0)),
        ],
        out_shape=[
            jax.ShapeDtypeStruct((ht * wt, width), bf),
            jax.ShapeDtypeStruct((ht * wt + 16, width), bf),
        ],
        scratch_shapes=[
            pltpu.VMEM((total, width), bf),
            pltpu.VMEM((total, LANES), jnp.float32),
            pltpu.VMEM((total, width), bf),
            pltpu.VMEM((total, width), bf),
            pltpu.VMEM((slab, 2 * LANES), bf),
            pltpu.VMEM((slab, 2 * LANES), bf),
            pltpu.VMEM((4 * nq, 2 * LANES), bf),
        ],
        compiler_params=pltpu.CompilerParams(vmem_limit_bytes=60 << 20),
        cost_estimate=pl.CostEstimate(
            flops=10_000_000_000, bytes_accessed=6_000_000, transcendentals=6_000_000
        ),
    )(*args)


def with_marks(tokens, mask):
    marks = jnp.broadcast_to(mask.astype(jnp.bfloat16)[..., None], (*mask.shape, LANES))
    return jnp.concatenate([tokens, marks], axis=-1)


def ahead_of(axis):
    return [(i, i + 1) for i in range(lax.axis_size(axis) - 1)]


def behind(axis):
    return [(i + 1, i) for i in range(lax.axis_size(axis) - 1)]


def halo_rows(tokens, mask):
    ht = tokens.shape[0]
    low, high = slice(ht - RADIUS, ht), slice(0, RADIUS)
    top = lax.ppermute(with_marks(tokens[low], mask[low]), ROW, ahead_of(ROW))
    bot = lax.ppermute(with_marks(tokens[high], mask[high]), ROW, behind(ROW))
    return top, bot


def halo_edges(tokens, mask, top, bot):
    def edge(cols):
        mine = with_marks(tokens[:, cols], mask[:, cols])
        return jnp.concatenate([top[:, cols], mine, bot[:, cols]], axis=0)

    wt = tokens.shape[1]
    return edge(slice(wt - SIDE, wt)), edge(slice(0, SIDE))


CHUNK = 512


def experts_kernel(plan, prior, who_ref, wr_ref, *refs):
    ds = list(plan)
    blocks, at = {}, 0
    for d in ds:
        blocks[d] = refs[at : at + (2 if d == 4 else 1)]
        at += len(blocks[d])
    so_far = {d: refs[at + 2 * i : at + 2 * i + 2] for i, d in enumerate(prior)}
    at += 2 * len(prior)
    users = {j: [d for d in ds if j in plan[d]] for j in range(4)}
    todo = [j for j in range(4) if users[j]]
    held_w = {}
    for j in todo:
        held_w[j] = refs[at : at + (2 if j < 2 else 5)]
        at += len(held_w[j])
    outs = {d: refs[at + 2 * i : at + 2 * i + 2] for i, d in enumerate(ds)}
    rows, share, done, acc, raw, buf_in, buf_down, sem = refs[at + 2 * len(ds) :]
    width = rows.shape[-1]
    patches = share.shape[-1]
    ff = buf_in.shape[-1]
    chunks = ff // CHUNK
    piece = ff // 4
    me = who_ref[0]

    def copies(n):
        j, slot = todo[n], n % 2
        put = lambda src, dst, i: pltpu.make_async_copy(src, dst, sem.at[slot, i])
        if j < 2:
            return (
                put(held_w[j][0], buf_in.at[slot], 0),
                put(held_w[j][1], buf_down.at[slot], 1),
            )
        out = []
        for i, ref in enumerate(held_w[j]):
            span = pl.ds(min(i, 3) * piece, piece)
            if i < 4:
                src = ref.at[pl.ds(0, width)]
                out.append(put(src, buf_in.at[slot, :, span], 2 * i))
            if i != 3:
                src = ref.at[pl.ds(width, piece)] if i < 3 else ref
                out.append(put(src, buf_down.at[slot, span, :], 2 * i + 1))
        return out

    for c in copies(0):
        c.start()
    before = lax.broadcasted_iota(jnp.int32, (patches, patches), 0)
    after = lax.broadcasted_iota(jnp.int32, (patches, patches), 1)
    upper = (before < after).astype(jnp.bfloat16)
    slot_of = lax.broadcasted_iota(jnp.int32, (CAP, patches), 0).astype(jnp.float32)
    held = [me ^ j for j in range(4)]
    lane_expert = lax.broadcasted_iota(jnp.int32, (wr_ref.shape[0], patches), 0)
    for i, d in enumerate(ds):
        whole = [ref[...] for ref in blocks[d]]
        whole = whole[0] if len(whole) == 1 else jnp.concatenate(whole, axis=0)
        x = whole[:patches]
        ids = whole[patches:].astype(jnp.float32).astype(jnp.int32)
        e0, e1 = ids[0:1], ids[1:2]
        logits = lax.dot_general(
            wr_ref[...], x, (((1,), (1,)), ((), ())), preferred_element_type=jnp.float32
        )
        pick = lambda e: jnp.sum(jnp.where(lane_expert == e, logits, 0.0), axis=0, keepdims=True)
        gap = pick(e0) - pick(e1)
        g0, g1 = jax.nn.sigmoid(gap), jax.nn.sigmoid(-gap)
        named = [((e0 == h) | (e1 == h)).astype(jnp.float32) for h in held]
        hot = jnp.concatenate(named + named, axis=0)
        rank = jnp.dot(hot.astype(jnp.bfloat16), upper, preferred_element_type=jnp.float32)
        for k, j in enumerate(plan[d]):
            place = jnp.where(named[j] > 0.5, rank[j : j + 1], -1.0)
            hit = slot_of == place
            gate = jnp.where(e0 == held[j], g0, g1)
            share[i, k * CAP : (k + 1) * CAP, :] = jnp.where(hit, gate, 0.0).astype(jnp.bfloat16)
            one = hit.astype(jnp.float32).astype(jnp.bfloat16)
            u = users[j].index(d)
            rows[todo.index(j), u * CAP : (u + 1) * CAP, :] = jnp.dot(
                one, x, preferred_element_type=jnp.float32
            ).astype(jnp.bfloat16)
    for n, j in enumerate(todo):
        if n + 1 < len(todo):
            for cp in copies(n + 1):
                cp.start()
        for cp in copies(n):
            cp.wait()
        m = len(users[j]) * CAP
        slot = n % 2

        def up(c):
            return jnp.dot(
                rows[n, :m],
                buf_in[slot, :, pl.ds(pl.multiple_of(c * CHUNK, CHUNK), CHUNK)],
                preferred_element_type=jnp.float32,
            )

        def down(c, hidden):
            return jnp.dot(
                jax.nn.gelu(hidden, approximate=True).astype(jnp.bfloat16),
                buf_down[slot, pl.ds(pl.multiple_of(c * CHUNK, CHUNK), CHUNK), :],
                preferred_element_type=jnp.float32,
            )

        raw[0, :m] = up(0)
        acc[:m] = jnp.zeros((m, width), jnp.float32)

        @pl.loop(0, chunks - 1)
        def _chunk(c):
            now = lax.rem(c, 2)
            raw[1 - now, :m] = up(c + 1)
            acc[:m] += down(c, raw[now, :m])

        whole = (acc[:m] + down(chunks - 1, raw[(chunks - 1) % 2, :m])).astype(jnp.bfloat16)
        for u, d in enumerate(users[j]):
            k = plan[d].index(j)
            done[ds.index(d), k * CAP : (k + 1) * CAP, :] = whole[u * CAP : (u + 1) * CAP]
    for i, d in enumerate(ds):
        n = len(plan[d]) * CAP
        total = lax.dot_general(
            share[i, :n], done[i, :n], (((0,), (0,)), ((), ())), preferred_element_type=jnp.float32
        )
        for h, out in enumerate(outs[d]):
            half = total[h * out.shape[0] : (h + 1) * out.shape[0]]
            if d in so_far:
                half = half + so_far[d][h][...]
            out[...] = half.astype(out.dtype)


def experts(plan, who, router, blocks, prior, weights, dtype):
    ds = list(plan)
    width, ff = weights[0][0].shape
    half = (sum(a.shape[0] for a in blocks[ds[0]]) - 16) // 2
    most = max(len(v) for v in plan.values())
    users = [sum(j in v for v in plan.values()) for j in range(4)]
    needed = [w for j in range(4) if users[j] for w in weights[j]]
    given = [a for d in ds for a in blocks[d]]
    kept = [d for d in ds if d in prior]
    vm = pl.BlockSpec(memory_space=pltpu.VMEM)
    hbm = pl.BlockSpec(memory_space=pl.ANY)
    bf = jnp.bfloat16
    work = sum(users) * CAP * width * ff * 4
    got = pl.pallas_call(
        functools.partial(experts_kernel, plan, kept),
        in_specs=[pl.BlockSpec(memory_space=pltpu.SMEM), vm]
        + [vm] * (len(given) + 2 * len(kept))
        + [hbm] * len(needed),
        out_specs=[vm] * (2 * len(ds)),
        out_shape=[jax.ShapeDtypeStruct((half, width), dtype)] * (2 * len(ds)),
        scratch_shapes=[
            pltpu.VMEM((sum(u > 0 for u in users), max(users) * CAP, width), bf),
            pltpu.VMEM((len(ds), most * CAP, 2 * half), bf),
            pltpu.VMEM((len(ds), most * CAP, width), bf),
            pltpu.VMEM((max(users) * CAP, width), jnp.float32),
            pltpu.VMEM((2, max(users) * CAP, CHUNK), jnp.float32),
            pltpu.VMEM((2, width, ff), bf),
            pltpu.VMEM((2, ff, width), bf),
            pltpu.SemaphoreType.DMA((2, 12)),
        ],
        compiler_params=pltpu.CompilerParams(vmem_limit_bytes=60 << 20),
        cost_estimate=pl.CostEstimate(
            flops=2 * work, bytes_accessed=12_000_000, transcendentals=sum(users) * CAP * ff
        ),
    )(who, router, *given, *[a for d in kept for a in prior[d]], *needed)
    return {d: tuple(got[2 * i : 2 * i + 2]) for i, d in enumerate(ds)}


def around(step):
    count = lax.axis_size("z")
    return [(i, (i + step) % count) for i in range(count)]


def add(a, b):
    return (a.astype(jnp.float32) + b.astype(jnp.float32)).astype(jnp.bfloat16)


def after(x, *others):
    return lax.optimization_barrier((x, *others))[0]


def expert_layer(x, who, router, weights, pieces):
    ahead, back = around(1), around(-1)
    send = lambda a, way: lax.ppermute(a, "z", way)
    near, far, every = (0, 1), (2, 3), (0, 1, 2, 3)
    wide, bf = jnp.float32, jnp.bfloat16
    half = (x.shape[0] - 16) // 2
    part, one, two, part_o = pieces
    width = part.shape[1]
    blocks, so_far = {0: (x,)}, {}
    weights = list(weights)
    run = lambda plan, dtype, prior={}: experts(plan, who, router, blocks, prior, weights, dtype)

    def keep(results, *arrays):
        flat = [a for d in results for a in results[d]]
        out = lax.optimization_barrier((*arrays, *flat))
        held = out[len(arrays) :]
        so_far.update({d: held[2 * i : 2 * i + 2] for i, d in enumerate(results)})
        return out[: len(arrays)]

    f, b = send(x, ahead), send(x, back)
    up, down = both_ways(one[:width], two[width:])
    f, b, up, down = keep({}, f, b, up, down)
    blocks[1], blocks[7] = (f,), (b,)
    f, b = send(f, ahead), send(b, back)
    one_o, two_o = swap(one), swap(two)
    f, b, one_o, two_o = keep(run({0: near, 1: near, 7: near}, wide), f, b, one_o, two_o)
    blocks[2], blocks[6] = (f,), (b,)
    f, b = send(f, ahead), send(b, back)
    up_o, down_o = swap(up), swap(down)
    f, b, up_o, down_o = keep(run({2: near, 6: near}, wide), f, b, up_o, down_o)
    blocks[3], blocks[5] = (f,), (b,)
    weights += [(part, one, two, up, down), (part_o, one_o, two_o, up_o, down_o)]
    f, b = send(f[:half], ahead), send(b[half:], back)
    parts = run({3: every, 5: every}, bf)
    blocks[4] = tuple(lax.optimization_barrier((f, b, *parts[3], *parts[5]))[:2])
    f1, b0 = send(parts[3][1], back), send(parts[5][0], ahead)
    parts.update(run({4: every}, bf))
    f0, b1 = send(parts[4][0], back), send(parts[4][1], ahead)
    blocks[2] = (after(blocks[2][0], *parts[4]),)
    parts.update(run({2: far, 6: far}, bf, so_far))
    f1, b0 = add(f1, parts[2][1]), add(b0, parts[6][0])
    f0, b1 = add(f0, parts[3][0]), add(b1, parts[5][1])
    blocks[0] = (after(x, f0, b1, f1, b0),)
    f1, b0 = send(f1, back), send(b0, ahead)
    f0, b1 = send(f0, back), send(b1, ahead)
    parts.update(run({1: far, 7: far, 0: far}, bf, so_far))
    f1, b0 = send(add(f1, parts[1][1]), back), send(add(b0, parts[7][0]), ahead)
    f0, b1 = send(add(f0, parts[2][0]), back), send(add(b1, parts[6][1]), ahead)
    f0, b1 = send(add(f0, parts[1][0]), back), send(add(b1, parts[7][1]), ahead)
    return [(parts[0][0], f0, b0), (parts[0][1], f1, b1)]


def far_piece(w_in, w_down):
    piece = w_in.shape[1] // lax.axis_size("y")
    first = lax.axis_index("y") * piece
    quarter = jnp.concatenate(
        [
            lax.dynamic_slice_in_dim(w_in, first, piece, 1),
            lax.dynamic_slice_in_dim(w_down, first, piece, 0),
        ],
        axis=0,
    )
    return lax.ppermute(quarter, ("xh", "xl"), [(0, 3), (3, 0), (1, 2), (2, 1)])


def both_ways(a, b):
    count = lax.axis_size("y")
    ahead = [(i, (i + 1) % count) for i in range(count)]
    back = [(i, (i - 1) % count) for i in range(count)]
    return lax.ppermute(a, "y", ahead), lax.ppermute(b, "y", back)


def swap(a):
    return lax.ppermute(a, "core", [(0, 1), (1, 0)])


def per_device(
    tokens, die_mask, expert_ids, gain_attn, w_qkv, w_out, gain_moe, w_router, w_in, w_down
):
    ht, wt, width = tokens.shape
    patches = ht * wt
    w_in, w_down = w_in[0], w_down[0]
    top, bot = halo_rows(tokens, die_mask)
    to_right, to_left = halo_edges(tokens, die_mask, top, bot)
    part = far_piece(w_in, w_down)
    left = lax.ppermute(to_right, COL, ahead_of(COL))
    right = lax.ppermute(to_left, COL, behind(COL))
    other = swap(w_in), swap(w_down)
    right, part, *other = lax.optimization_barrier((right, part, *other))
    one, two = both_ways(part, part)
    part_o = swap(part)
    ids = expert_ids.reshape(patches, 2).T
    marks = jnp.broadcast_to(die_mask.astype(jnp.bfloat16)[..., None], (ht, wt, LANES))
    resid, x = attention(
        tokens, marks, top, bot, left, right, gain_attn, w_qkv, w_out, gain_moe, ids
    )
    who = lax.axis_index(ROW).reshape(1).astype(jnp.int32)
    x, one, two, part_o = lax.optimization_barrier((x, one, two, part_o))
    weights = ((w_in, w_down), tuple(other))
    wide = lambda a: a.astype(jnp.float32)
    moe = expert_layer(x, who, w_router.T, weights, (part, one, two, part_o))
    moe = jnp.concatenate([wide(p) + (wide(f) + wide(b)) for p, f, b in moe], axis=0)
    final = (wide(resid) + moe).astype(jnp.bfloat16)
    return final.reshape(ht, wt, width)


def solution(mesh):
    fine = Mesh(mesh.devices.reshape(8, 2, 2, 2, 4), ROW + COL)
    return jax.shard_map(
        per_device,
        mesh=fine,
        in_specs=(
            P(ROW, COL, None),
            P(ROW, COL),
            P(ROW, COL, None, None),
            P(),
            P(),
            P(),
            P(),
            P(),
            P(ROW, None, None),
            P(ROW, None, None),
        ),
        out_specs=P(ROW, COL, None),
        check_vma=False,
    )
```

```python
import functools

import jax
import jax.numpy as jnp
import numpy as np
from jax import lax
from jax.experimental import pallas as pl
from jax.experimental.pallas import tpu as pltpu
from jax.sharding import Mesh, PartitionSpec as P

HEADS = 16
RADIUS = 6
CAP = 96
SIDE = 8
QROWS = 4
LANES = 128
BIG = 1e30

ROW = ("z", "xh", "core")
COL = ("xl", "y")


def norm(wide, gain):
    power = jnp.mean(wide * wide, axis=-1, keepdims=True)
    return (wide * lax.rsqrt(power + 1e-06) * gain).astype(jnp.bfloat16)


def window_bias(marks, wt):
    keyw = wt + 2 * SIDE
    shape = (QROWS + 2 * RADIUS, keyw, QROWS * wt)
    kr, kc, q = (lax.broadcasted_iota(jnp.int32, shape, i) for i in range(3))
    col = jnp.where(kc < wt + SIDE, kc, kc - keyw)
    rise = kr - q // wt - RADIUS
    reach = col - q % wt
    inside = (jnp.abs(rise) <= RADIUS) & (jnp.abs(reach) <= RADIUS)
    centre = (rise == 0) & (reach == 0)
    open_ = (inside & (marks.reshape(shape) > 0.5)) | centre
    return jnp.where(open_, 0.0, -BIG).reshape(shape[0] * shape[1], shape[2])


def attention_kernel(
    gain_ref, gain2_ref, ids_ref, *refs,
):
    sources, (resid_ref, moe_ref), refs = refs[:8], refs[8:10], refs[10:]
    xn, marks, keys, vals, kaug, vaug, qaug, *local, sem = refs
    tok_ref, mask_ref, top_ref, bot_ref, left_ref, right_ref, wqkv_ref, wout_ref = local
    ht, wt, width = tok_ref.shape
    keyw = wt + 2 * SIDE
    krows = QROWS + 2 * RADIUS
    slab = krows * keyw
    nq = QROWS * wt
    gain = gain_ref[...]
    step = pl.program_id(0)

    @pl.when(step == 0)
    def _prepare():
        fetch = [
            pltpu.make_async_copy(src, dst, sem.at[i])
            for i, (src, dst) in enumerate(zip(sources, local))
        ]
        for cp in fetch:
            cp.start()

        def rows(first, count, body_of):
            @pl.loop(0, count)
            def _row(i):
                body, mark = body_of(i)
                at = pl.multiple_of((first + i) * keyw, 16)
                xn[pl.ds(at, wt), :] = norm(body.astype(jnp.float32), gain)
                marks[pl.ds(at, wt), :] = mark.astype(jnp.float32)
                edge = jnp.concatenate(
                    [
                        right_ref[first + i].astype(jnp.float32),
                        left_ref[first + i].astype(jnp.float32),
                    ],
                    axis=0,
                )
                beside = pl.ds(pl.multiple_of(at + wt, 16), 2 * SIDE)
                xn[beside, :] = norm(edge[:, :width], gain)
                marks[beside, :] = edge[:, width:]

        for cp in fetch[:6]:
            cp.wait()
        rows(0, RADIUS, lambda i: (top_ref[i, :, :width], top_ref[i, :, width:]))
        rows(RADIUS, ht, lambda i: (tok_ref[i], mask_ref[i]))
        rows(ht + RADIUS, RADIUS, lambda i: (bot_ref[i, :, :width], bot_ref[i, :, width:]))
        for cp in fetch[6:]:
            cp.wait()
        every = xn[...]
        keys[...] = jnp.dot(
            every, wqkv_ref[:, width : 2 * width], preferred_element_type=jnp.float32
        ).astype(jnp.bfloat16)
        vals[...] = jnp.dot(
            every, wqkv_ref[:, 2 * width :], preferred_element_type=jnp.float32
        ).astype(jnp.bfloat16)
        for p in range(2):
            vaug[p, :, LANES:] = jnp.ones((slab, LANES), jnp.bfloat16)
        spot = lax.broadcasted_iota(jnp.int32, (nq, nq), 0)
        lane = lax.broadcasted_iota(jnp.int32, (nq, nq), 1)
        unit = (spot == lane).astype(jnp.bfloat16)
        for i in range(4):
            for p in range(2):
                qaug[p, i * nq : (i + 1) * nq, LANES:] = unit
        named = ids_ref[...].astype(jnp.float32)
        spare = jnp.zeros((16 - named.shape[0], named.shape[1]), jnp.float32)
        moe_ref[ht * wt :, :] = jnp.concatenate([named, spare], axis=0).astype(jnp.bfloat16)

    base = pl.multiple_of(step * (QROWS * keyw), QROWS * keyw)
    own = [
        xn[pl.ds(pl.multiple_of(base + (RADIUS + i) * keyw, 16), wt), :] for i in range(QROWS)
    ]
    query = jnp.dot(
        jnp.concatenate(own, axis=0), wqkv_ref[:, :width], preferred_element_type=jnp.float32
    )
    hdim = width // HEADS
    query = (query * hdim ** (-0.5)).astype(jnp.bfloat16)
    bias = window_bias(marks[pl.ds(base, slab), :], wt).astype(jnp.bfloat16)
    for p in range(2):
        kaug[p, :, LANES:] = bias
    per = LANES // hdim
    head_of = lax.broadcasted_iota(jnp.int32, (nq, LANES), 1) // hdim
    pieces = []
    for g in range(width // LANES):
        cols = slice(g * LANES, (g + 1) * LANES)
        qg = query[:, cols]
        for i in range(per):
            qaug[g % 2, i * nq : (i + 1) * nq, :LANES] = jnp.where(head_of == i, qg, 0).astype(
                jnp.bfloat16
            )
        kaug[g % 2, :, :LANES] = keys[pl.ds(base, slab), cols]
        vaug[g % 2, :, :LANES] = vals[pl.ds(base, slab), cols]
        scores = lax.dot_general(
            qaug[g % 2], kaug[g % 2], (((1,), (1,)), ((), ())), preferred_element_type=jnp.float32
        )
        highest = jnp.max(scores, axis=-1, keepdims=True)
        weights = jnp.exp(scores - highest).astype(jnp.bfloat16)
        mixed = jnp.dot(weights, vaug[g % 2], preferred_element_type=jnp.float32)
        share = mixed[:, :LANES] / mixed[:, LANES:]
        both = share[:nq]
        for i in range(1, per):
            both = jnp.where(head_of == i, share[i * nq : (i + 1) * nq], both)
        pieces.append(both.astype(jnp.bfloat16))
    attended = jnp.concatenate(pieces, axis=1)
    mixed = jnp.dot(attended, wout_ref[...], preferred_element_type=jnp.float32)
    mine = tok_ref[pl.ds(step * QROWS, QROWS)].reshape(nq, width)
    resid = (mine.astype(jnp.float32) + mixed).astype(jnp.bfloat16)
    resid_ref[...] = resid
    moe_ref[pl.ds(pl.multiple_of(step * nq, nq), nq), :] = norm(
        resid.astype(jnp.float32), gain2_ref[...]
    )


def attention(tokens, marks, top, bot, left, right, gain, wqkv, wout, gain2, ids):
    ht, wt, width = tokens.shape
    slab, nq = (QROWS + 2 * RADIUS) * (wt + 2 * SIDE), QROWS * wt
    total = (ht + 2 * RADIUS) * (wt + 2 * SIDE)
    whole = lambda a: pl.BlockSpec(a.shape, functools.partial(lambda n, i: (0,) * n, a.ndim))
    args = (gain.reshape(1, width), gain2.reshape(1, width), ids)
    large = (tokens, marks, top, bot, left, right, wqkv, wout)
    bf = jnp.bfloat16
    return pl.pallas_call(
        attention_kernel,
        grid=(ht // QROWS,),
        in_specs=[whole(a) for a in args] + [pl.BlockSpec(memory_space=pl.ANY)] * len(large),
        out_specs=[
            pl.BlockSpec((nq, width), lambda i: (i, 0)),
            pl.BlockSpec((ht * wt + 16, width), lambda i: (0, 0)),
        ],
        out_shape=[
            jax.ShapeDtypeStruct((ht * wt, width), bf),
            jax.ShapeDtypeStruct((ht * wt + 16, width), bf),
        ],
        scratch_shapes=[
            pltpu.VMEM((total, width), bf),
            pltpu.VMEM((total, LANES), jnp.float32),
            pltpu.VMEM((total, width), bf),
            pltpu.VMEM((total, width), bf),
            pltpu.VMEM((2, slab, 2 * LANES), bf),
            pltpu.VMEM((2, slab, 2 * LANES), bf),
            pltpu.VMEM((2, 4 * nq, 2 * LANES), bf),
            *[pltpu.VMEM(a.shape, bf) for a in large],
            pltpu.SemaphoreType.DMA((len(large),)),
        ],
        compiler_params=pltpu.CompilerParams(vmem_limit_bytes=60 << 20),
        cost_estimate=pl.CostEstimate(
            flops=10_000_000_000, bytes_accessed=6_000_000, transcendentals=6_000_000
        ),
    )(*args, *large)


def with_marks(tokens, mask):
    marks = jnp.broadcast_to(mask.astype(jnp.bfloat16)[..., None], (*mask.shape, LANES))
    return jnp.concatenate([tokens, marks], axis=-1)


def ahead_of(axis):
    return [(i, i + 1) for i in range(lax.axis_size(axis) - 1)]


def behind(axis):
    return [(i + 1, i) for i in range(lax.axis_size(axis) - 1)]


def halo_rows(tokens, mask):
    ht = tokens.shape[0]
    low, high = slice(ht - RADIUS, ht), slice(0, RADIUS)
    top = lax.ppermute(with_marks(tokens[low], mask[low]), ROW, ahead_of(ROW))
    bot = lax.ppermute(with_marks(tokens[high], mask[high]), ROW, behind(ROW))
    return top, bot


def halo_edges(tokens, mask, top, bot):
    def edge(cols):
        mine = with_marks(tokens[:, cols], mask[:, cols])
        return jnp.concatenate([top[:, cols], mine, bot[:, cols]], axis=0)

    wt = tokens.shape[1]
    return edge(slice(wt - SIDE, wt)), edge(slice(0, SIDE))


CHUNK = 512


def experts_kernel(plan, who_ref, wr_ref, *refs):
    ds = list(plan)
    blocks, at = {}, 0
    for d in ds:
        blocks[d] = refs[at : at + (2 if d == 4 else 1)]
        at += len(blocks[d])
    users = {j: [d for d in ds if j in plan[d]] for j in range(4)}
    todo = [j for j in range(4) if users[j]]
    held_w = {}
    for j in todo:
        held_w[j] = refs[at : at + (2 if j < 2 else 5)]
        at += len(held_w[j])
    outs = {d: refs[at + 2 * i : at + 2 * i + 2] for i, d in enumerate(ds)}
    rows, share, done, acc, raw, buf_in, buf_down, held_x, sem, sem_x = refs[at + 2 * len(ds) :]
    width = rows.shape[-1]
    patches = share.shape[-1]
    ff = buf_in.shape[-1]
    chunks = ff // CHUNK
    piece = ff // 4
    me = who_ref[0]

    def copies(n):
        j, slot = todo[n], n % 2
        put = lambda src, dst, i: pltpu.make_async_copy(src, dst, sem.at[slot, i])
        if j < 2:
            return (
                put(held_w[j][0], buf_in.at[slot], 0),
                put(held_w[j][1], buf_down.at[slot], 1),
            )
        out = []
        for i, ref in enumerate(held_w[j]):
            span = pl.ds(min(i, 3) * piece, piece)
            if i < 4:
                src = ref.at[pl.ds(0, width)]
                out.append(put(src, buf_in.at[slot, :, span], 2 * i))
            if i != 3:
                src = ref.at[pl.ds(width, piece)] if i < 3 else ref
                out.append(put(src, buf_down.at[slot, span, :], 2 * i + 1))
        return out

    def arrive(i):
        out, first = [], 0
        for k, ref in enumerate(blocks[ds[i]]):
            n = ref.shape[0]
            out.append(
                pltpu.make_async_copy(ref, held_x.at[i, pl.ds(first, n)], sem_x.at[i, k])
            )
            first += n
        return out

    for i in range(len(ds)):
        for c in arrive(i):
            c.start()
    for c in copies(0):
        c.start()
    before = lax.broadcasted_iota(jnp.int32, (patches, patches), 0)
    after = lax.broadcasted_iota(jnp.int32, (patches, patches), 1)
    upper = (before < after).astype(jnp.bfloat16)
    slot_of = lax.broadcasted_iota(jnp.int32, (CAP, patches), 0).astype(jnp.float32)
    held = [me ^ j for j in range(4)]
    lane_expert = lax.broadcasted_iota(jnp.int32, (wr_ref.shape[0], patches), 0)
    for i, d in enumerate(ds):
        for c in arrive(i):
            c.wait()
        x = held_x[i, :patches]
        ids = held_x[i, patches:].astype(jnp.float32).astype(jnp.int32)
        e0, e1 = ids[0:1], ids[1:2]
        logits = lax.dot_general(
            wr_ref[...], x, (((1,), (1,)), ((), ())), preferred_element_type=jnp.float32
        )
        pick = lambda e: jnp.sum(jnp.where(lane_expert == e, logits, 0.0), axis=0, keepdims=True)
        gap = pick(e0) - pick(e1)
        g0, g1 = jax.nn.sigmoid(gap), jax.nn.sigmoid(-gap)
        named = [((e0 == h) | (e1 == h)).astype(jnp.float32) for h in held]
        hot = jnp.concatenate(named + named, axis=0)
        rank = jnp.dot(hot.astype(jnp.bfloat16), upper, preferred_element_type=jnp.float32)
        for k, j in enumerate(plan[d]):
            place = jnp.where(named[j] > 0.5, rank[j : j + 1], -1.0)
            hit = slot_of == place
            gate = jnp.where(e0 == held[j], g0, g1)
            share[i, k * CAP : (k + 1) * CAP, :] = jnp.where(hit, gate, 0.0).astype(jnp.bfloat16)
            one = hit.astype(jnp.float32).astype(jnp.bfloat16)
            u = users[j].index(d)
            rows[todo.index(j), u * CAP : (u + 1) * CAP, :] = jnp.dot(
                one, x, preferred_element_type=jnp.float32
            ).astype(jnp.bfloat16)
    for n, j in enumerate(todo):
        if n + 1 < len(todo):
            for cp in copies(n + 1):
                cp.start()
        for cp in copies(n):
            cp.wait()
        m = len(users[j]) * CAP
        slot = n % 2

        def up(c):
            return jnp.dot(
                rows[n, :m],
                buf_in[slot, :, pl.ds(pl.multiple_of(c * CHUNK, CHUNK), CHUNK)],
                preferred_element_type=jnp.float32,
            )

        def down(c, hidden):
            return jnp.dot(
                jax.nn.gelu(hidden, approximate=True).astype(jnp.bfloat16),
                buf_down[slot, pl.ds(pl.multiple_of(c * CHUNK, CHUNK), CHUNK), :],
                preferred_element_type=jnp.float32,
            )

        raw[0, :m] = up(0)
        acc[:m] = jnp.zeros((m, width), jnp.float32)

        @pl.loop(0, chunks - 1)
        def _chunk(c):
            now = lax.rem(c, 2)
            raw[1 - now, :m] = up(c + 1)
            acc[:m] += down(c, raw[now, :m])

        whole = (acc[:m] + down(chunks - 1, raw[(chunks - 1) % 2, :m])).astype(jnp.bfloat16)
        for u, d in enumerate(users[j]):
            k = plan[d].index(j)
            done[ds.index(d), k * CAP : (k + 1) * CAP, :] = whole[u * CAP : (u + 1) * CAP]
    for i, d in enumerate(ds):
        n = len(plan[d]) * CAP
        total = lax.dot_general(
            share[i, :n], done[i, :n], (((0,), (0,)), ((), ())), preferred_element_type=jnp.float32
        )
        for h, out in enumerate(outs[d]):
            out[...] = total[h * out.shape[0] : (h + 1) * out.shape[0]].astype(out.dtype)


def experts(plan, who, router, blocks, weights):
    ds = list(plan)
    width, ff = weights[0][0].shape
    half = (sum(a.shape[0] for a in blocks[ds[0]]) - 16) // 2
    most = max(len(v) for v in plan.values())
    users = [sum(j in v for v in plan.values()) for j in range(4)]
    needed = [w for j in range(4) if users[j] for w in weights[j]]
    given = [a for d in ds for a in blocks[d]]
    vm = pl.BlockSpec(memory_space=pltpu.VMEM)
    hbm = pl.BlockSpec(memory_space=pl.ANY)
    bf = jnp.bfloat16
    work = sum(users) * CAP * width * ff * 4
    got = pl.pallas_call(
        functools.partial(experts_kernel, plan),
        in_specs=[pl.BlockSpec(memory_space=pltpu.SMEM), vm] + [hbm] * (len(given) + len(needed)),
        out_specs=[vm] * (2 * len(ds)),
        out_shape=[jax.ShapeDtypeStruct((half, width), bf)] * (2 * len(ds)),
        scratch_shapes=[
            pltpu.VMEM((sum(u > 0 for u in users), max(users) * CAP, width), bf),
            pltpu.VMEM((len(ds), most * CAP, 2 * half), bf),
            pltpu.VMEM((len(ds), most * CAP, width), bf),
            pltpu.VMEM((max(users) * CAP, width), jnp.float32),
            pltpu.VMEM((2, max(users) * CAP, CHUNK), jnp.float32),
            pltpu.VMEM((2, width, ff), bf),
            pltpu.VMEM((2, ff, width), bf),
            pltpu.VMEM((len(ds), 2 * half + 16, width), bf),
            pltpu.SemaphoreType.DMA((2, 12)),
            pltpu.SemaphoreType.DMA((len(ds), 2)),
        ],
        compiler_params=pltpu.CompilerParams(vmem_limit_bytes=60 << 20),
        cost_estimate=pl.CostEstimate(
            flops=2 * work, bytes_accessed=12_000_000, transcendentals=sum(users) * CAP * ff
        ),
    )(who, router, *given, *needed)
    return {d: tuple(got[2 * i : 2 * i + 2]) for i, d in enumerate(ds)}


def around(step):
    count = lax.axis_size("z")
    return [(i, (i + step) % count) for i in range(count)]


def add(*arrays):
    return sum(a.astype(jnp.float32) for a in arrays).astype(jnp.bfloat16)


def after(x, *others):
    return lax.optimization_barrier((x, *others))[0]


def expert_layer(x, who, router, weights, part):
    ahead, back = around(1), around(-1)
    send = lambda a, way: lax.ppermute(a, "z", way)
    near, far, every = (0, 1), (2, 3), (0, 1, 2, 3)
    half = (x.shape[0] - 16) // 2
    width = x.shape[1]
    blocks, so_far = {0: (x,)}, {}
    weights = list(weights)
    run = lambda plan: experts(plan, who, router, blocks, weights)

    def keep(results, *arrays):
        flat = [a for d in results for a in results[d]]
        out = lax.optimization_barrier((*arrays, *flat))
        held = out[len(arrays) :]
        so_far.update({d: held[2 * i : 2 * i + 2] for i, d in enumerate(results)})
        return out[: len(arrays)]

    f, b = send(x, ahead), send(x, back)
    one, two = both_ways(part, part)
    f, b, one, two = keep({}, f, b, one, two)
    blocks[1], blocks[7] = (f,), (b,)
    f, b = send(f, ahead), send(b, back)
    up, down = both_ways(one[:width], two[width:])
    part_o = swap(part)
    f, b, up, down, part_o = keep(run({0: near, 1: near, 7: near}), f, b, up, down, part_o)
    blocks[2], blocks[6] = (f,), (b,)
    f, b = send(f, ahead), send(b, back)
    one_o, two_o, up_o, down_o = swap(one), swap(two), swap(up), swap(down)
    f, b, one_o, two_o, up_o, down_o = keep(
        run({2: near, 6: near}), f, b, one_o, two_o, up_o, down_o
    )
    blocks[3], blocks[5] = (f,), (b,)
    weights += [(part, one, two, up, down), (part_o, one_o, two_o, up_o, down_o)]
    f, b = send(f[:half], ahead), send(b[half:], back)
    parts = run({2: far, 6: far, 1: far, 7: far, 0: far})
    last = [a for d in parts for a in parts[d]]
    f, b = lax.optimization_barrier((f, b, *last))[:2]
    blocks[4] = (f, b)
    parts.update(run({4: every, 3: every, 5: every}))
    f0, b1 = send(parts[4][0], back), send(parts[4][1], ahead)
    f1, b0 = send(parts[3][1], back), send(parts[5][0], ahead)
    f0, b1 = send(add(f0, parts[3][0]), back), send(add(b1, parts[5][1]), ahead)
    for i in (2, 1):
        f1 = send(add(f1, parts[i][1], so_far[i][1]), back)
        b0 = send(add(b0, parts[8 - i][0], so_far[8 - i][0]), ahead)
        f0 = send(add(f0, parts[i][0], so_far[i][0]), back)
        b1 = send(add(b1, parts[8 - i][1], so_far[8 - i][1]), ahead)
    return [(parts[0][0], so_far[0][0], f0, b0), (parts[0][1], so_far[0][1], f1, b1)]


def far_piece(w_in, w_down):
    piece = w_in.shape[1] // lax.axis_size("y")
    first = lax.axis_index("y") * piece
    quarter = jnp.concatenate(
        [
            lax.dynamic_slice_in_dim(w_in, first, piece, 1),
            lax.dynamic_slice_in_dim(w_down, first, piece, 0),
        ],
        axis=0,
    )
    return lax.ppermute(quarter, ("xh", "xl"), [(0, 3), (3, 0), (1, 2), (2, 1)])


def both_ways(a, b):
    count = lax.axis_size("y")
    ahead = [(i, (i + 1) % count) for i in range(count)]
    back = [(i, (i - 1) % count) for i in range(count)]
    return lax.ppermute(a, "y", ahead), lax.ppermute(b, "y", back)


def swap(a):
    return lax.ppermute(a, "core", [(0, 1), (1, 0)])


def per_device(
    tokens, die_mask, expert_ids, gain_attn, w_qkv, w_out, gain_moe, w_router, w_in, w_down
):
    ht, wt, width = tokens.shape
    patches = ht * wt
    w_in, w_down = w_in[0], w_down[0]
    top, bot = halo_rows(tokens, die_mask)
    to_right, to_left = halo_edges(tokens, die_mask, top, bot)
    left = lax.ppermute(to_right, COL, ahead_of(COL))
    right = lax.ppermute(to_left, COL, behind(COL))
    late_in, late_down = after(w_in, top, bot), after(w_down, top, bot)
    part = far_piece(late_in, late_down)
    other = swap(late_in), swap(late_down)
    ids = expert_ids.reshape(patches, 2).T
    marks = jnp.broadcast_to(die_mask.astype(jnp.bfloat16)[..., None], (ht, wt, LANES))
    resid, x = attention(
        tokens, marks, top, bot, left, right, gain_attn, w_qkv, w_out, gain_moe, ids
    )
    who = lax.axis_index(ROW).reshape(1).astype(jnp.int32)
    x, part, *other = lax.optimization_barrier((x, part, *other))
    weights = ((w_in, w_down), tuple(other))
    wide = lambda a: a.astype(jnp.float32)
    moe = expert_layer(x, who, w_router.T, weights, part)
    moe = jnp.concatenate([sum(wide(a) for a in half) for half in moe], axis=0)
    final = (wide(resid) + moe).astype(jnp.bfloat16)
    return final.reshape(ht, wt, width)


def solution(mesh):
    fine = Mesh(mesh.devices.reshape(8, 2, 2, 2, 4), ROW + COL)
    return jax.shard_map(
        per_device,
        mesh=fine,
        in_specs=(
            P(ROW, COL, None),
            P(ROW, COL),
            P(ROW, COL, None, None),
            P(),
            P(),
            P(),
            P(),
            P(),
            P(ROW, None, None),
            P(ROW, None, None),
        ),
        out_specs=P(ROW, COL, None),
        check_vma=False,
    )
```

```python
import functools

import jax
import jax.numpy as jnp
import numpy as np
from jax import lax
from jax.experimental import pallas as pl
from jax.experimental.pallas import tpu as pltpu
from jax.sharding import Mesh, PartitionSpec as P

HEADS = 16
RADIUS = 6
CAP = 96
SIDE = 8
QROWS = 4
LANES = 128
BIG = 1e30

ROW = ("z", "xh", "core")
COL = ("xl", "y")


def norm(wide, gain):
    power = jnp.mean(wide * wide, axis=-1, keepdims=True)
    return (wide * lax.rsqrt(power + 1e-06) * gain).astype(jnp.bfloat16)


def window_bias(marks, wt):
    keyw = wt + 2 * SIDE
    shape = (QROWS + 2 * RADIUS, keyw, QROWS * wt)
    kr, kc, q = (lax.broadcasted_iota(jnp.int32, shape, i) for i in range(3))
    col = jnp.where(kc < wt + SIDE, kc, kc - keyw)
    rise = kr - q // wt - RADIUS
    reach = col - q % wt
    inside = (jnp.abs(rise) <= RADIUS) & (jnp.abs(reach) <= RADIUS)
    centre = (rise == 0) & (reach == 0)
    open_ = (inside & (marks.reshape(shape) > 0.5)) | centre
    return jnp.where(open_, 0.0, -BIG).reshape(shape[0] * shape[1], shape[2])


def attention_kernel(
    gain_ref, gain2_ref, ids_ref, *refs,
):
    sources, (resid_ref, moe_ref), refs = refs[:8], refs[8:10], refs[10:]
    xn, marks, keys, vals, kaug, vaug, qaug, *local, sem = refs
    tok_ref, mask_ref, top_ref, bot_ref, left_ref, right_ref, wqkv_ref, wout_ref = local
    ht, wt, width = tok_ref.shape
    keyw = wt + 2 * SIDE
    krows = QROWS + 2 * RADIUS
    slab = krows * keyw
    nq = QROWS * wt
    gain = gain_ref[...]
    step = pl.program_id(0)

    @pl.when(step == 0)
    def _prepare():
        fetch = [
            pltpu.make_async_copy(src, dst, sem.at[i])
            for i, (src, dst) in enumerate(zip(sources, local))
        ]
        for cp in fetch:
            cp.start()

        def rows(first, count, body_of):
            @pl.loop(0, count)
            def _row(i):
                body, mark = body_of(i)
                at = pl.multiple_of((first + i) * keyw, 16)
                xn[pl.ds(at, wt), :] = norm(body.astype(jnp.float32), gain)
                marks[pl.ds(at, wt), :] = mark.astype(jnp.float32)
                edge = jnp.concatenate(
                    [
                        right_ref[first + i].astype(jnp.float32),
                        left_ref[first + i].astype(jnp.float32),
                    ],
                    axis=0,
                )
                beside = pl.ds(pl.multiple_of(at + wt, 16), 2 * SIDE)
                xn[beside, :] = norm(edge[:, :width], gain)
                marks[beside, :] = edge[:, width:]

        for cp in fetch[:6]:
            cp.wait()
        rows(0, RADIUS, lambda i: (top_ref[i, :, :width], top_ref[i, :, width:]))
        rows(RADIUS, ht, lambda i: (tok_ref[i], mask_ref[i]))
        rows(ht + RADIUS, RADIUS, lambda i: (bot_ref[i, :, :width], bot_ref[i, :, width:]))
        for cp in fetch[6:]:
            cp.wait()
        every = xn[...]
        keys[...] = jnp.dot(
            every, wqkv_ref[:, width : 2 * width], preferred_element_type=jnp.float32
        ).astype(jnp.bfloat16)
        vals[...] = jnp.dot(
            every, wqkv_ref[:, 2 * width :], preferred_element_type=jnp.float32
        ).astype(jnp.bfloat16)
        for p in range(2):
            vaug[p, :, LANES:] = jnp.ones((slab, LANES), jnp.bfloat16)
        spot = lax.broadcasted_iota(jnp.int32, (nq, nq), 0)
        lane = lax.broadcasted_iota(jnp.int32, (nq, nq), 1)
        unit = (spot == lane).astype(jnp.bfloat16)
        for i in range(4):
            for p in range(2):
                qaug[p, i * nq : (i + 1) * nq, LANES:] = unit
        named = ids_ref[...].astype(jnp.float32)
        spare = jnp.zeros((16 - named.shape[0], named.shape[1]), jnp.float32)
        moe_ref[ht * wt :, :] = jnp.concatenate([named, spare], axis=0).astype(jnp.bfloat16)

    base = pl.multiple_of(step * (QROWS * keyw), QROWS * keyw)
    own = [
        xn[pl.ds(pl.multiple_of(base + (RADIUS + i) * keyw, 16), wt), :] for i in range(QROWS)
    ]
    query = jnp.dot(
        jnp.concatenate(own, axis=0), wqkv_ref[:, :width], preferred_element_type=jnp.float32
    )
    hdim = width // HEADS
    query = (query * hdim ** (-0.5)).astype(jnp.bfloat16)
    bias = window_bias(marks[pl.ds(base, slab), :], wt).astype(jnp.bfloat16)
    for p in range(2):
        kaug[p, :, LANES:] = bias
    per = LANES // hdim
    head_of = lax.broadcasted_iota(jnp.int32, (nq, LANES), 1) // hdim
    pieces = []
    for g in range(width // LANES):
        cols = slice(g * LANES, (g + 1) * LANES)
        qg = query[:, cols]
        for i in range(per):
            qaug[g % 2, i * nq : (i + 1) * nq, :LANES] = jnp.where(head_of == i, qg, 0).astype(
                jnp.bfloat16
            )
        kaug[g % 2, :, :LANES] = keys[pl.ds(base, slab), cols]
        vaug[g % 2, :, :LANES] = vals[pl.ds(base, slab), cols]
        scores = lax.dot_general(
            qaug[g % 2], kaug[g % 2], (((1,), (1,)), ((), ())), preferred_element_type=jnp.float32
        )
        highest = jnp.max(scores, axis=-1, keepdims=True)
        weights = jnp.exp(scores - highest).astype(jnp.bfloat16)
        mixed = jnp.dot(weights, vaug[g % 2], preferred_element_type=jnp.float32)
        share = mixed[:, :LANES] / mixed[:, LANES:]
        both = share[:nq]
        for i in range(1, per):
            both = jnp.where(head_of == i, share[i * nq : (i + 1) * nq], both)
        pieces.append(both.astype(jnp.bfloat16))
    attended = jnp.concatenate(pieces, axis=1)
    mixed = jnp.dot(attended, wout_ref[...], preferred_element_type=jnp.float32)
    mine = tok_ref[pl.ds(step * QROWS, QROWS)].reshape(nq, width)
    resid = (mine.astype(jnp.float32) + mixed).astype(jnp.bfloat16)
    resid_ref[...] = resid
    moe_ref[pl.ds(pl.multiple_of(step * nq, nq), nq), :] = norm(
        resid.astype(jnp.float32), gain2_ref[...]
    )


def attention(tokens, marks, top, bot, left, right, gain, wqkv, wout, gain2, ids):
    ht, wt, width = tokens.shape
    slab, nq = (QROWS + 2 * RADIUS) * (wt + 2 * SIDE), QROWS * wt
    total = (ht + 2 * RADIUS) * (wt + 2 * SIDE)
    whole = lambda a: pl.BlockSpec(a.shape, functools.partial(lambda n, i: (0,) * n, a.ndim))
    args = (gain.reshape(1, width), gain2.reshape(1, width), ids)
    large = (tokens, marks, top, bot, left, right, wqkv, wout)
    bf = jnp.bfloat16
    return pl.pallas_call(
        attention_kernel,
        grid=(ht // QROWS,),
        in_specs=[whole(a) for a in args] + [pl.BlockSpec(memory_space=pl.ANY)] * len(large),
        out_specs=[
            pl.BlockSpec((nq, width), lambda i: (i, 0)),
            pl.BlockSpec((ht * wt + 16, width), lambda i: (0, 0)),
        ],
        out_shape=[
            jax.ShapeDtypeStruct((ht * wt, width), bf),
            jax.ShapeDtypeStruct((ht * wt + 16, width), bf),
        ],
        scratch_shapes=[
            pltpu.VMEM((total, width), bf),
            pltpu.VMEM((total, LANES), jnp.float32),
            pltpu.VMEM((total, width), bf),
            pltpu.VMEM((total, width), bf),
            pltpu.VMEM((2, slab, 2 * LANES), bf),
            pltpu.VMEM((2, slab, 2 * LANES), bf),
            pltpu.VMEM((2, 4 * nq, 2 * LANES), bf),
            *[pltpu.VMEM(a.shape, bf) for a in large],
            pltpu.SemaphoreType.DMA((len(large),)),
        ],
        compiler_params=pltpu.CompilerParams(vmem_limit_bytes=60 << 20),
        cost_estimate=pl.CostEstimate(
            flops=10_000_000_000, bytes_accessed=6_000_000, transcendentals=6_000_000
        ),
    )(*args, *large)


def with_marks(tokens, mask):
    marks = jnp.broadcast_to(mask.astype(jnp.bfloat16)[..., None], (*mask.shape, LANES))
    return jnp.concatenate([tokens, marks], axis=-1)


def ahead_of(axis):
    return [(i, i + 1) for i in range(lax.axis_size(axis) - 1)]


def behind(axis):
    return [(i + 1, i) for i in range(lax.axis_size(axis) - 1)]


def halo_rows(tokens, mask):
    ht = tokens.shape[0]
    low, high = slice(ht - RADIUS, ht), slice(0, RADIUS)
    top = lax.ppermute(with_marks(tokens[low], mask[low]), ROW, ahead_of(ROW))
    bot = lax.ppermute(with_marks(tokens[high], mask[high]), ROW, behind(ROW))
    return top, bot


def halo_edges(tokens, mask, top, bot):
    def edge(cols):
        mine = with_marks(tokens[:, cols], mask[:, cols])
        return jnp.concatenate([top[:, cols], mine, bot[:, cols]], axis=0)

    wt = tokens.shape[1]
    return edge(slice(wt - SIDE, wt)), edge(slice(0, SIDE))


CHUNK = 512


def experts_kernel(plan, who_ref, wr_ref, *refs):
    ds = list(plan)
    blocks, at = {}, 0
    for d in ds:
        blocks[d] = refs[at : at + (2 if d == 4 else 1)]
        at += len(blocks[d])
    users = {j: [d for d in ds if j in plan[d]] for j in range(4)}
    todo = [j for j in range(4) if users[j]]
    held_w = {}
    for j in todo:
        held_w[j] = refs[at : at + (2 if j < 2 else 5)]
        at += len(held_w[j])
    outs = {d: refs[at + 2 * i : at + 2 * i + 2] for i, d in enumerate(ds)}
    rows, share, done, acc, raw, buf_in, buf_down, held_x, sem, sem_x = refs[at + 2 * len(ds) :]
    width = rows.shape[-1]
    patches = share.shape[-1]
    ff = buf_in.shape[-1]
    chunks = ff // CHUNK
    piece = ff // 4
    me = who_ref[0]

    def copies(n):
        j, slot = todo[n], n % 2
        put = lambda src, dst, i: pltpu.make_async_copy(src, dst, sem.at[slot, i])
        if j < 2:
            return (
                put(held_w[j][0], buf_in.at[slot], 0),
                put(held_w[j][1], buf_down.at[slot], 1),
            )
        out = []
        for i, ref in enumerate(held_w[j]):
            span = pl.ds(min(i, 3) * piece, piece)
            if i < 4:
                src = ref.at[pl.ds(0, width)]
                out.append(put(src, buf_in.at[slot, :, span], 2 * i))
            if i != 3:
                src = ref.at[pl.ds(width, piece)] if i < 3 else ref
                out.append(put(src, buf_down.at[slot, span, :], 2 * i + 1))
        return out

    def arrive(i):
        out, first = [], 0
        for k, ref in enumerate(blocks[ds[i]]):
            n = ref.shape[0]
            out.append(
                pltpu.make_async_copy(ref, held_x.at[i, pl.ds(first, n)], sem_x.at[i, k])
            )
            first += n
        return out

    for i in range(len(ds)):
        for c in arrive(i):
            c.start()
    for c in copies(0):
        c.start()
    before = lax.broadcasted_iota(jnp.int32, (patches, patches), 0)
    after = lax.broadcasted_iota(jnp.int32, (patches, patches), 1)
    upper = (before < after).astype(jnp.bfloat16)
    slot_of = lax.broadcasted_iota(jnp.int32, (CAP, patches), 0).astype(jnp.float32)
    held = [me ^ j for j in range(4)]
    lane_expert = lax.broadcasted_iota(jnp.int32, (wr_ref.shape[0], patches), 0)
    for i, d in enumerate(ds):
        for c in arrive(i):
            c.wait()
        x = held_x[i, :patches]
        ids = held_x[i, patches:].astype(jnp.float32).astype(jnp.int32)
        e0, e1 = ids[0:1], ids[1:2]
        logits = lax.dot_general(
            wr_ref[...], x, (((1,), (1,)), ((), ())), preferred_element_type=jnp.float32
        )
        pick = lambda e: jnp.sum(jnp.where(lane_expert == e, logits, 0.0), axis=0, keepdims=True)
        gap = pick(e0) - pick(e1)
        g0, g1 = jax.nn.sigmoid(gap), jax.nn.sigmoid(-gap)
        named = [((e0 == h) | (e1 == h)).astype(jnp.float32) for h in held]
        hot = jnp.concatenate(named + named, axis=0)
        rank = jnp.dot(hot.astype(jnp.bfloat16), upper, preferred_element_type=jnp.float32)
        for k, j in enumerate(plan[d]):
            place = jnp.where(named[j] > 0.5, rank[j : j + 1], -1.0)
            hit = slot_of == place
            gate = jnp.where(e0 == held[j], g0, g1)
            share[i, k * CAP : (k + 1) * CAP, :] = jnp.where(hit, gate, 0.0).astype(jnp.bfloat16)
            one = hit.astype(jnp.float32).astype(jnp.bfloat16)
            u = users[j].index(d)
            rows[todo.index(j), u * CAP : (u + 1) * CAP, :] = jnp.dot(
                one, x, preferred_element_type=jnp.float32
            ).astype(jnp.bfloat16)
    for n, j in enumerate(todo):
        if n + 1 < len(todo):
            for cp in copies(n + 1):
                cp.start()
        for cp in copies(n):
            cp.wait()
        m = len(users[j]) * CAP
        slot = n % 2

        def up(c):
            return jnp.dot(
                rows[n, :m],
                buf_in[slot, :, pl.ds(pl.multiple_of(c * CHUNK, CHUNK), CHUNK)],
                preferred_element_type=jnp.float32,
            )

        def down(c, hidden):
            return jnp.dot(
                jax.nn.gelu(hidden, approximate=True).astype(jnp.bfloat16),
                buf_down[slot, pl.ds(pl.multiple_of(c * CHUNK, CHUNK), CHUNK), :],
                preferred_element_type=jnp.float32,
            )

        raw[0, :m] = up(0)
        acc[:m] = jnp.zeros((m, width), jnp.float32)

        @pl.loop(0, chunks - 1)
        def _chunk(c):
            now = lax.rem(c, 2)
            raw[1 - now, :m] = up(c + 1)
            acc[:m] += down(c, raw[now, :m])

        whole = (acc[:m] + down(chunks - 1, raw[(chunks - 1) % 2, :m])).astype(jnp.bfloat16)
        for u, d in enumerate(users[j]):
            k = plan[d].index(j)
            done[ds.index(d), k * CAP : (k + 1) * CAP, :] = whole[u * CAP : (u + 1) * CAP]
    for i, d in enumerate(ds):
        n = len(plan[d]) * CAP
        total = lax.dot_general(
            share[i, :n], done[i, :n], (((0,), (0,)), ((), ())), preferred_element_type=jnp.float32
        )
        for h, out in enumerate(outs[d]):
            out[...] = total[h * out.shape[0] : (h + 1) * out.shape[0]].astype(out.dtype)


def experts(plan, who, router, blocks, weights):
    ds = list(plan)
    width, ff = weights[0][0].shape
    half = (sum(a.shape[0] for a in blocks[ds[0]]) - 16) // 2
    most = max(len(v) for v in plan.values())
    users = [sum(j in v for v in plan.values()) for j in range(4)]
    needed = [w for j in range(4) if users[j] for w in weights[j]]
    given = [a for d in ds for a in blocks[d]]
    vm = pl.BlockSpec(memory_space=pltpu.VMEM)
    hbm = pl.BlockSpec(memory_space=pl.ANY)
    bf = jnp.bfloat16
    work = sum(users) * CAP * width * ff * 4
    got = pl.pallas_call(
        functools.partial(experts_kernel, plan),
        in_specs=[pl.BlockSpec(memory_space=pltpu.SMEM), vm] + [hbm] * (len(given) + len(needed)),
        out_specs=[vm] * (2 * len(ds)),
        out_shape=[jax.ShapeDtypeStruct((half, width), bf)] * (2 * len(ds)),
        scratch_shapes=[
            pltpu.VMEM((sum(u > 0 for u in users), max(users) * CAP, width), bf),
            pltpu.VMEM((len(ds), most * CAP, 2 * half), bf),
            pltpu.VMEM((len(ds), most * CAP, width), bf),
            pltpu.VMEM((max(users) * CAP, width), jnp.float32),
            pltpu.VMEM((2, max(users) * CAP, CHUNK), jnp.float32),
            pltpu.VMEM((2, width, ff), bf),
            pltpu.VMEM((2, ff, width), bf),
            pltpu.VMEM((len(ds), 2 * half + 16, width), bf),
            pltpu.SemaphoreType.DMA((2, 12)),
            pltpu.SemaphoreType.DMA((len(ds), 2)),
        ],
        compiler_params=pltpu.CompilerParams(vmem_limit_bytes=60 << 20),
        cost_estimate=pl.CostEstimate(
            flops=2 * work, bytes_accessed=12_000_000, transcendentals=sum(users) * CAP * ff
        ),
    )(who, router, *given, *needed)
    return {d: tuple(got[2 * i : 2 * i + 2]) for i, d in enumerate(ds)}


def around(step):
    count = lax.axis_size("z")
    return [(i, (i + step) % count) for i in range(count)]


def add(*arrays):
    return sum(a.astype(jnp.float32) for a in arrays).astype(jnp.bfloat16)


def after(x, *others):
    return lax.optimization_barrier((x, *others))[0]


def expert_layer(x, who, router, weights, pieces):
    ahead, back = around(1), around(-1)
    send = lambda a, way: lax.ppermute(a, "z", way)
    near, far, every = (0, 1), (2, 3), (0, 1, 2, 3)
    half = (x.shape[0] - 16) // 2
    width = x.shape[1]
    blocks, so_far = {0: (x,)}, {}
    weights = list(weights)
    run = lambda plan: experts(plan, who, router, blocks, weights)

    def keep(results, *arrays):
        flat = [a for d in results for a in results[d]]
        out = lax.optimization_barrier((*arrays, *flat))
        held = out[len(arrays) :]
        so_far.update({d: held[2 * i : 2 * i + 2] for i, d in enumerate(results)})
        return out[: len(arrays)]

    part, one, two, part_o = pieces
    f, b = send(x, ahead), send(x, back)
    one, two = keep(run({0: near}), one, two)
    up, down = both_ways(one[:width], two[width:])
    one_o, two_o = swap(one), swap(two)
    f, b = keep({}, f, b)
    blocks[1], blocks[7] = (f,), (b,)
    f, b = send(f, ahead), send(b, back)
    f, b, up, down, one_o, two_o = keep(run({1: near, 7: near}), f, b, up, down, one_o, two_o)
    up_o, down_o = swap(up), swap(down)
    blocks[2], blocks[6] = (f,), (b,)
    f, b = send(f, ahead), send(b, back)
    f, b, up_o, down_o = keep(run({2: near, 6: near}), f, b, up_o, down_o)
    blocks[3], blocks[5] = (f,), (b,)
    weights += [(part, one, two, up, down), (part_o, one_o, two_o, up_o, down_o)]
    f, b = send(f[:half], ahead), send(b[half:], back)
    parts = run({2: far, 6: far, 1: far, 7: far, 0: far})
    last = [a for d in parts for a in parts[d]]
    f, b = lax.optimization_barrier((f, b, *last))[:2]
    blocks[4] = (f, b)
    parts.update(run({4: every, 3: every, 5: every}))
    f0, b1 = send(parts[4][0], back), send(parts[4][1], ahead)
    f1, b0 = send(parts[3][1], back), send(parts[5][0], ahead)
    f0, b1 = send(add(f0, parts[3][0]), back), send(add(b1, parts[5][1]), ahead)
    for i in (2, 1):
        f1 = send(add(f1, parts[i][1], so_far[i][1]), back)
        b0 = send(add(b0, parts[8 - i][0], so_far[8 - i][0]), ahead)
        f0 = send(add(f0, parts[i][0], so_far[i][0]), back)
        b1 = send(add(b1, parts[8 - i][1], so_far[8 - i][1]), ahead)
    return [(parts[0][0], so_far[0][0], f0, b0), (parts[0][1], so_far[0][1], f1, b1)]


def own_quarter(w_in, w_down):
    piece = w_in.shape[1] // lax.axis_size("y")
    first = lax.axis_index("y") * piece
    return jnp.concatenate(
        [
            lax.dynamic_slice_in_dim(w_in, first, piece, 1),
            lax.dynamic_slice_in_dim(w_down, first, piece, 0),
        ],
        axis=0,
    )


def across_x(quarter):
    return lax.ppermute(quarter, ("xh", "xl"), [(0, 3), (3, 0), (1, 2), (2, 1)])


def both_ways(a, b):
    count = lax.axis_size("y")
    ahead = [(i, (i + 1) % count) for i in range(count)]
    back = [(i, (i - 1) % count) for i in range(count)]
    return lax.ppermute(a, "y", ahead), lax.ppermute(b, "y", back)


def swap(a):
    return lax.ppermute(a, "core", [(0, 1), (1, 0)])


def per_device(
    tokens, die_mask, expert_ids, gain_attn, w_qkv, w_out, gain_moe, w_router, w_in, w_down
):
    ht, wt, width = tokens.shape
    patches = ht * wt
    w_in, w_down = w_in[0], w_down[0]
    quarter = own_quarter(w_in, w_down)
    top, bot = halo_rows(after(tokens, quarter), die_mask)
    part = across_x(quarter)
    to_right, to_left = halo_edges(tokens, die_mask, top, bot)
    left = lax.ppermute(to_right, COL, ahead_of(COL))
    right = lax.ppermute(to_left, COL, behind(COL))
    other = swap(after(w_in, top, bot)), swap(after(w_down, top, bot))
    right, part = lax.optimization_barrier((right, part))
    one, two = both_ways(part, part)
    part_o = swap(part)
    ids = expert_ids.reshape(patches, 2).T
    marks = jnp.broadcast_to(die_mask.astype(jnp.bfloat16)[..., None], (ht, wt, LANES))
    resid, x = attention(
        tokens, marks, top, bot, left, right, gain_attn, w_qkv, w_out, gain_moe, ids
    )
    who = lax.axis_index(ROW).reshape(1).astype(jnp.int32)
    x, one, two, part_o, *other = lax.optimization_barrier((x, one, two, part_o, *other))
    weights = ((w_in, w_down), tuple(other))
    wide = lambda a: a.astype(jnp.float32)
    moe = expert_layer(x, who, w_router.T, weights, (part, one, two, part_o))
    moe = jnp.concatenate([sum(wide(a) for a in half) for half in moe], axis=0)
    final = (wide(resid) + moe).astype(jnp.bfloat16)
    return final.reshape(ht, wt, width)


def solution(mesh):
    fine = Mesh(mesh.devices.reshape(8, 2, 2, 2, 4), ROW + COL)
    return jax.shard_map(
        per_device,
        mesh=fine,
        in_specs=(
            P(ROW, COL, None),
            P(ROW, COL),
            P(ROW, COL, None, None),
            P(),
            P(),
            P(),
            P(),
            P(),
            P(ROW, None, None),
            P(ROW, None, None),
        ),
        out_specs=P(ROW, COL, None),
        check_vma=False,
    )
```

```python
import functools

import jax
import jax.numpy as jnp
import numpy as np
from jax import lax
from jax.experimental import pallas as pl
from jax.experimental.pallas import tpu as pltpu
from jax.sharding import Mesh, PartitionSpec as P

HEADS = 16
RADIUS = 6
CAP = 96
SIDE = 8
QROWS = 4
LANES = 128
BIG = 1e30

ROW = ("z", "xh", "core")
COL = ("xl", "y")


def norm(wide, gain):
    power = jnp.mean(wide * wide, axis=-1, keepdims=True)
    return (wide * lax.rsqrt(power + 1e-06) * gain).astype(jnp.bfloat16)


def window_bias(marks, wt):
    keyw = wt + 2 * SIDE
    shape = (QROWS + 2 * RADIUS, keyw, QROWS * wt)
    kr, kc, q = (lax.broadcasted_iota(jnp.int32, shape, i) for i in range(3))
    col = jnp.where(kc < wt + SIDE, kc, kc - keyw)
    rise = kr - q // wt - RADIUS
    reach = col - q % wt
    inside = (jnp.abs(rise) <= RADIUS) & (jnp.abs(reach) <= RADIUS)
    centre = (rise == 0) & (reach == 0)
    open_ = (inside & (marks.reshape(shape) > 0.5)) | centre
    return jnp.where(open_, 0.0, -BIG).reshape(shape[0] * shape[1], shape[2])


def attention_kernel(
    gain_ref, gain2_ref, ids_ref, *refs,
):
    sources, (resid_ref, moe_ref), refs = refs[:8], refs[8:10], refs[10:]
    xn, marks, keys, vals, kaug, vaug, qaug, *local, sem = refs
    tok_ref, mask_ref, top_ref, bot_ref, left_ref, right_ref, wqkv_ref, wout_ref = local
    ht, wt, width = tok_ref.shape
    keyw = wt + 2 * SIDE
    krows = QROWS + 2 * RADIUS
    slab = krows * keyw
    nq = QROWS * wt
    gain = gain_ref[...]
    step = pl.program_id(0)

    @pl.when(step == 0)
    def _prepare():
        fetch = [
            pltpu.make_async_copy(src, dst, sem.at[i])
            for i, (src, dst) in enumerate(zip(sources, local))
        ]
        for cp in fetch:
            cp.start()

        def rows(first, count, body_of):
            @pl.loop(0, count)
            def _row(i):
                body, mark = body_of(i)
                at = pl.multiple_of((first + i) * keyw, 16)
                xn[pl.ds(at, wt), :] = norm(body.astype(jnp.float32), gain)
                marks[pl.ds(at, wt), :] = mark.astype(jnp.float32)
                edge = jnp.concatenate(
                    [
                        right_ref[first + i].astype(jnp.float32),
                        left_ref[first + i].astype(jnp.float32),
                    ],
                    axis=0,
                )
                beside = pl.ds(pl.multiple_of(at + wt, 16), 2 * SIDE)
                xn[beside, :] = norm(edge[:, :width], gain)
                marks[beside, :] = edge[:, width:]

        for cp in fetch[:6]:
            cp.wait()
        rows(0, RADIUS, lambda i: (top_ref[i, :, :width], top_ref[i, :, width:]))
        rows(RADIUS, ht, lambda i: (tok_ref[i], mask_ref[i]))
        rows(ht + RADIUS, RADIUS, lambda i: (bot_ref[i, :, :width], bot_ref[i, :, width:]))
        for cp in fetch[6:]:
            cp.wait()
        every = xn[...]
        keys[...] = jnp.dot(
            every, wqkv_ref[:, width : 2 * width], preferred_element_type=jnp.float32
        ).astype(jnp.bfloat16)
        vals[...] = jnp.dot(
            every, wqkv_ref[:, 2 * width :], preferred_element_type=jnp.float32
        ).astype(jnp.bfloat16)
        for p in range(2):
            vaug[p, :, LANES:] = jnp.ones((slab, LANES), jnp.bfloat16)
        spot = lax.broadcasted_iota(jnp.int32, (nq, nq), 0)
        lane = lax.broadcasted_iota(jnp.int32, (nq, nq), 1)
        unit = (spot == lane).astype(jnp.bfloat16)
        for i in range(4):
            for p in range(2):
                qaug[p, i * nq : (i + 1) * nq, LANES:] = unit
        named = ids_ref[...].astype(jnp.float32)
        spare = jnp.zeros((16 - named.shape[0], named.shape[1]), jnp.float32)
        moe_ref[ht * wt :, :] = jnp.concatenate([named, spare], axis=0).astype(jnp.bfloat16)

    base = pl.multiple_of(step * (QROWS * keyw), QROWS * keyw)
    own = [
        xn[pl.ds(pl.multiple_of(base + (RADIUS + i) * keyw, 16), wt), :] for i in range(QROWS)
    ]
    query = jnp.dot(
        jnp.concatenate(own, axis=0), wqkv_ref[:, :width], preferred_element_type=jnp.float32
    )
    hdim = width // HEADS
    query = (query * hdim ** (-0.5)).astype(jnp.bfloat16)
    bias = window_bias(marks[pl.ds(base, slab), :], wt).astype(jnp.bfloat16)
    for p in range(2):
        kaug[p, :, LANES:] = bias
    per = LANES // hdim
    head_of = lax.broadcasted_iota(jnp.int32, (nq, LANES), 1) // hdim
    pieces = []
    for g in range(width // LANES):
        cols = slice(g * LANES, (g + 1) * LANES)
        qg = query[:, cols]
        for i in range(per):
            qaug[g % 2, i * nq : (i + 1) * nq, :LANES] = jnp.where(head_of == i, qg, 0).astype(
                jnp.bfloat16
            )
        kaug[g % 2, :, :LANES] = keys[pl.ds(base, slab), cols]
        vaug[g % 2, :, :LANES] = vals[pl.ds(base, slab), cols]
        scores = lax.dot_general(
            qaug[g % 2], kaug[g % 2], (((1,), (1,)), ((), ())), preferred_element_type=jnp.float32
        )
        highest = jnp.max(scores, axis=-1, keepdims=True)
        weights = jnp.exp(scores - highest).astype(jnp.bfloat16)
        mixed = jnp.dot(weights, vaug[g % 2], preferred_element_type=jnp.float32)
        share = mixed[:, :LANES] / mixed[:, LANES:]
        both = share[:nq]
        for i in range(1, per):
            both = jnp.where(head_of == i, share[i * nq : (i + 1) * nq], both)
        pieces.append(both.astype(jnp.bfloat16))
    attended = jnp.concatenate(pieces, axis=1)
    mixed = jnp.dot(attended, wout_ref[...], preferred_element_type=jnp.float32)
    mine = tok_ref[pl.ds(step * QROWS, QROWS)].reshape(nq, width)
    resid = (mine.astype(jnp.float32) + mixed).astype(jnp.bfloat16)
    resid_ref[...] = resid
    moe_ref[pl.ds(pl.multiple_of(step * nq, nq), nq), :] = norm(
        resid.astype(jnp.float32), gain2_ref[...]
    )


def attention(tokens, marks, top, bot, left, right, gain, wqkv, wout, gain2, ids):
    ht, wt, width = tokens.shape
    slab, nq = (QROWS + 2 * RADIUS) * (wt + 2 * SIDE), QROWS * wt
    total = (ht + 2 * RADIUS) * (wt + 2 * SIDE)
    whole = lambda a: pl.BlockSpec(a.shape, functools.partial(lambda n, i: (0,) * n, a.ndim))
    args = (gain.reshape(1, width), gain2.reshape(1, width), ids)
    large = (tokens, marks, top, bot, left, right, wqkv, wout)
    bf = jnp.bfloat16
    return pl.pallas_call(
        attention_kernel,
        grid=(ht // QROWS,),
        in_specs=[whole(a) for a in args] + [pl.BlockSpec(memory_space=pl.ANY)] * len(large),
        out_specs=[
            pl.BlockSpec((nq, width), lambda i: (i, 0)),
            pl.BlockSpec((ht * wt + 16, width), lambda i: (0, 0)),
        ],
        out_shape=[
            jax.ShapeDtypeStruct((ht * wt, width), bf),
            jax.ShapeDtypeStruct((ht * wt + 16, width), bf),
        ],
        scratch_shapes=[
            pltpu.VMEM((total, width), bf),
            pltpu.VMEM((total, LANES), jnp.float32),
            pltpu.VMEM((total, width), bf),
            pltpu.VMEM((total, width), bf),
            pltpu.VMEM((2, slab, 2 * LANES), bf),
            pltpu.VMEM((2, slab, 2 * LANES), bf),
            pltpu.VMEM((2, 4 * nq, 2 * LANES), bf),
            *[pltpu.VMEM(a.shape, bf) for a in large],
            pltpu.SemaphoreType.DMA((len(large),)),
        ],
        compiler_params=pltpu.CompilerParams(vmem_limit_bytes=60 << 20),
        cost_estimate=pl.CostEstimate(
            flops=10_000_000_000, bytes_accessed=6_000_000, transcendentals=6_000_000
        ),
    )(*args, *large)


def with_marks(tokens, mask):
    marks = jnp.broadcast_to(mask.astype(jnp.bfloat16)[..., None], (*mask.shape, LANES))
    return jnp.concatenate([tokens, marks], axis=-1)


def ahead_of(axis):
    return [(i, i + 1) for i in range(lax.axis_size(axis) - 1)]


def behind(axis):
    return [(i + 1, i) for i in range(lax.axis_size(axis) - 1)]


def halo_rows(tokens, mask):
    ht = tokens.shape[0]
    low, high = slice(ht - RADIUS, ht), slice(0, RADIUS)
    top = lax.ppermute(with_marks(tokens[low], mask[low]), ROW, ahead_of(ROW))
    bot = lax.ppermute(with_marks(tokens[high], mask[high]), ROW, behind(ROW))
    return top, bot


def halo_edges(tokens, mask, top, bot):
    def edge(cols):
        mine = with_marks(tokens[:, cols], mask[:, cols])
        return jnp.concatenate([top[:, cols], mine, bot[:, cols]], axis=0)

    wt = tokens.shape[1]
    return edge(slice(wt - SIDE, wt)), edge(slice(0, SIDE))


CHUNK = 1024


def experts_kernel(plan, who_ref, wr_ref, *refs):
    ds = list(plan)
    blocks, at = {}, 0
    for d in ds:
        blocks[d] = refs[at : at + (2 if d == 4 else 1)]
        at += len(blocks[d])
    users = {j: [d for d in ds if j in plan[d]] for j in range(4)}
    todo = [j for j in range(4) if users[j]]
    held_w = {}
    for j in todo:
        held_w[j] = refs[at : at + (2 if j < 2 else 5)]
        at += len(held_w[j])
    outs = {d: refs[at + 2 * i : at + 2 * i + 2] for i, d in enumerate(ds)}
    rows, share, done, acc, raw, buf_in, buf_down, held_x, sem, sem_x = refs[at + 2 * len(ds) :]
    width = rows.shape[-1]
    patches = share.shape[-1]
    ff = buf_in.shape[-1]
    chunks = ff // CHUNK
    piece = ff // 4
    me = who_ref[0]

    def copies(n):
        j, slot = todo[n], n % 2
        put = lambda src, dst, i: pltpu.make_async_copy(src, dst, sem.at[slot, i])
        if j < 2:
            return (
                put(held_w[j][0], buf_in.at[slot], 0),
                put(held_w[j][1], buf_down.at[slot], 1),
            )
        out = []
        for i, ref in enumerate(held_w[j]):
            span = pl.ds(min(i, 3) * piece, piece)
            if i < 4:
                src = ref.at[pl.ds(0, width)]
                out.append(put(src, buf_in.at[slot, :, span], 2 * i))
            if i != 3:
                src = ref.at[pl.ds(width, piece)] if i < 3 else ref
                out.append(put(src, buf_down.at[slot, span, :], 2 * i + 1))
        return out

    def arrive(i):
        out, first = [], 0
        for k, ref in enumerate(blocks[ds[i]]):
            n = ref.shape[0]
            out.append(
                pltpu.make_async_copy(ref, held_x.at[i, pl.ds(first, n)], sem_x.at[i, k])
            )
            first += n
        return out

    for i in range(len(ds)):
        for c in arrive(i):
            c.start()
    for c in copies(0):
        c.start()
    before = lax.broadcasted_iota(jnp.int32, (patches, patches), 0)
    after = lax.broadcasted_iota(jnp.int32, (patches, patches), 1)
    upper = (before < after).astype(jnp.bfloat16)
    slot_of = lax.broadcasted_iota(jnp.int32, (CAP, patches), 0).astype(jnp.float32)
    held = [me ^ j for j in range(4)]
    lane_expert = lax.broadcasted_iota(jnp.int32, (wr_ref.shape[0], patches), 0)
    for i, d in enumerate(ds):
        for c in arrive(i):
            c.wait()
        x = held_x[i, :patches]
        ids = held_x[i, patches:].astype(jnp.float32).astype(jnp.int32)
        e0, e1 = ids[0:1], ids[1:2]
        logits = lax.dot_general(
            wr_ref[...], x, (((1,), (1,)), ((), ())), preferred_element_type=jnp.float32
        )
        pick = lambda e: jnp.sum(jnp.where(lane_expert == e, logits, 0.0), axis=0, keepdims=True)
        gap = pick(e0) - pick(e1)
        g0, g1 = jax.nn.sigmoid(gap), jax.nn.sigmoid(-gap)
        named = [((e0 == h) | (e1 == h)).astype(jnp.float32) for h in held]
        hot = jnp.concatenate(named + named, axis=0)
        rank = jnp.dot(hot.astype(jnp.bfloat16), upper, preferred_element_type=jnp.float32)
        for k, j in enumerate(plan[d]):
            place = jnp.where(named[j] > 0.5, rank[j : j + 1], -1.0)
            hit = slot_of == place
            gate = jnp.where(e0 == held[j], g0, g1)
            share[i, k * CAP : (k + 1) * CAP, :] = jnp.where(hit, gate, 0.0).astype(jnp.bfloat16)
            one = hit.astype(jnp.float32).astype(jnp.bfloat16)
            u = users[j].index(d)
            rows[todo.index(j), u * CAP : (u + 1) * CAP, :] = jnp.dot(
                one, x, preferred_element_type=jnp.float32
            ).astype(jnp.bfloat16)
    for n, j in enumerate(todo):
        if n + 1 < len(todo):
            for cp in copies(n + 1):
                cp.start()
        for cp in copies(n):
            cp.wait()
        m = len(users[j]) * CAP
        slot = n % 2

        def up(c):
            return jnp.dot(
                rows[n, :m],
                buf_in[slot, :, pl.ds(pl.multiple_of(c * CHUNK, CHUNK), CHUNK)],
                preferred_element_type=jnp.float32,
            )

        def down(c, hidden):
            return jnp.dot(
                jax.nn.gelu(hidden, approximate=True).astype(jnp.bfloat16),
                buf_down[slot, pl.ds(pl.multiple_of(c * CHUNK, CHUNK), CHUNK), :],
                preferred_element_type=jnp.float32,
            )

        raw[0, :m] = up(0)
        acc[:m] = jnp.zeros((m, width), jnp.float32)

        @pl.loop(0, chunks - 1)
        def _chunk(c):
            now = lax.rem(c, 2)
            raw[1 - now, :m] = up(c + 1)
            acc[:m] += down(c, raw[now, :m])

        whole = (acc[:m] + down(chunks - 1, raw[(chunks - 1) % 2, :m])).astype(jnp.bfloat16)
        for u, d in enumerate(users[j]):
            k = plan[d].index(j)
            done[ds.index(d), k * CAP : (k + 1) * CAP, :] = whole[u * CAP : (u + 1) * CAP]
    for i, d in enumerate(ds):
        n = len(plan[d]) * CAP
        total = lax.dot_general(
            share[i, :n], done[i, :n], (((0,), (0,)), ((), ())), preferred_element_type=jnp.float32
        )
        for h, out in enumerate(outs[d]):
            out[...] = total[h * out.shape[0] : (h + 1) * out.shape[0]].astype(out.dtype)


def experts(plan, who, router, blocks, weights):
    ds = list(plan)
    width, ff = weights[0][0].shape
    half = (sum(a.shape[0] for a in blocks[ds[0]]) - 16) // 2
    most = max(len(v) for v in plan.values())
    users = [sum(j in v for v in plan.values()) for j in range(4)]
    needed = [w for j in range(4) if users[j] for w in weights[j]]
    given = [a for d in ds for a in blocks[d]]
    vm = pl.BlockSpec(memory_space=pltpu.VMEM)
    hbm = pl.BlockSpec(memory_space=pl.ANY)
    bf = jnp.bfloat16
    work = sum(users) * CAP * width * ff * 4
    got = pl.pallas_call(
        functools.partial(experts_kernel, plan),
        in_specs=[pl.BlockSpec(memory_space=pltpu.SMEM), vm] + [hbm] * (len(given) + len(needed)),
        out_specs=[vm] * (2 * len(ds)),
        out_shape=[jax.ShapeDtypeStruct((half, width), bf)] * (2 * len(ds)),
        scratch_shapes=[
            pltpu.VMEM((sum(u > 0 for u in users), max(users) * CAP, width), bf),
            pltpu.VMEM((len(ds), most * CAP, 2 * half), bf),
            pltpu.VMEM((len(ds), most * CAP, width), bf),
            pltpu.VMEM((max(users) * CAP, width), jnp.float32),
            pltpu.VMEM((2, max(users) * CAP, CHUNK), jnp.float32),
            pltpu.VMEM((2, width, ff), bf),
            pltpu.VMEM((2, ff, width), bf),
            pltpu.VMEM((len(ds), 2 * half + 16, width), bf),
            pltpu.SemaphoreType.DMA((2, 12)),
            pltpu.SemaphoreType.DMA((len(ds), 2)),
        ],
        compiler_params=pltpu.CompilerParams(vmem_limit_bytes=60 << 20),
        cost_estimate=pl.CostEstimate(
            flops=2 * work, bytes_accessed=12_000_000, transcendentals=sum(users) * CAP * ff
        ),
    )(who, router, *given, *needed)
    return {d: tuple(got[2 * i : 2 * i + 2]) for i, d in enumerate(ds)}


def around(step):
    count = lax.axis_size("z")
    return [(i, (i + step) % count) for i in range(count)]


def add(*arrays):
    return sum(a.astype(jnp.float32) for a in arrays).astype(jnp.bfloat16)


def after(x, *others):
    return lax.optimization_barrier((x, *others))[0]


def expert_layer(x, who, router, weights, part):
    ahead, back = around(1), around(-1)
    send = lambda a, way: lax.ppermute(a, "z", way)
    near, far, every = (0, 1), (2, 3), (0, 1, 2, 3)
    half = (x.shape[0] - 16) // 2
    width = x.shape[1]
    blocks, so_far = {0: (x,)}, {}
    weights = list(weights)
    run = lambda plan: experts(plan, who, router, blocks, weights)

    def keep(results, *arrays):
        flat = [a for d in results for a in results[d]]
        out = lax.optimization_barrier((*arrays, *flat))
        held = out[len(arrays) :]
        so_far.update({d: held[2 * i : 2 * i + 2] for i, d in enumerate(results)})
        return out[: len(arrays)]

    one, two = both_ways(part, part)
    part_o = swap(part)
    f, b = send(x, ahead), send(x, back)
    f, b = keep({}, f, b)
    blocks[1], blocks[7] = (f,), (b,)
    f, b = send(f, ahead), send(b, back)
    f, b, one, two = keep(run({0: near, 1: near, 7: near}), f, b, one, two)
    up, down = both_ways(one[:width], two[width:])
    one_o, two_o = swap(one), swap(two)
    blocks[2], blocks[6] = (f,), (b,)
    f, b = send(f, ahead), send(b, back)
    f, b, up, down, part_o, one_o, two_o = keep(
        run({2: near, 6: near}), f, b, up, down, part_o, one_o, two_o
    )
    up_o, down_o = swap(up), swap(down)
    blocks[3], blocks[5] = (f,), (b,)
    weights += [(part, one, two, up, down), (part_o, one_o, two_o, up_o, down_o)]
    f, b = lax.optimization_barrier((f[:half], b[half:]))
    blocks[4] = (send(f, ahead), send(b, back))
    parts = run({**dict.fromkeys((4, 3, 5), every), **dict.fromkeys((2, 6, 1, 7, 0), far)})
    f0, b1 = send(parts[4][0], back), send(parts[4][1], ahead)
    f1, b0 = send(parts[3][1], back), send(parts[5][0], ahead)
    f0, b1 = send(add(f0, parts[3][0]), back), send(add(b1, parts[5][1]), ahead)
    for i in (2, 1):
        f1 = send(add(f1, parts[i][1], so_far[i][1]), back)
        b0 = send(add(b0, parts[8 - i][0], so_far[8 - i][0]), ahead)
        f0 = send(add(f0, parts[i][0], so_far[i][0]), back)
        b1 = send(add(b1, parts[8 - i][1], so_far[8 - i][1]), ahead)
    return [(parts[0][0], so_far[0][0], f0, b0), (parts[0][1], so_far[0][1], f1, b1)]


def own_quarter(w_in, w_down):
    piece = w_in.shape[1] // lax.axis_size("y")
    first = lax.axis_index("y") * piece
    return jnp.concatenate(
        [
            lax.dynamic_slice_in_dim(w_in, first, piece, 1),
            lax.dynamic_slice_in_dim(w_down, first, piece, 0),
        ],
        axis=0,
    )


def across_x(quarter):
    return lax.ppermute(quarter, ("xh", "xl"), [(0, 3), (3, 0), (1, 2), (2, 1)])


def both_ways(a, b):
    count = lax.axis_size("y")
    ahead = [(i, (i + 1) % count) for i in range(count)]
    back = [(i, (i - 1) % count) for i in range(count)]
    return lax.ppermute(a, "y", ahead), lax.ppermute(b, "y", back)


def swap(a):
    return lax.ppermute(a, "core", [(0, 1), (1, 0)])


def per_device(
    tokens, die_mask, expert_ids, gain_attn, w_qkv, w_out, gain_moe, w_router, w_in, w_down
):
    ht, wt, width = tokens.shape
    patches = ht * wt
    w_in, w_down = w_in[0], w_down[0]
    top, bot = halo_rows(tokens, die_mask)
    to_right, to_left = halo_edges(tokens, die_mask, top, bot)
    left = lax.ppermute(to_right, COL, ahead_of(COL))
    right = lax.ppermute(to_left, COL, behind(COL))
    late_in, late_down = after(w_in, top, bot), after(w_down, top, bot)
    part = across_x(own_quarter(late_in, late_down))
    other = swap(late_in), swap(late_down)
    ids = expert_ids.reshape(patches, 2).T
    marks = jnp.broadcast_to(die_mask.astype(jnp.bfloat16)[..., None], (ht, wt, LANES))
    resid, x = attention(
        tokens, marks, top, bot, left, right, gain_attn, w_qkv, w_out, gain_moe, ids
    )
    who = lax.axis_index(ROW).reshape(1).astype(jnp.int32)
    x, part, *other = lax.optimization_barrier((x, part, *other))
    weights = ((w_in, w_down), tuple(other))
    wide = lambda a: a.astype(jnp.float32)
    moe = expert_layer(x, who, w_router.T, weights, part)
    moe = jnp.concatenate([sum(wide(a) for a in half) for half in moe], axis=0)
    final = (wide(resid) + moe).astype(jnp.bfloat16)
    return final.reshape(ht, wt, width)


def solution(mesh):
    fine = Mesh(mesh.devices.reshape(8, 2, 2, 2, 4), ROW + COL)
    return jax.shard_map(
        per_device,
        mesh=fine,
        in_specs=(
            P(ROW, COL, None),
            P(ROW, COL),
            P(ROW, COL, None, None),
            P(),
            P(),
            P(),
            P(),
            P(),
            P(ROW, None, None),
            P(ROW, None, None),
        ),
        out_specs=P(ROW, COL, None),
        check_vma=False,
    )
```

```python
import functools

import jax
import jax.numpy as jnp
import numpy as np
from jax import lax
from jax.experimental import pallas as pl
from jax.experimental.pallas import tpu as pltpu
from jax.sharding import Mesh, PartitionSpec as P

HEADS = 16
RADIUS = 6
CAP = 96
SIDE = 8
QROWS = 4
LANES = 128
BIG = 1e30

ROW = ("z", "xh", "core")
COL = ("xl", "y")


def norm(wide, gain):
    power = jnp.mean(wide * wide, axis=-1, keepdims=True)
    return (wide * lax.rsqrt(power + 1e-06) * gain).astype(jnp.bfloat16)


def window_bias(marks, wt):
    keyw = wt + 2 * SIDE
    shape = (QROWS + 2 * RADIUS, keyw, QROWS * wt)
    kr, kc, q = (lax.broadcasted_iota(jnp.int32, shape, i) for i in range(3))
    col = jnp.where(kc < wt + SIDE, kc, kc - keyw)
    rise = kr - q // wt - RADIUS
    reach = col - q % wt
    inside = (jnp.abs(rise) <= RADIUS) & (jnp.abs(reach) <= RADIUS)
    centre = (rise == 0) & (reach == 0)
    open_ = (inside & (marks.reshape(shape) > 0.5)) | centre
    return jnp.where(open_, 0.0, -BIG).reshape(shape[0] * shape[1], shape[2])


def attention_kernel(
    gain_ref, gain2_ref, ids_ref, *refs,
):
    sources, (resid_ref, moe_ref), refs = refs[:8], refs[8:10], refs[10:]
    xn, marks, keys, vals, kaug, vaug, qaug, *local, sem = refs
    tok_ref, mask_ref, top_ref, bot_ref, left_ref, right_ref, wqkv_ref, wout_ref = local
    ht, wt, width = tok_ref.shape
    keyw = wt + 2 * SIDE
    krows = QROWS + 2 * RADIUS
    slab = krows * keyw
    nq = QROWS * wt
    gain = gain_ref[...]
    step = pl.program_id(0)

    @pl.when(step == 0)
    def _prepare():
        fetch = [
            pltpu.make_async_copy(src, dst, sem.at[i])
            for i, (src, dst) in enumerate(zip(sources, local))
        ]
        for cp in fetch:
            cp.start()

        def rows(first, count, body_of):
            @pl.loop(0, count)
            def _row(i):
                body, mark = body_of(i)
                at = pl.multiple_of((first + i) * keyw, 16)
                xn[pl.ds(at, wt), :] = norm(body.astype(jnp.float32), gain)
                marks[pl.ds(at, wt), :] = mark.astype(jnp.float32)
                edge = jnp.concatenate(
                    [
                        right_ref[first + i].astype(jnp.float32),
                        left_ref[first + i].astype(jnp.float32),
                    ],
                    axis=0,
                )
                beside = pl.ds(pl.multiple_of(at + wt, 16), 2 * SIDE)
                xn[beside, :] = norm(edge[:, :width], gain)
                marks[beside, :] = edge[:, width:]

        for cp in fetch[:6]:
            cp.wait()
        rows(0, RADIUS, lambda i: (top_ref[i, :, :width], top_ref[i, :, width:]))
        rows(RADIUS, ht, lambda i: (tok_ref[i], mask_ref[i]))
        rows(ht + RADIUS, RADIUS, lambda i: (bot_ref[i, :, :width], bot_ref[i, :, width:]))
        for cp in fetch[6:]:
            cp.wait()
        every = xn[...]
        keys[...] = jnp.dot(
            every, wqkv_ref[:, width : 2 * width], preferred_element_type=jnp.float32
        ).astype(jnp.bfloat16)
        vals[...] = jnp.dot(
            every, wqkv_ref[:, 2 * width :], preferred_element_type=jnp.float32
        ).astype(jnp.bfloat16)
        for p in range(2):
            vaug[p, :, LANES:] = jnp.ones((slab, LANES), jnp.bfloat16)
        spot = lax.broadcasted_iota(jnp.int32, (nq, nq), 0)
        lane = lax.broadcasted_iota(jnp.int32, (nq, nq), 1)
        unit = (spot == lane).astype(jnp.bfloat16)
        for i in range(4):
            for p in range(2):
                qaug[p, i * nq : (i + 1) * nq, LANES:] = unit
        named = ids_ref[...].astype(jnp.float32)
        spare = jnp.zeros((16 - named.shape[0], named.shape[1]), jnp.float32)
        moe_ref[ht * wt :, :] = jnp.concatenate([named, spare], axis=0).astype(jnp.bfloat16)

    base = pl.multiple_of(step * (QROWS * keyw), QROWS * keyw)
    own = [
        xn[pl.ds(pl.multiple_of(base + (RADIUS + i) * keyw, 16), wt), :] for i in range(QROWS)
    ]
    query = jnp.dot(
        jnp.concatenate(own, axis=0), wqkv_ref[:, :width], preferred_element_type=jnp.float32
    )
    hdim = width // HEADS
    query = (query * hdim ** (-0.5)).astype(jnp.bfloat16)
    bias = window_bias(marks[pl.ds(base, slab), :], wt).astype(jnp.bfloat16)
    for p in range(2):
        kaug[p, :, LANES:] = bias
    per = LANES // hdim
    head_of = lax.broadcasted_iota(jnp.int32, (nq, LANES), 1) // hdim
    pieces = []
    for g in range(width // LANES):
        cols = slice(g * LANES, (g + 1) * LANES)
        qg = query[:, cols]
        for i in range(per):
            qaug[g % 2, i * nq : (i + 1) * nq, :LANES] = jnp.where(head_of == i, qg, 0).astype(
                jnp.bfloat16
            )
        kaug[g % 2, :, :LANES] = keys[pl.ds(base, slab), cols]
        vaug[g % 2, :, :LANES] = vals[pl.ds(base, slab), cols]
        scores = lax.dot_general(
            qaug[g % 2], kaug[g % 2], (((1,), (1,)), ((), ())), preferred_element_type=jnp.float32
        )
        highest = jnp.max(scores, axis=-1, keepdims=True)
        weights = jnp.exp(scores - highest).astype(jnp.bfloat16)
        mixed = jnp.dot(weights, vaug[g % 2], preferred_element_type=jnp.float32)
        share = mixed[:, :LANES] / mixed[:, LANES:]
        both = share[:nq]
        for i in range(1, per):
            both = jnp.where(head_of == i, share[i * nq : (i + 1) * nq], both)
        pieces.append(both.astype(jnp.bfloat16))
    attended = jnp.concatenate(pieces, axis=1)
    mixed = jnp.dot(attended, wout_ref[...], preferred_element_type=jnp.float32)
    mine = tok_ref[pl.ds(step * QROWS, QROWS)].reshape(nq, width)
    resid = (mine.astype(jnp.float32) + mixed).astype(jnp.bfloat16)
    resid_ref[...] = resid
    moe_ref[pl.ds(pl.multiple_of(step * nq, nq), nq), :] = norm(
        resid.astype(jnp.float32), gain2_ref[...]
    )


def attention(tokens, marks, top, bot, left, right, gain, wqkv, wout, gain2, ids):
    ht, wt, width = tokens.shape
    slab, nq = (QROWS + 2 * RADIUS) * (wt + 2 * SIDE), QROWS * wt
    total = (ht + 2 * RADIUS) * (wt + 2 * SIDE)
    whole = lambda a: pl.BlockSpec(a.shape, functools.partial(lambda n, i: (0,) * n, a.ndim))
    args = (gain.reshape(1, width), gain2.reshape(1, width), ids)
    large = (tokens, marks, top, bot, left, right, wqkv, wout)
    bf = jnp.bfloat16
    return pl.pallas_call(
        attention_kernel,
        grid=(ht // QROWS,),
        in_specs=[whole(a) for a in args] + [pl.BlockSpec(memory_space=pl.ANY)] * len(large),
        out_specs=[
            pl.BlockSpec((nq, width), lambda i: (i, 0)),
            pl.BlockSpec((ht * wt + 16, width), lambda i: (0, 0)),
        ],
        out_shape=[
            jax.ShapeDtypeStruct((ht * wt, width), bf),
            jax.ShapeDtypeStruct((ht * wt + 16, width), bf),
        ],
        scratch_shapes=[
            pltpu.VMEM((total, width), bf),
            pltpu.VMEM((total, LANES), jnp.float32),
            pltpu.VMEM((total, width), bf),
            pltpu.VMEM((total, width), bf),
            pltpu.VMEM((2, slab, 2 * LANES), bf),
            pltpu.VMEM((2, slab, 2 * LANES), bf),
            pltpu.VMEM((2, 4 * nq, 2 * LANES), bf),
            *[pltpu.VMEM(a.shape, bf) for a in large],
            pltpu.SemaphoreType.DMA((len(large),)),
        ],
        compiler_params=pltpu.CompilerParams(vmem_limit_bytes=60 << 20),
        cost_estimate=pl.CostEstimate(
            flops=10_000_000_000, bytes_accessed=6_000_000, transcendentals=6_000_000
        ),
    )(*args, *large)


def with_marks(tokens, mask):
    marks = jnp.broadcast_to(mask.astype(jnp.bfloat16)[..., None], (*mask.shape, LANES))
    return jnp.concatenate([tokens, marks], axis=-1)


def ahead_of(axis):
    return [(i, i + 1) for i in range(lax.axis_size(axis) - 1)]


def behind(axis):
    return [(i + 1, i) for i in range(lax.axis_size(axis) - 1)]


def halo_rows(tokens, mask):
    ht = tokens.shape[0]
    low, high = slice(ht - RADIUS, ht), slice(0, RADIUS)
    top = lax.ppermute(with_marks(tokens[low], mask[low]), ROW, ahead_of(ROW))
    bot = lax.ppermute(with_marks(tokens[high], mask[high]), ROW, behind(ROW))
    return top, bot


def halo_edges(tokens, mask, top, bot):
    def edge(cols):
        mine = with_marks(tokens[:, cols], mask[:, cols])
        return jnp.concatenate([top[:, cols], mine, bot[:, cols]], axis=0)

    wt = tokens.shape[1]
    return edge(slice(wt - SIDE, wt)), edge(slice(0, SIDE))


CHUNK = 1024


def experts_kernel(plan, who_ref, wr_ref, *refs):
    ds = list(plan)
    blocks, at = {}, 0
    for d in ds:
        blocks[d] = refs[at : at + (2 if d == 4 else 1)]
        at += len(blocks[d])
    users = {j: [d for d in ds if j in plan[d]] for j in range(4)}
    todo = [j for j in range(4) if users[j]]
    held_w = {}
    for j in todo:
        held_w[j] = refs[at : at + (2 if j < 2 else 3)]
        at += len(held_w[j])
    outs = {d: refs[at + 2 * i : at + 2 * i + 2] for i, d in enumerate(ds)}
    rows, share, done, acc, raw, buf_in, buf_down, held_x, sem, sem_x = refs[at + 2 * len(ds) :]
    width = rows.shape[-1]
    patches = share.shape[-1]
    ff = buf_in.shape[-1]
    chunks = ff // CHUNK
    piece = ff // 4
    me = who_ref[0]

    def copies(n):
        j, slot = todo[n], n % 2
        put = lambda src, dst, i: pltpu.make_async_copy(src, dst, sem.at[slot, i])
        if j < 2:
            return (
                put(held_w[j][0], buf_in.at[slot], 0),
                put(held_w[j][1], buf_down.at[slot], 1),
            )
        out, i = [], 0
        for ref in held_w[j]:
            for first in range(0, ref.shape[0], width + piece):
                span = pl.ds(i * piece, piece)
                up, down = pl.ds(first, width), pl.ds(first + width, piece)
                out.append(put(ref.at[up], buf_in.at[slot, :, span], 2 * i))
                out.append(put(ref.at[down], buf_down.at[slot, span, :], 2 * i + 1))
                i += 1
        return out

    def arrive(i):
        out, first = [], 0
        for k, ref in enumerate(blocks[ds[i]]):
            n = ref.shape[0]
            out.append(
                pltpu.make_async_copy(ref, held_x.at[i, pl.ds(first, n)], sem_x.at[i, k])
            )
            first += n
        return out

    for i in range(len(ds)):
        for c in arrive(i):
            c.start()
    for c in copies(0):
        c.start()
    before = lax.broadcasted_iota(jnp.int32, (patches, patches), 0)
    after = lax.broadcasted_iota(jnp.int32, (patches, patches), 1)
    upper = (before < after).astype(jnp.bfloat16)
    slot_of = lax.broadcasted_iota(jnp.int32, (CAP, patches), 0).astype(jnp.float32)
    held = [me ^ j for j in range(4)]
    lane_expert = lax.broadcasted_iota(jnp.int32, (wr_ref.shape[0], patches), 0)
    for i, d in enumerate(ds):
        for c in arrive(i):
            c.wait()
        x = held_x[i, :patches]
        ids = held_x[i, patches:].astype(jnp.float32).astype(jnp.int32)
        e0, e1 = ids[0:1], ids[1:2]
        logits = lax.dot_general(
            wr_ref[...], x, (((1,), (1,)), ((), ())), preferred_element_type=jnp.float32
        )
        pick = lambda e: jnp.sum(jnp.where(lane_expert == e, logits, 0.0), axis=0, keepdims=True)
        gap = pick(e0) - pick(e1)
        g0, g1 = jax.nn.sigmoid(gap), jax.nn.sigmoid(-gap)
        named = [((e0 == h) | (e1 == h)).astype(jnp.float32) for h in held]
        hot = jnp.concatenate(named + named, axis=0)
        rank = jnp.dot(hot.astype(jnp.bfloat16), upper, preferred_element_type=jnp.float32)
        for k, j in enumerate(plan[d]):
            place = jnp.where(named[j] > 0.5, rank[j : j + 1], -1.0)
            hit = slot_of == place
            gate = jnp.where(e0 == held[j], g0, g1)
            share[i, k * CAP : (k + 1) * CAP, :] = jnp.where(hit, gate, 0.0).astype(jnp.bfloat16)
            one = hit.astype(jnp.float32).astype(jnp.bfloat16)
            u = users[j].index(d)
            rows[todo.index(j), u * CAP : (u + 1) * CAP, :] = jnp.dot(
                one, x, preferred_element_type=jnp.float32
            ).astype(jnp.bfloat16)
    for n, j in enumerate(todo):
        if n + 1 < len(todo):
            for cp in copies(n + 1):
                cp.start()
        for cp in copies(n):
            cp.wait()
        m = len(users[j]) * CAP
        slot = n % 2

        def up(c):
            return jnp.dot(
                rows[n, :m],
                buf_in[slot, :, pl.ds(pl.multiple_of(c * CHUNK, CHUNK), CHUNK)],
                preferred_element_type=jnp.float32,
            )

        def down(c, hidden):
            return jnp.dot(
                jax.nn.gelu(hidden, approximate=True).astype(jnp.bfloat16),
                buf_down[slot, pl.ds(pl.multiple_of(c * CHUNK, CHUNK), CHUNK), :],
                preferred_element_type=jnp.float32,
            )

        raw[0, :m] = up(0)
        acc[:m] = jnp.zeros((m, width), jnp.float32)

        @pl.loop(0, chunks - 1)
        def _chunk(c):
            now = lax.rem(c, 2)
            raw[1 - now, :m] = up(c + 1)
            acc[:m] += down(c, raw[now, :m])

        whole = (acc[:m] + down(chunks - 1, raw[(chunks - 1) % 2, :m])).astype(jnp.bfloat16)
        for u, d in enumerate(users[j]):
            k = plan[d].index(j)
            done[ds.index(d), k * CAP : (k + 1) * CAP, :] = whole[u * CAP : (u + 1) * CAP]
    for i, d in enumerate(ds):
        n = len(plan[d]) * CAP
        total = lax.dot_general(
            share[i, :n], done[i, :n], (((0,), (0,)), ((), ())), preferred_element_type=jnp.float32
        )
        for h, out in enumerate(outs[d]):
            out[...] = total[h * out.shape[0] : (h + 1) * out.shape[0]].astype(out.dtype)


def experts(plan, who, router, blocks, weights):
    ds = list(plan)
    width, ff = weights[0][0].shape
    half = (sum(a.shape[0] for a in blocks[ds[0]]) - 16) // 2
    most = max(len(v) for v in plan.values())
    users = [sum(j in v for v in plan.values()) for j in range(4)]
    needed = [w for j in range(4) if users[j] for w in weights[j]]
    given = [a for d in ds for a in blocks[d]]
    vm = pl.BlockSpec(memory_space=pltpu.VMEM)
    hbm = pl.BlockSpec(memory_space=pl.ANY)
    bf = jnp.bfloat16
    work = sum(users) * CAP * width * ff * 4
    got = pl.pallas_call(
        functools.partial(experts_kernel, plan),
        in_specs=[pl.BlockSpec(memory_space=pltpu.SMEM), vm] + [hbm] * (len(given) + len(needed)),
        out_specs=[vm] * (2 * len(ds)),
        out_shape=[jax.ShapeDtypeStruct((half, width), bf)] * (2 * len(ds)),
        scratch_shapes=[
            pltpu.VMEM((sum(u > 0 for u in users), max(users) * CAP, width), bf),
            pltpu.VMEM((len(ds), most * CAP, 2 * half), bf),
            pltpu.VMEM((len(ds), most * CAP, width), bf),
            pltpu.VMEM((max(users) * CAP, width), jnp.float32),
            pltpu.VMEM((2, max(users) * CAP, CHUNK), jnp.float32),
            pltpu.VMEM((2, width, ff), bf),
            pltpu.VMEM((2, ff, width), bf),
            pltpu.VMEM((len(ds), 2 * half + 16, width), bf),
            pltpu.SemaphoreType.DMA((2, 12)),
            pltpu.SemaphoreType.DMA((len(ds), 2)),
        ],
        compiler_params=pltpu.CompilerParams(vmem_limit_bytes=60 << 20),
        cost_estimate=pl.CostEstimate(
            flops=2 * work, bytes_accessed=12_000_000, transcendentals=sum(users) * CAP * ff
        ),
    )(who, router, *given, *needed)
    return {d: tuple(got[2 * i : 2 * i + 2]) for i, d in enumerate(ds)}


def around(step):
    count = lax.axis_size("z")
    return [(i, (i + step) % count) for i in range(count)]


def add(*arrays):
    return sum(a.astype(jnp.float32) for a in arrays).astype(jnp.bfloat16)


def after(x, *others):
    return lax.optimization_barrier((x, *others))[0]


def expert_layer(x, who, router, weights, part):
    ahead, back = around(1), around(-1)
    send = lambda a, way: lax.ppermute(a, "z", way)
    near, far, every = (0, 1), (2, 3), (0, 1, 2, 3)
    half = (x.shape[0] - 16) // 2
    width = x.shape[1]
    blocks, so_far = {0: (x,)}, {}
    weights = list(weights)
    run = lambda plan: experts(plan, who, router, blocks, weights)

    def keep(results, *arrays):
        flat = [a for d in results for a in results[d]]
        out = lax.optimization_barrier((*arrays, *flat))
        held = out[len(arrays) :]
        so_far.update({d: held[2 * i : 2 * i + 2] for i, d in enumerate(results)})
        return out[: len(arrays)]

    one, two = both_ways(part, part)
    part_o = swap(part)
    f, b = send(x, ahead), send(x, back)
    f, b = keep({}, f, b)
    blocks[1], blocks[7] = (f,), (b,)
    f, b = send(f, ahead), send(b, back)
    f, b, one, two = keep(run({0: near, 1: near, 7: near}), f, b, one, two)
    up, down = both_ways(one[:width], two[width:])
    pair = jnp.concatenate([one, two], axis=0)
    pair_o = swap(pair)
    blocks[2], blocks[6] = (f,), (b,)
    f, b = send(f, ahead), send(b, back)
    f, b, up, down, part_o, pair_o = keep(
        run({2: near, 6: near}), f, b, up, down, part_o, pair_o
    )
    last = jnp.concatenate([up, down], axis=0)
    last_o = swap(last)
    blocks[3], blocks[5] = (f,), (b,)
    weights += [(part, pair, last), (part_o, pair_o, last_o)]
    f, b = lax.optimization_barrier((f[:half], b[half:]))
    blocks[4] = (send(f, ahead), send(b, back))
    parts = run({**dict.fromkeys((4, 3, 5), every), **dict.fromkeys((2, 6, 1, 7, 0), far)})
    f0, b1 = send(parts[4][0], back), send(parts[4][1], ahead)
    f1, b0 = send(parts[3][1], back), send(parts[5][0], ahead)
    f0, b1 = send(add(f0, parts[3][0]), back), send(add(b1, parts[5][1]), ahead)
    for i in (2, 1):
        f1 = send(add(f1, parts[i][1], so_far[i][1]), back)
        b0 = send(add(b0, parts[8 - i][0], so_far[8 - i][0]), ahead)
        f0 = send(add(f0, parts[i][0], so_far[i][0]), back)
        b1 = send(add(b1, parts[8 - i][1], so_far[8 - i][1]), ahead)
    return [(parts[0][0], so_far[0][0], f0, b0), (parts[0][1], so_far[0][1], f1, b1)]


def own_quarter(w_in, w_down):
    piece = w_in.shape[1] // lax.axis_size("y")
    first = lax.axis_index("y") * piece
    return jnp.concatenate(
        [
            lax.dynamic_slice_in_dim(w_in, first, piece, 1),
            lax.dynamic_slice_in_dim(w_down, first, piece, 0),
        ],
        axis=0,
    )


def across_x(quarter):
    return lax.ppermute(quarter, ("xh", "xl"), [(0, 3), (3, 0), (1, 2), (2, 1)])


def both_ways(a, b):
    count = lax.axis_size("y")
    ahead = [(i, (i + 1) % count) for i in range(count)]
    back = [(i, (i - 1) % count) for i in range(count)]
    return lax.ppermute(a, "y", ahead), lax.ppermute(b, "y", back)


def swap(a):
    return lax.ppermute(a, "core", [(0, 1), (1, 0)])


def per_device(
    tokens, die_mask, expert_ids, gain_attn, w_qkv, w_out, gain_moe, w_router, w_in, w_down
):
    ht, wt, width = tokens.shape
    patches = ht * wt
    w_in, w_down = w_in[0], w_down[0]
    top, bot = halo_rows(tokens, die_mask)
    to_right, to_left = halo_edges(tokens, die_mask, top, bot)
    left = lax.ppermute(to_right, COL, ahead_of(COL))
    right = lax.ppermute(to_left, COL, behind(COL))
    late_in, late_down = after(w_in, top, bot), after(w_down, top, bot)
    part = across_x(own_quarter(late_in, late_down))
    other = swap(late_in), swap(late_down)
    ids = expert_ids.reshape(patches, 2).T
    marks = jnp.broadcast_to(die_mask.astype(jnp.bfloat16)[..., None], (ht, wt, LANES))
    resid, x = attention(
        tokens, marks, top, bot, left, right, gain_attn, w_qkv, w_out, gain_moe, ids
    )
    who = lax.axis_index(ROW).reshape(1).astype(jnp.int32)
    x, part, *other = lax.optimization_barrier((x, part, *other))
    weights = ((w_in, w_down), tuple(other))
    wide = lambda a: a.astype(jnp.float32)
    moe = expert_layer(x, who, w_router.T, weights, part)
    moe = jnp.concatenate([sum(wide(a) for a in half) for half in moe], axis=0)
    final = (wide(resid) + moe).astype(jnp.bfloat16)
    return final.reshape(ht, wt, width)


def solution(mesh):
    fine = Mesh(mesh.devices.reshape(8, 2, 2, 2, 4), ROW + COL)
    return jax.shard_map(
        per_device,
        mesh=fine,
        in_specs=(
            P(ROW, COL, None),
            P(ROW, COL),
            P(ROW, COL, None, None),
            P(),
            P(),
            P(),
            P(),
            P(),
            P(ROW, None, None),
            P(ROW, None, None),
        ),
        out_specs=P(ROW, COL, None),
        check_vma=False,
    )
```

```python
import functools

import jax
import jax.numpy as jnp
import numpy as np
from jax import lax
from jax.experimental import pallas as pl
from jax.experimental.pallas import tpu as pltpu
from jax.sharding import Mesh, PartitionSpec as P

HEADS = 16
RADIUS = 6
CAP = 96
SIDE = 8
QROWS = 4
LANES = 128
BIG = 1e30

ROW = ("z", "xh", "core")
COL = ("xl", "y")


def norm(wide, gain):
    power = jnp.mean(wide * wide, axis=-1, keepdims=True)
    return (wide * lax.rsqrt(power + 1e-06) * gain).astype(jnp.bfloat16)


def window_bias(marks, wt):
    keyw = wt + 2 * SIDE
    shape = (QROWS + 2 * RADIUS, keyw, QROWS * wt)
    kr, kc, q = (lax.broadcasted_iota(jnp.int32, shape, i) for i in range(3))
    col = jnp.where(kc < wt + SIDE, kc, kc - keyw)
    rise = kr - q // wt - RADIUS
    reach = col - q % wt
    inside = (jnp.abs(rise) <= RADIUS) & (jnp.abs(reach) <= RADIUS)
    centre = (rise == 0) & (reach == 0)
    open_ = (inside & (marks.reshape(shape) > 0.5)) | centre
    return jnp.where(open_, 0.0, -BIG).reshape(shape[0] * shape[1], shape[2])


def attention_kernel(
    gain_ref, gain2_ref, ids_ref, *refs,
):
    sources, (resid_ref, moe_ref), refs = refs[:8], refs[8:10], refs[10:]
    xn, marks, keys, vals, kaug, vaug, qaug, *local, sem = refs
    tok_ref, mask_ref, top_ref, bot_ref, left_ref, right_ref, wqkv_ref, wout_ref = local
    ht, wt, width = tok_ref.shape
    keyw = wt + 2 * SIDE
    krows = QROWS + 2 * RADIUS
    slab = krows * keyw
    nq = QROWS * wt
    gain = gain_ref[...]
    step = pl.program_id(0)

    @pl.when(step == 0)
    def _prepare():
        fetch = [
            pltpu.make_async_copy(src, dst, sem.at[i])
            for i, (src, dst) in enumerate(zip(sources, local))
        ]
        for cp in fetch:
            cp.start()

        def rows(first, count, body_of):
            @pl.loop(0, count)
            def _row(i):
                body, mark = body_of(i)
                at = pl.multiple_of((first + i) * keyw, 16)
                xn[pl.ds(at, wt), :] = norm(body.astype(jnp.float32), gain)
                marks[pl.ds(at, wt), :] = mark.astype(jnp.float32)
                edge = jnp.concatenate(
                    [
                        right_ref[first + i].astype(jnp.float32),
                        left_ref[first + i].astype(jnp.float32),
                    ],
                    axis=0,
                )
                beside = pl.ds(pl.multiple_of(at + wt, 16), 2 * SIDE)
                xn[beside, :] = norm(edge[:, :width], gain)
                marks[beside, :] = edge[:, width:]

        for cp in fetch[:6]:
            cp.wait()
        rows(0, RADIUS, lambda i: (top_ref[i, :, :width], top_ref[i, :, width:]))
        rows(RADIUS, ht, lambda i: (tok_ref[i], mask_ref[i]))
        rows(ht + RADIUS, RADIUS, lambda i: (bot_ref[i, :, :width], bot_ref[i, :, width:]))
        for cp in fetch[6:]:
            cp.wait()
        every = xn[...]
        keys[...] = jnp.dot(
            every, wqkv_ref[:, width : 2 * width], preferred_element_type=jnp.float32
        ).astype(jnp.bfloat16)
        vals[...] = jnp.dot(
            every, wqkv_ref[:, 2 * width :], preferred_element_type=jnp.float32
        ).astype(jnp.bfloat16)
        for p in range(2):
            vaug[p, :, LANES:] = jnp.ones((slab, LANES), jnp.bfloat16)
        spot = lax.broadcasted_iota(jnp.int32, (nq, nq), 0)
        lane = lax.broadcasted_iota(jnp.int32, (nq, nq), 1)
        unit = (spot == lane).astype(jnp.bfloat16)
        for i in range(4):
            for p in range(2):
                qaug[p, i * nq : (i + 1) * nq, LANES:] = unit
        named = ids_ref[...].astype(jnp.float32)
        spare = jnp.zeros((16 - named.shape[0], named.shape[1]), jnp.float32)
        moe_ref[ht * wt :, :] = jnp.concatenate([named, spare], axis=0).astype(jnp.bfloat16)

    base = pl.multiple_of(step * (QROWS * keyw), QROWS * keyw)
    own = [
        xn[pl.ds(pl.multiple_of(base + (RADIUS + i) * keyw, 16), wt), :] for i in range(QROWS)
    ]
    query = jnp.dot(
        jnp.concatenate(own, axis=0), wqkv_ref[:, :width], preferred_element_type=jnp.float32
    )
    hdim = width // HEADS
    query = (query * hdim ** (-0.5)).astype(jnp.bfloat16)
    bias = window_bias(marks[pl.ds(base, slab), :], wt).astype(jnp.bfloat16)
    for p in range(2):
        kaug[p, :, LANES:] = bias
    per = LANES // hdim
    head_of = lax.broadcasted_iota(jnp.int32, (nq, LANES), 1) // hdim
    pieces = []
    for g in range(width // LANES):
        cols = slice(g * LANES, (g + 1) * LANES)
        qg = query[:, cols]
        for i in range(per):
            qaug[g % 2, i * nq : (i + 1) * nq, :LANES] = jnp.where(head_of == i, qg, 0).astype(
                jnp.bfloat16
            )
        kaug[g % 2, :, :LANES] = keys[pl.ds(base, slab), cols]
        vaug[g % 2, :, :LANES] = vals[pl.ds(base, slab), cols]
        scores = lax.dot_general(
            qaug[g % 2], kaug[g % 2], (((1,), (1,)), ((), ())), preferred_element_type=jnp.float32
        )
        highest = jnp.max(scores, axis=-1, keepdims=True)
        weights = jnp.exp(scores - highest).astype(jnp.bfloat16)
        mixed = jnp.dot(weights, vaug[g % 2], preferred_element_type=jnp.float32)
        share = mixed[:, :LANES] / mixed[:, LANES:]
        both = share[:nq]
        for i in range(1, per):
            both = jnp.where(head_of == i, share[i * nq : (i + 1) * nq], both)
        pieces.append(both.astype(jnp.bfloat16))
    attended = jnp.concatenate(pieces, axis=1)
    mixed = jnp.dot(attended, wout_ref[...], preferred_element_type=jnp.float32)
    mine = tok_ref[pl.ds(step * QROWS, QROWS)].reshape(nq, width)
    resid = (mine.astype(jnp.float32) + mixed).astype(jnp.bfloat16)
    resid_ref[...] = resid
    moe_ref[pl.ds(pl.multiple_of(step * nq, nq), nq), :] = norm(
        resid.astype(jnp.float32), gain2_ref[...]
    )


def attention(tokens, marks, top, bot, left, right, gain, wqkv, wout, gain2, ids):
    ht, wt, width = tokens.shape
    slab, nq = (QROWS + 2 * RADIUS) * (wt + 2 * SIDE), QROWS * wt
    total = (ht + 2 * RADIUS) * (wt + 2 * SIDE)
    whole = lambda a: pl.BlockSpec(a.shape, functools.partial(lambda n, i: (0,) * n, a.ndim))
    args = (gain.reshape(1, width), gain2.reshape(1, width), ids)
    large = (tokens, marks, top, bot, left, right, wqkv, wout)
    bf = jnp.bfloat16
    return pl.pallas_call(
        attention_kernel,
        grid=(ht // QROWS,),
        in_specs=[whole(a) for a in args] + [pl.BlockSpec(memory_space=pl.ANY)] * len(large),
        out_specs=[
            pl.BlockSpec((nq, width), lambda i: (i, 0)),
            pl.BlockSpec((ht * wt + 16, width), lambda i: (0, 0)),
        ],
        out_shape=[
            jax.ShapeDtypeStruct((ht * wt, width), bf),
            jax.ShapeDtypeStruct((ht * wt + 16, width), bf),
        ],
        scratch_shapes=[
            pltpu.VMEM((total, width), bf),
            pltpu.VMEM((total, LANES), jnp.float32),
            pltpu.VMEM((total, width), bf),
            pltpu.VMEM((total, width), bf),
            pltpu.VMEM((2, slab, 2 * LANES), bf),
            pltpu.VMEM((2, slab, 2 * LANES), bf),
            pltpu.VMEM((2, 4 * nq, 2 * LANES), bf),
            *[pltpu.VMEM(a.shape, bf) for a in large],
            pltpu.SemaphoreType.DMA((len(large),)),
        ],
        compiler_params=pltpu.CompilerParams(vmem_limit_bytes=60 << 20),
        cost_estimate=pl.CostEstimate(
            flops=10_000_000_000, bytes_accessed=6_000_000, transcendentals=6_000_000
        ),
    )(*args, *large)


def with_marks(tokens, mask):
    marks = jnp.broadcast_to(mask.astype(jnp.bfloat16)[..., None], (*mask.shape, LANES))
    return jnp.concatenate([tokens, marks], axis=-1)


def ahead_of(axis):
    return [(i, i + 1) for i in range(lax.axis_size(axis) - 1)]


def behind(axis):
    return [(i + 1, i) for i in range(lax.axis_size(axis) - 1)]


def halo_rows(tokens, mask):
    ht = tokens.shape[0]
    low, high = slice(ht - RADIUS, ht), slice(0, RADIUS)
    top = lax.ppermute(with_marks(tokens[low], mask[low]), ROW, ahead_of(ROW))
    bot = lax.ppermute(with_marks(tokens[high], mask[high]), ROW, behind(ROW))
    return top, bot


def halo_edges(tokens, mask, top, bot):
    def edge(cols):
        mine = with_marks(tokens[:, cols], mask[:, cols])
        return jnp.concatenate([top[:, cols], mine, bot[:, cols]], axis=0)

    wt = tokens.shape[1]
    return edge(slice(wt - SIDE, wt)), edge(slice(0, SIDE))


CHUNK = 1024


def experts_kernel(plan, who_ref, wr_ref, *refs):
    ds = list(plan)
    blocks, at = {}, 0
    for d in ds:
        blocks[d] = refs[at : at + (2 if d == 4 else 1)]
        at += len(blocks[d])
    users = {j: [d for d in ds if j in plan[d]] for j in range(4)}
    todo = [j for j in range(4) if users[j]]
    held_w = {}
    for j in todo:
        held_w[j] = refs[at : at + (2 if j < 2 else 3)]
        at += len(held_w[j])
    outs = {d: refs[at + 2 * i : at + 2 * i + 2] for i, d in enumerate(ds)}
    rows, share, done, acc, raw, buf_in, buf_down, held_x, sem, sem_x = refs[at + 2 * len(ds) :]
    width = rows.shape[-1]
    patches = share.shape[-1]
    ff = buf_in.shape[-1]
    chunks = ff // CHUNK
    piece = ff // 4
    me = who_ref[0]

    def copies(n):
        j, slot = todo[n], n % 2
        put = lambda src, dst, i: pltpu.make_async_copy(src, dst, sem.at[slot, i])
        if j < 2:
            return (
                put(held_w[j][0], buf_in.at[slot], 0),
                put(held_w[j][1], buf_down.at[slot], 1),
            )
        out, i = [], 0
        for ref in held_w[j]:
            for first in range(0, ref.shape[0], width + piece):
                span = pl.ds(i * piece, piece)
                up, down = pl.ds(first, width), pl.ds(first + width, piece)
                out.append(put(ref.at[up], buf_in.at[slot, :, span], 2 * i))
                out.append(put(ref.at[down], buf_down.at[slot, span, :], 2 * i + 1))
                i += 1
        return out

    def arrive(i):
        out, first = [], 0
        for k, ref in enumerate(blocks[ds[i]]):
            n = ref.shape[0]
            out.append(
                pltpu.make_async_copy(ref, held_x.at[i, pl.ds(first, n)], sem_x.at[i, k])
            )
            first += n
        return out

    for i in range(len(ds)):
        for c in arrive(i):
            c.start()
    for c in copies(0):
        c.start()
    before = lax.broadcasted_iota(jnp.int32, (patches, patches), 0)
    after = lax.broadcasted_iota(jnp.int32, (patches, patches), 1)
    upper = (before < after).astype(jnp.bfloat16)
    slot_of = lax.broadcasted_iota(jnp.int32, (CAP, patches), 0).astype(jnp.float32)
    held = [me ^ j for j in range(4)]
    lane_expert = lax.broadcasted_iota(jnp.int32, (wr_ref.shape[0], patches), 0)
    for i, d in enumerate(ds):
        for c in arrive(i):
            c.wait()
        x = held_x[i, :patches]
        ids = held_x[i, patches:].astype(jnp.float32).astype(jnp.int32)
        e0, e1 = ids[0:1], ids[1:2]
        logits = lax.dot_general(
            wr_ref[...], x, (((1,), (1,)), ((), ())), preferred_element_type=jnp.float32
        )
        pick = lambda e: jnp.sum(jnp.where(lane_expert == e, logits, 0.0), axis=0, keepdims=True)
        gap = pick(e0) - pick(e1)
        g0, g1 = jax.nn.sigmoid(gap), jax.nn.sigmoid(-gap)
        named = [((e0 == h) | (e1 == h)).astype(jnp.float32) for h in held]
        hot = jnp.concatenate(named + named, axis=0)
        rank = jnp.dot(hot.astype(jnp.bfloat16), upper, preferred_element_type=jnp.float32)
        for k, j in enumerate(plan[d]):
            place = jnp.where(named[j] > 0.5, rank[j : j + 1], -1.0)
            hit = slot_of == place
            gate = jnp.where(e0 == held[j], g0, g1)
            share[i, k * CAP : (k + 1) * CAP, :] = jnp.where(hit, gate, 0.0).astype(jnp.bfloat16)
            one = hit.astype(jnp.float32).astype(jnp.bfloat16)
            u = users[j].index(d)
            rows[todo.index(j), u * CAP : (u + 1) * CAP, :] = jnp.dot(
                one, x, preferred_element_type=jnp.float32
            ).astype(jnp.bfloat16)
    for n, j in enumerate(todo):
        if n + 1 < len(todo):
            for cp in copies(n + 1):
                cp.start()
        for cp in copies(n):
            cp.wait()
        m = len(users[j]) * CAP
        slot = n % 2

        def up(c):
            return jnp.dot(
                rows[n, :m],
                buf_in[slot, :, pl.ds(pl.multiple_of(c * CHUNK, CHUNK), CHUNK)],
                preferred_element_type=jnp.float32,
            )

        def down(c, hidden):
            return jnp.dot(
                jax.nn.gelu(hidden, approximate=True).astype(jnp.bfloat16),
                buf_down[slot, pl.ds(pl.multiple_of(c * CHUNK, CHUNK), CHUNK), :],
                preferred_element_type=jnp.float32,
            )

        raw[0, :m] = up(0)
        acc[:m] = jnp.zeros((m, width), jnp.float32)

        @pl.loop(0, chunks - 1)
        def _chunk(c):
            now = lax.rem(c, 2)
            raw[1 - now, :m] = up(c + 1)
            acc[:m] += down(c, raw[now, :m])

        whole = (acc[:m] + down(chunks - 1, raw[(chunks - 1) % 2, :m])).astype(jnp.bfloat16)
        for u, d in enumerate(users[j]):
            k = plan[d].index(j)
            done[ds.index(d), k * CAP : (k + 1) * CAP, :] = whole[u * CAP : (u + 1) * CAP]
    for i, d in enumerate(ds):
        n = len(plan[d]) * CAP
        total = lax.dot_general(
            share[i, :n], done[i, :n], (((0,), (0,)), ((), ())), preferred_element_type=jnp.float32
        )
        for h, out in enumerate(outs[d]):
            out[...] = total[h * out.shape[0] : (h + 1) * out.shape[0]].astype(out.dtype)


def experts(plan, who, router, blocks, weights):
    ds = list(plan)
    width, ff = weights[0][0].shape
    half = (sum(a.shape[0] for a in blocks[ds[0]]) - 16) // 2
    most = max(len(v) for v in plan.values())
    users = [sum(j in v for v in plan.values()) for j in range(4)]
    needed = [w for j in range(4) if users[j] for w in weights[j]]
    given = [a for d in ds for a in blocks[d]]
    vm = pl.BlockSpec(memory_space=pltpu.VMEM)
    hbm = pl.BlockSpec(memory_space=pl.ANY)
    bf = jnp.bfloat16
    work = sum(users) * CAP * width * ff * 4
    got = pl.pallas_call(
        functools.partial(experts_kernel, plan),
        in_specs=[pl.BlockSpec(memory_space=pltpu.SMEM), vm] + [hbm] * (len(given) + len(needed)),
        out_specs=[vm] * (2 * len(ds)),
        out_shape=[jax.ShapeDtypeStruct((half, width), bf)] * (2 * len(ds)),
        scratch_shapes=[
            pltpu.VMEM((sum(u > 0 for u in users), max(users) * CAP, width), bf),
            pltpu.VMEM((len(ds), most * CAP, 2 * half), bf),
            pltpu.VMEM((len(ds), most * CAP, width), bf),
            pltpu.VMEM((max(users) * CAP, width), jnp.float32),
            pltpu.VMEM((2, max(users) * CAP, CHUNK), jnp.float32),
            pltpu.VMEM((2, width, ff), bf),
            pltpu.VMEM((2, ff, width), bf),
            pltpu.VMEM((len(ds), 2 * half + 16, width), bf),
            pltpu.SemaphoreType.DMA((2, 12)),
            pltpu.SemaphoreType.DMA((len(ds), 2)),
        ],
        compiler_params=pltpu.CompilerParams(vmem_limit_bytes=60 << 20),
        cost_estimate=pl.CostEstimate(
            flops=2 * work, bytes_accessed=12_000_000, transcendentals=sum(users) * CAP * ff
        ),
    )(who, router, *given, *needed)
    return {d: tuple(got[2 * i : 2 * i + 2]) for i, d in enumerate(ds)}


def around(step):
    count = lax.axis_size("z")
    return [(i, (i + step) % count) for i in range(count)]


def add(*arrays):
    return sum(a.astype(jnp.float32) for a in arrays).astype(jnp.bfloat16)


def after(x, *others):
    return lax.optimization_barrier((x, *others))[0]


def expert_layer(x, who, router, weights, part, diag):
    ahead, back = around(1), around(-1)
    send = lambda a, way: lax.ppermute(a, "z", way)
    near, far, every = (0, 1), (2, 3), (0, 1, 2, 3)
    half = (x.shape[0] - 16) // 2
    blocks, so_far = {0: (x,)}, {}
    weights = list(weights)
    run = lambda plan: experts(plan, who, router, blocks, weights)

    def keep(results, *arrays):
        flat = [a for d in results for a in results[d]]
        out = lax.optimization_barrier((*arrays, *flat))
        held = out[len(arrays) :]
        so_far.update({d: held[2 * i : 2 * i + 2] for i, d in enumerate(results)})
        return out[: len(arrays)]

    one, two = both_ways(part, part)
    part_o = swap(part)
    f, b = send(x, ahead), send(x, back)
    f, b = keep({}, f, b)
    blocks[1], blocks[7] = (f,), (b,)
    f, b = send(f, ahead), send(b, back)
    f, b, one, two, diag = keep(run({0: near, 1: near, 7: near}), f, b, one, two, diag)
    diag_o = swap(diag)
    pair = jnp.concatenate([one, two], axis=0)
    pair_o = swap(pair)
    blocks[2], blocks[6] = (f,), (b,)
    f, b = send(f, ahead), send(b, back)
    f, b, diag_o, part_o, pair_o = keep(
        run({2: near, 6: near}), f, b, diag_o, part_o, pair_o
    )
    blocks[3], blocks[5] = (f,), (b,)
    weights += [(part, pair, diag), (part_o, pair_o, diag_o)]
    f, b = lax.optimization_barrier((f[:half], b[half:]))
    blocks[4] = (send(f, ahead), send(b, back))
    parts = run({**dict.fromkeys((4, 3, 5), every), **dict.fromkeys((2, 6, 1, 7, 0), far)})
    f0, b1 = send(parts[4][0], back), send(parts[4][1], ahead)
    f1, b0 = send(parts[3][1], back), send(parts[5][0], ahead)
    f0, b1 = send(add(f0, parts[3][0]), back), send(add(b1, parts[5][1]), ahead)
    for i in (2, 1):
        f1 = send(add(f1, parts[i][1], so_far[i][1]), back)
        b0 = send(add(b0, parts[8 - i][0], so_far[8 - i][0]), ahead)
        f0 = send(add(f0, parts[i][0], so_far[i][0]), back)
        b1 = send(add(b1, parts[8 - i][1], so_far[8 - i][1]), ahead)
    return [(parts[0][0], so_far[0][0], f0, b0), (parts[0][1], so_far[0][1], f1, b1)]


def own_quarter(w_in, w_down, beyond):
    piece = w_in.shape[1] // lax.axis_size("y")
    first = lax.rem(lax.axis_index("y") + beyond, lax.axis_size("y")) * piece
    return jnp.concatenate(
        [
            lax.dynamic_slice_in_dim(w_in, first, piece, 1),
            lax.dynamic_slice_in_dim(w_down, first, piece, 0),
        ],
        axis=0,
    )


def across_x(quarter):
    return lax.ppermute(quarter, ("xh", "xl"), [(0, 3), (3, 0), (1, 2), (2, 1)])


def both_ways(a, b):
    count = lax.axis_size("y")
    ahead = [(i, (i + 1) % count) for i in range(count)]
    back = [(i, (i - 1) % count) for i in range(count)]
    return lax.ppermute(a, "y", ahead), lax.ppermute(b, "y", back)


def swap(a):
    return lax.ppermute(a, "core", [(0, 1), (1, 0)])


def per_device(
    tokens, die_mask, expert_ids, gain_attn, w_qkv, w_out, gain_moe, w_router, w_in, w_down
):
    ht, wt, width = tokens.shape
    patches = ht * wt
    w_in, w_down = w_in[0], w_down[0]
    top, bot = halo_rows(tokens, die_mask)
    to_right, to_left = halo_edges(tokens, die_mask, top, bot)
    left = lax.ppermute(to_right, COL, ahead_of(COL))
    right = lax.ppermute(to_left, COL, behind(COL))
    late_in, late_down = after(w_in, top, bot), after(w_down, top, bot)
    part = across_x(own_quarter(late_in, late_down, 0))
    diag = across_x(after(own_quarter(late_in, late_down, 2), part))
    other = swap(late_in), swap(late_down)
    ids = expert_ids.reshape(patches, 2).T
    marks = jnp.broadcast_to(die_mask.astype(jnp.bfloat16)[..., None], (ht, wt, LANES))
    resid, x = attention(
        tokens, marks, top, bot, left, right, gain_attn, w_qkv, w_out, gain_moe, ids
    )
    who = lax.axis_index(ROW).reshape(1).astype(jnp.int32)
    x, part, *other = lax.optimization_barrier((x, part, *other))
    weights = ((w_in, w_down), tuple(other))
    wide = lambda a: a.astype(jnp.float32)
    moe = expert_layer(x, who, w_router.T, weights, part, diag)
    moe = jnp.concatenate([sum(wide(a) for a in half) for half in moe], axis=0)
    final = (wide(resid) + moe).astype(jnp.bfloat16)
    return final.reshape(ht, wt, width)


def solution(mesh):
    fine = Mesh(mesh.devices.reshape(8, 2, 2, 2, 4), ROW + COL)
    return jax.shard_map(
        per_device,
        mesh=fine,
        in_specs=(
            P(ROW, COL, None),
            P(ROW, COL),
            P(ROW, COL, None, None),
            P(),
            P(),
            P(),
            P(),
            P(),
            P(ROW, None, None),
            P(ROW, None, None),
        ),
        out_specs=P(ROW, COL, None),
        check_vma=False,
    )
```

```python
import functools

import jax
import jax.numpy as jnp
import numpy as np
from jax import lax
from jax.experimental import pallas as pl
from jax.experimental.pallas import tpu as pltpu
from jax.sharding import Mesh, PartitionSpec as P

HEADS = 16
RADIUS = 6
CAP = 96
SIDE = 8
QROWS = 4
LANES = 128
BIG = 1e30

ROW = ("z", "xh", "core")
COL = ("xl", "y")


def norm(wide, gain):
    power = jnp.mean(wide * wide, axis=-1, keepdims=True)
    return (wide * lax.rsqrt(power + 1e-06) * gain).astype(jnp.bfloat16)


def window_bias(marks, wt):
    keyw = wt + 2 * SIDE
    shape = (QROWS + 2 * RADIUS, keyw, QROWS * wt)
    kr, kc, q = (lax.broadcasted_iota(jnp.int32, shape, i) for i in range(3))
    col = jnp.where(kc < wt + SIDE, kc, kc - keyw)
    rise = kr - q // wt - RADIUS
    reach = col - q % wt
    inside = (jnp.abs(rise) <= RADIUS) & (jnp.abs(reach) <= RADIUS)
    centre = (rise == 0) & (reach == 0)
    open_ = (inside & (marks.reshape(shape) > 0.5)) | centre
    return jnp.where(open_, 0.0, -BIG).reshape(shape[0] * shape[1], shape[2])


def attention_kernel(
    gain_ref, gain2_ref, ids_ref, *refs,
):
    sources, (resid_ref, moe_ref), refs = refs[:8], refs[8:10], refs[10:]
    xn, marks, keys, vals, kaug, vaug, qaug, *local, sem = refs
    tok_ref, mask_ref, top_ref, bot_ref, left_ref, right_ref, wqkv_ref, wout_ref = local
    ht, wt, width = tok_ref.shape
    keyw = wt + 2 * SIDE
    krows = QROWS + 2 * RADIUS
    slab = krows * keyw
    nq = QROWS * wt
    gain = gain_ref[...]
    step = pl.program_id(0)

    @pl.when(step == 0)
    def _prepare():
        fetch = [
            pltpu.make_async_copy(src, dst, sem.at[i])
            for i, (src, dst) in enumerate(zip(sources, local))
        ]
        for cp in fetch:
            cp.start()

        def rows(first, count, body_of):
            @pl.loop(0, count)
            def _row(i):
                body, mark = body_of(i)
                at = pl.multiple_of((first + i) * keyw, 16)
                xn[pl.ds(at, wt), :] = norm(body.astype(jnp.float32), gain)
                marks[pl.ds(at, wt), :] = mark.astype(jnp.float32)
                edge = jnp.concatenate(
                    [
                        right_ref[first + i].astype(jnp.float32),
                        left_ref[first + i].astype(jnp.float32),
                    ],
                    axis=0,
                )
                beside = pl.ds(pl.multiple_of(at + wt, 16), 2 * SIDE)
                xn[beside, :] = norm(edge[:, :width], gain)
                marks[beside, :] = edge[:, width:]

        for cp in fetch[:6]:
            cp.wait()
        rows(0, RADIUS, lambda i: (top_ref[i, :, :width], top_ref[i, :, width:]))
        rows(RADIUS, ht, lambda i: (tok_ref[i], mask_ref[i]))
        rows(ht + RADIUS, RADIUS, lambda i: (bot_ref[i, :, :width], bot_ref[i, :, width:]))
        for cp in fetch[6:]:
            cp.wait()
        every = xn[...]
        keys[...] = jnp.dot(
            every, wqkv_ref[:, width : 2 * width], preferred_element_type=jnp.float32
        ).astype(jnp.bfloat16)
        vals[...] = jnp.dot(
            every, wqkv_ref[:, 2 * width :], preferred_element_type=jnp.float32
        ).astype(jnp.bfloat16)
        for p in range(2):
            vaug[p, :, LANES:] = jnp.ones((slab, LANES), jnp.bfloat16)
        spot = lax.broadcasted_iota(jnp.int32, (nq, nq), 0)
        lane = lax.broadcasted_iota(jnp.int32, (nq, nq), 1)
        unit = (spot == lane).astype(jnp.bfloat16)
        for i in range(4):
            for p in range(2):
                qaug[p, i * nq : (i + 1) * nq, LANES:] = unit
        named = ids_ref[...].astype(jnp.float32)
        spare = jnp.zeros((16 - named.shape[0], named.shape[1]), jnp.float32)
        moe_ref[ht * wt :, :] = jnp.concatenate([named, spare], axis=0).astype(jnp.bfloat16)

    base = pl.multiple_of(step * (QROWS * keyw), QROWS * keyw)
    own = [
        xn[pl.ds(pl.multiple_of(base + (RADIUS + i) * keyw, 16), wt), :] for i in range(QROWS)
    ]
    query = jnp.dot(
        jnp.concatenate(own, axis=0), wqkv_ref[:, :width], preferred_element_type=jnp.float32
    )
    hdim = width // HEADS
    query = (query * hdim ** (-0.5)).astype(jnp.bfloat16)
    bias = window_bias(marks[pl.ds(base, slab), :], wt).astype(jnp.bfloat16)
    for p in range(2):
        kaug[p, :, LANES:] = bias
    per = LANES // hdim
    head_of = lax.broadcasted_iota(jnp.int32, (nq, LANES), 1) // hdim
    pieces = []
    for g in range(width // LANES):
        cols = slice(g * LANES, (g + 1) * LANES)
        qg = query[:, cols]
        for i in range(per):
            qaug[g % 2, i * nq : (i + 1) * nq, :LANES] = jnp.where(head_of == i, qg, 0).astype(
                jnp.bfloat16
            )
        kaug[g % 2, :, :LANES] = keys[pl.ds(base, slab), cols]
        vaug[g % 2, :, :LANES] = vals[pl.ds(base, slab), cols]
        scores = lax.dot_general(
            qaug[g % 2], kaug[g % 2], (((1,), (1,)), ((), ())), preferred_element_type=jnp.float32
        )
        highest = jnp.max(scores, axis=-1, keepdims=True)
        weights = jnp.exp(scores - highest).astype(jnp.bfloat16)
        mixed = jnp.dot(weights, vaug[g % 2], preferred_element_type=jnp.float32)
        share = mixed[:, :LANES] / mixed[:, LANES:]
        both = share[:nq]
        for i in range(1, per):
            both = jnp.where(head_of == i, share[i * nq : (i + 1) * nq], both)
        pieces.append(both.astype(jnp.bfloat16))
    attended = jnp.concatenate(pieces, axis=1)
    mixed = jnp.dot(attended, wout_ref[...], preferred_element_type=jnp.float32)
    mine = tok_ref[pl.ds(step * QROWS, QROWS)].reshape(nq, width)
    resid = (mine.astype(jnp.float32) + mixed).astype(jnp.bfloat16)
    resid_ref[...] = resid
    moe_ref[pl.ds(pl.multiple_of(step * nq, nq), nq), :] = norm(
        resid.astype(jnp.float32), gain2_ref[...]
    )


def attention(tokens, marks, top, bot, left, right, gain, wqkv, wout, gain2, ids):
    ht, wt, width = tokens.shape
    slab, nq = (QROWS + 2 * RADIUS) * (wt + 2 * SIDE), QROWS * wt
    total = (ht + 2 * RADIUS) * (wt + 2 * SIDE)
    whole = lambda a: pl.BlockSpec(a.shape, functools.partial(lambda n, i: (0,) * n, a.ndim))
    args = (gain.reshape(1, width), gain2.reshape(1, width), ids)
    large = (tokens, marks, top, bot, left, right, wqkv, wout)
    bf = jnp.bfloat16
    return pl.pallas_call(
        attention_kernel,
        grid=(ht // QROWS,),
        in_specs=[whole(a) for a in args] + [pl.BlockSpec(memory_space=pl.ANY)] * len(large),
        out_specs=[
            pl.BlockSpec((nq, width), lambda i: (i, 0)),
            pl.BlockSpec((ht * wt + 16, width), lambda i: (0, 0)),
        ],
        out_shape=[
            jax.ShapeDtypeStruct((ht * wt, width), bf),
            jax.ShapeDtypeStruct((ht * wt + 16, width), bf),
        ],
        scratch_shapes=[
            pltpu.VMEM((total, width), bf),
            pltpu.VMEM((total, LANES), jnp.float32),
            pltpu.VMEM((total, width), bf),
            pltpu.VMEM((total, width), bf),
            pltpu.VMEM((2, slab, 2 * LANES), bf),
            pltpu.VMEM((2, slab, 2 * LANES), bf),
            pltpu.VMEM((2, 4 * nq, 2 * LANES), bf),
            *[pltpu.VMEM(a.shape, bf) for a in large],
            pltpu.SemaphoreType.DMA((len(large),)),
        ],
        compiler_params=pltpu.CompilerParams(vmem_limit_bytes=60 << 20),
        cost_estimate=pl.CostEstimate(
            flops=10_000_000_000, bytes_accessed=6_000_000, transcendentals=6_000_000
        ),
    )(*args, *large)


def with_marks(tokens, mask):
    marks = jnp.broadcast_to(mask.astype(jnp.bfloat16)[..., None], (*mask.shape, LANES))
    return jnp.concatenate([tokens, marks], axis=-1)


def ahead_of(axis):
    return [(i, i + 1) for i in range(lax.axis_size(axis) - 1)]


def behind(axis):
    return [(i + 1, i) for i in range(lax.axis_size(axis) - 1)]


def halo_rows(tokens, mask):
    ht = tokens.shape[0]
    low, high = slice(ht - RADIUS, ht), slice(0, RADIUS)
    top = lax.ppermute(with_marks(tokens[low], mask[low]), ROW, ahead_of(ROW))
    bot = lax.ppermute(with_marks(tokens[high], mask[high]), ROW, behind(ROW))
    return top, bot


def halo_edges(tokens, mask, top, bot):
    def edge(cols):
        mine = with_marks(tokens[:, cols], mask[:, cols])
        return jnp.concatenate([top[:, cols], mine, bot[:, cols]], axis=0)

    wt = tokens.shape[1]
    return edge(slice(wt - SIDE, wt)), edge(slice(0, SIDE))


CHUNK = 1024


def experts_kernel(plan, who_ref, wr_ref, *refs):
    ds = list(plan)
    blocks, at = {}, 0
    for d in ds:
        blocks[d] = refs[at : at + (2 if d == 4 else 1)]
        at += len(blocks[d])
    users = {j: [d for d in ds if j in plan[d]] for j in range(4)}
    todo = [j for j in range(4) if users[j]]
    held_w = {}
    for j in todo:
        held_w[j] = refs[at : at + (2 if j < 2 else 3)]
        at += len(held_w[j])
    outs = {d: refs[at + 2 * i : at + 2 * i + 2] for i, d in enumerate(ds)}
    rows, share, done, acc, raw, buf_in, buf_down, held_x, sem, sem_x = refs[at + 2 * len(ds) :]
    width = rows.shape[-1]
    patches = share.shape[-1]
    ff = buf_in.shape[-1]
    chunks = ff // CHUNK
    piece = ff // 4
    me = who_ref[0]

    def copies(n):
        j, slot = todo[n], n % 2
        put = lambda src, dst, i: pltpu.make_async_copy(src, dst, sem.at[slot, i])
        if j < 2:
            return (
                put(held_w[j][0], buf_in.at[slot], 0),
                put(held_w[j][1], buf_down.at[slot], 1),
            )
        out, i = [], 0
        for ref in held_w[j]:
            for first in range(0, ref.shape[0], width + piece):
                span = pl.ds(i * piece, piece)
                up, down = pl.ds(first, width), pl.ds(first + width, piece)
                out.append(put(ref.at[up], buf_in.at[slot, :, span], 2 * i))
                out.append(put(ref.at[down], buf_down.at[slot, span, :], 2 * i + 1))
                i += 1
        return out

    def arrive(i):
        out, first = [], 0
        for k, ref in enumerate(blocks[ds[i]]):
            n = ref.shape[0]
            out.append(
                pltpu.make_async_copy(ref, held_x.at[i, pl.ds(first, n)], sem_x.at[i, k])
            )
            first += n
        return out

    for i in range(len(ds)):
        for c in arrive(i):
            c.start()
    for c in copies(0):
        c.start()
    before = lax.broadcasted_iota(jnp.int32, (patches, patches), 0)
    after = lax.broadcasted_iota(jnp.int32, (patches, patches), 1)
    upper = (before < after).astype(jnp.bfloat16)
    slot_of = lax.broadcasted_iota(jnp.int32, (CAP, patches), 0).astype(jnp.float32)
    held = [me ^ j for j in range(4)]
    lane_expert = lax.broadcasted_iota(jnp.int32, (wr_ref.shape[0], patches), 0)
    for i, d in enumerate(ds):
        for c in arrive(i):
            c.wait()
        x = held_x[i, :patches]
        ids = held_x[i, patches:].astype(jnp.float32).astype(jnp.int32)
        e0, e1 = ids[0:1], ids[1:2]
        logits = lax.dot_general(
            wr_ref[...], x, (((1,), (1,)), ((), ())), preferred_element_type=jnp.float32
        )
        pick = lambda e: jnp.sum(jnp.where(lane_expert == e, logits, 0.0), axis=0, keepdims=True)
        gap = pick(e0) - pick(e1)
        g0, g1 = jax.nn.sigmoid(gap), jax.nn.sigmoid(-gap)
        named = [((e0 == h) | (e1 == h)).astype(jnp.float32) for h in held]
        hot = jnp.concatenate(named + named, axis=0)
        rank = jnp.dot(hot.astype(jnp.bfloat16), upper, preferred_element_type=jnp.float32)
        for k, j in enumerate(plan[d]):
            place = jnp.where(named[j] > 0.5, rank[j : j + 1], -1.0)
            hit = slot_of == place
            gate = jnp.where(e0 == held[j], g0, g1)
            share[i, k * CAP : (k + 1) * CAP, :] = jnp.where(hit, gate, 0.0).astype(jnp.bfloat16)
            one = hit.astype(jnp.float32).astype(jnp.bfloat16)
            u = users[j].index(d)
            rows[todo.index(j), u * CAP : (u + 1) * CAP, :] = jnp.dot(
                one, x, preferred_element_type=jnp.float32
            ).astype(jnp.bfloat16)
    for n, j in enumerate(todo):
        if n + 1 < len(todo):
            for cp in copies(n + 1):
                cp.start()
        for cp in copies(n):
            cp.wait()
        m = len(users[j]) * CAP
        slot = n % 2

        def up(c):
            return jnp.dot(
                rows[n, :m],
                buf_in[slot, :, pl.ds(pl.multiple_of(c * CHUNK, CHUNK), CHUNK)],
                preferred_element_type=jnp.float32,
            )

        def down(c, hidden):
            return jnp.dot(
                jax.nn.gelu(hidden, approximate=True).astype(jnp.bfloat16),
                buf_down[slot, pl.ds(pl.multiple_of(c * CHUNK, CHUNK), CHUNK), :],
                preferred_element_type=jnp.float32,
            )

        raw[0, :m] = up(0)
        acc[:m] = jnp.zeros((m, width), jnp.float32)

        @pl.loop(0, chunks - 1)
        def _chunk(c):
            now = lax.rem(c, 2)
            raw[1 - now, :m] = up(c + 1)
            acc[:m] += down(c, raw[now, :m])

        whole = (acc[:m] + down(chunks - 1, raw[(chunks - 1) % 2, :m])).astype(jnp.bfloat16)
        for u, d in enumerate(users[j]):
            k = plan[d].index(j)
            done[ds.index(d), k * CAP : (k + 1) * CAP, :] = whole[u * CAP : (u + 1) * CAP]
    for i, d in enumerate(ds):
        n = len(plan[d]) * CAP
        total = lax.dot_general(
            share[i, :n], done[i, :n], (((0,), (0,)), ((), ())), preferred_element_type=jnp.float32
        )
        for h, out in enumerate(outs[d]):
            out[...] = total[h * out.shape[0] : (h + 1) * out.shape[0]].astype(out.dtype)


def experts(plan, who, router, blocks, weights):
    ds = list(plan)
    width, ff = weights[0][0].shape
    half = (sum(a.shape[0] for a in blocks[ds[0]]) - 16) // 2
    most = max(len(v) for v in plan.values())
    users = [sum(j in v for v in plan.values()) for j in range(4)]
    needed = [w for j in range(4) if users[j] for w in weights[j]]
    given = [a for d in ds for a in blocks[d]]
    vm = pl.BlockSpec(memory_space=pltpu.VMEM)
    hbm = pl.BlockSpec(memory_space=pl.ANY)
    bf = jnp.bfloat16
    work = sum(users) * CAP * width * ff * 4
    got = pl.pallas_call(
        functools.partial(experts_kernel, plan),
        in_specs=[pl.BlockSpec(memory_space=pltpu.SMEM), vm] + [hbm] * (len(given) + len(needed)),
        out_specs=[vm] * (2 * len(ds)),
        out_shape=[jax.ShapeDtypeStruct((half, width), bf)] * (2 * len(ds)),
        scratch_shapes=[
            pltpu.VMEM((sum(u > 0 for u in users), max(users) * CAP, width), bf),
            pltpu.VMEM((len(ds), most * CAP, 2 * half), bf),
            pltpu.VMEM((len(ds), most * CAP, width), bf),
            pltpu.VMEM((max(users) * CAP, width), jnp.float32),
            pltpu.VMEM((2, max(users) * CAP, CHUNK), jnp.float32),
            pltpu.VMEM((2, width, ff), bf),
            pltpu.VMEM((2, ff, width), bf),
            pltpu.VMEM((len(ds), 2 * half + 16, width), bf),
            pltpu.SemaphoreType.DMA((2, 12)),
            pltpu.SemaphoreType.DMA((len(ds), 2)),
        ],
        compiler_params=pltpu.CompilerParams(vmem_limit_bytes=60 << 20),
        cost_estimate=pl.CostEstimate(
            flops=2 * work, bytes_accessed=12_000_000, transcendentals=sum(users) * CAP * ff
        ),
    )(who, router, *given, *needed)
    return {d: tuple(got[2 * i : 2 * i + 2]) for i, d in enumerate(ds)}


def around(step):
    count = lax.axis_size("z")
    return [(i, (i + step) % count) for i in range(count)]


def add(*arrays):
    return sum(a.astype(jnp.float32) for a in arrays).astype(jnp.bfloat16)


def after(x, *others):
    return lax.optimization_barrier((x, *others))[0]


def expert_layer(x, who, router, weights, part, diag):
    ahead, back = around(1), around(-1)
    send = lambda a, way: lax.ppermute(a, "z", way)
    near, far, every = (0, 1), (2, 3), (0, 1, 2, 3)
    half = (x.shape[0] - 16) // 2
    blocks, so_far = {0: (x,)}, {}
    weights = list(weights)
    run = lambda plan: experts(plan, who, router, blocks, weights)

    def keep(results, *arrays):
        flat = [a for d in results for a in results[d]]
        out = lax.optimization_barrier((*arrays, *flat))
        held = out[len(arrays) :]
        so_far.update({d: held[2 * i : 2 * i + 2] for i, d in enumerate(results)})
        return out[: len(arrays)]

    one, two = both_ways(part, part)
    part_o = swap(part)
    f, b = send(x, ahead), send(x, back)
    f, b = keep({}, f, b)
    blocks[1], blocks[7] = (f,), (b,)
    f, b = send(f, ahead), send(b, back)
    f, b, one, two, diag = keep(run({0: near, 1: near, 7: near}), f, b, one, two, diag)
    diag_o = swap(diag)
    pair = jnp.concatenate([one, two], axis=0)
    pair_o = swap(pair)
    blocks[2], blocks[6] = (f,), (b,)
    f, b = send(f, ahead), send(b, back)
    f, b, diag_o, part_o, pair_o = keep(
        run({2: near, 6: near}), f, b, diag_o, part_o, pair_o
    )
    blocks[3], blocks[5] = (f,), (b,)
    weights += [(part, pair, diag), (part_o, pair_o, diag_o)]
    f, b = lax.optimization_barrier((f[:half], b[half:]))
    f, b = send(f, ahead), send(b, back)
    parts = run(dict.fromkeys((2, 6, 1, 7, 0), far))
    blocks[4] = tuple(lax.optimization_barrier((f, b, *(a for d in parts for a in parts[d])))[:2])
    parts.update(run(dict.fromkeys((4, 3, 5), every)))
    f0, b1 = send(parts[4][0], back), send(parts[4][1], ahead)
    f1, b0 = send(parts[3][1], back), send(parts[5][0], ahead)
    f0, b1 = send(add(f0, parts[3][0]), back), send(add(b1, parts[5][1]), ahead)
    for i in (2, 1):
        f1 = send(add(f1, parts[i][1], so_far[i][1]), back)
        b0 = send(add(b0, parts[8 - i][0], so_far[8 - i][0]), ahead)
        f0 = send(add(f0, parts[i][0], so_far[i][0]), back)
        b1 = send(add(b1, parts[8 - i][1], so_far[8 - i][1]), ahead)
    return [(parts[0][0], so_far[0][0], f0, b0), (parts[0][1], so_far[0][1], f1, b1)]


def own_quarter(w_in, w_down, beyond):
    piece = w_in.shape[1] // lax.axis_size("y")
    first = lax.rem(lax.axis_index("y") + beyond, lax.axis_size("y")) * piece
    return jnp.concatenate(
        [
            lax.dynamic_slice_in_dim(w_in, first, piece, 1),
            lax.dynamic_slice_in_dim(w_down, first, piece, 0),
        ],
        axis=0,
    )


def across_x(quarter):
    return lax.ppermute(quarter, ("xh", "xl"), [(0, 3), (3, 0), (1, 2), (2, 1)])


def both_ways(a, b):
    count = lax.axis_size("y")
    ahead = [(i, (i + 1) % count) for i in range(count)]
    back = [(i, (i - 1) % count) for i in range(count)]
    return lax.ppermute(a, "y", ahead), lax.ppermute(b, "y", back)


def swap(a):
    return lax.ppermute(a, "core", [(0, 1), (1, 0)])


def per_device(
    tokens, die_mask, expert_ids, gain_attn, w_qkv, w_out, gain_moe, w_router, w_in, w_down
):
    ht, wt, width = tokens.shape
    patches = ht * wt
    w_in, w_down = w_in[0], w_down[0]
    top, bot = halo_rows(tokens, die_mask)
    to_right, to_left = halo_edges(tokens, die_mask, top, bot)
    left = lax.ppermute(to_right, COL, ahead_of(COL))
    right = lax.ppermute(to_left, COL, behind(COL))
    late_in, late_down = after(w_in, top, bot), after(w_down, top, bot)
    part = across_x(own_quarter(late_in, late_down, 0))
    diag = across_x(after(own_quarter(late_in, late_down, 2), part))
    other = swap(late_in), swap(late_down)
    ids = expert_ids.reshape(patches, 2).T
    marks = jnp.broadcast_to(die_mask.astype(jnp.bfloat16)[..., None], (ht, wt, LANES))
    resid, x = attention(
        tokens, marks, top, bot, left, right, gain_attn, w_qkv, w_out, gain_moe, ids
    )
    who = lax.axis_index(ROW).reshape(1).astype(jnp.int32)
    x, part, *other = lax.optimization_barrier((x, part, *other))
    weights = ((w_in, w_down), tuple(other))
    wide = lambda a: a.astype(jnp.float32)
    moe = expert_layer(x, who, w_router.T, weights, part, diag)
    moe = jnp.concatenate([sum(wide(a) for a in half) for half in moe], axis=0)
    final = (wide(resid) + moe).astype(jnp.bfloat16)
    return final.reshape(ht, wt, width)


def solution(mesh):
    fine = Mesh(mesh.devices.reshape(8, 2, 2, 2, 4), ROW + COL)
    return jax.shard_map(
        per_device,
        mesh=fine,
        in_specs=(
            P(ROW, COL, None),
            P(ROW, COL),
            P(ROW, COL, None, None),
            P(),
            P(),
            P(),
            P(),
            P(),
            P(ROW, None, None),
            P(ROW, None, None),
        ),
        out_specs=P(ROW, COL, None),
        check_vma=False,
    )
```
